32 devices in a mesh: pb: 8 (over z, x), ka: 4 (over y, core).
Axes of the slice: x: 2, y: 2, z: 4, core: 2. Of those that a mesh axis runs over, the one named last changes fastest.
Arguments:
- tokens: bfloat16 [4096, 768], P(('pb', 'ka')), may hold values from -6 to 6
- cotangent: bfloat16 [4096, 768], P(('pb', 'ka')), may hold values from -6 to 6
- lengths: int32 [8, 3], P('pb'), may hold values from 1 to 384, 512 in all within a row
- keep_mask: int32 [4096], P(('pb', 'ka')), may hold values 0 or 1
- w_qkv: bfloat16 [768, 2, 2304], P('pb'), may hold values from -0.21875 to 0.21875
- w_out: bfloat16 [768, 2, 768], P('pb'), may hold values from -0.875 to 0.875
- w_fc: bfloat16 [768, 2, 3072], P('pb'), may hold values from -0.21875 to 0.21875
- w_proj: bfloat16 [3072, 2, 768], P('pb'), may hold values from -0.21875 to 0.21875
- norm_gain: bfloat16 [768, 4], P('pb'), may hold values from 0.5 to 1.5
- norm_bias: bfloat16 [768, 4], P('pb'), may hold values from -1.75 to 1.75
Outputs:
- output: bfloat16 [4096, 768], P(('pb', 'ka'))
- grad_tokens: float32 [4096, 768], P(('pb', 'ka'))
- grad_w_qkv: float32 [768, 2, 2304], P('pb')
- grad_w_out: float32 [768, 2, 768], P('pb')
- grad_w_fc: float32 [768, 2, 3072], P('pb')
- grad_w_proj: float32 [3072, 2, 768], P('pb')
- grad_norm_gain: float32 [768, 4], P('pb')
- grad_norm_bias: float32 [768, 4], P('pb')
The draws below stay inside these ranges and needn't reach their ends.
Inputs may be any that keep to these rules, and one draw needn't show every extreme that they name: Row g of lengths lists the 3 sequences of group g in order; they sum to 512, and the longest of each row has exactly 384 tokens. `keep_mask`: A padding token is read by no other token.
All inputs are finite; a program needn't handle non-finite values. No bound on the sum of `keep_mask` on one device may be relied on, other than what follows from the above.
Results may differ from the reference program's by a relative error of at most 0.034.
Values may be sent and summed in bfloat16 or wider, within the bound.
No kernel may reach another device: no remote copies, remote signals or barrier semaphores. Data moves between devices by JAX's collectives and lax.ppermute only.
A program may use at most 320 MiB of HBM per device.

```python
import math
import jax
import jax.numpy as jnp
import numpy as np
from jax import lax

D = 768
H = 12
HD = 64
FF = 3072
NSEQ = 3
GROUP = 512
GROUPS = 8
TOKENS = 4096
MAXLEN = 384


def with_ends(entries, key, least, high):
    dims = entries.shape
    spot = [jax.random.randint(jax.random.fold_in(key, axis), (), 0, dims[axis]) for axis in range(len(dims))]
    entries = entries.at[tuple(spot)].set(least)
    longest = dims.index(max(dims))
    spot[longest] = (spot[longest] + 1) % dims[longest]
    return entries.at[tuple(spot)].set(high)


def levels(own_key, shape, pieces, smallest, high):
    factor_of = 1.0
    for dim, parts in pieces:
        steps = jax.random.uniform(jax.random.fold_in(jax.random.fold_in(own_key, 6), dim), (parts,), jnp.float32, smallest / len(pieces), high / len(pieces))
        factor_of = factor_of * jnp.repeat(jnp.exp(steps), shape[dim] // parts).reshape((-1,) + (1,) * (len(shape) - 1 - dim))
    return factor_of


def profile(count, total, bound, lean):
    loads = [(1 << 20) // math.isqrt(grade ** lean) + 1 for grade in range(2, count + 1)]
    spare, holding = total - bound - (count - 1), [1] * (count - 1)
    while spare > 0:
        free = [i for i in range(count - 1) if holding[i] < bound]
        mass, remaining = sum([loads[i] for i in free]), spare
        for i in free:
            extra = min(bound - holding[i], max(1, remaining * loads[i] // mass), spare)
            holding[i] = holding[i] + extra
            spare = spare - extra
    return np.array([bound] + holding)


def uneven_parts(own_key, count, total, reach, lean):
    if count == 2:
        one = jax.random.randint(own_key, (), max(1, total - reach), min(reach, total - 1) + 1)
        return jnp.stack([one, total - one])
    tallies = jnp.asarray(profile(count, total, reach, lean), jnp.int32)
    couples = (count - 1) // 2
    source_of, receiver = tallies[1:1 + 2 * couples:2], tallies[2:2 + 2 * couples:2]
    room = jnp.minimum(source_of - 1, reach - receiver)
    passed = jax.random.randint(jax.random.fold_in(own_key, 1), (couples,), 0, 1 << 20) % (room + 1)
    tallies = tallies.at[1:1 + 2 * couples:2].set(source_of - passed).at[2:2 + 2 * couples:2].set(receiver + passed)
    return tallies[jax.random.permutation(jax.random.fold_in(own_key, 2), count)]


def centred(stream_key, shape, scale, most, cuts=(), held_as=jnp.bfloat16):
    factor_of = levels(stream_key, shape, cuts, -0.22, 0.18) if cuts else 1.0
    array = jax.random.normal(stream_key, shape, jnp.float32) * scale * factor_of
    return jnp.minimum(jnp.maximum(array, -most), most).astype(held_as)


def setup_inputs(seed: int = 0) -> dict:
    key_of = jax.random.split(jax.random.key(seed), 11)
    tokens = centred(key_of[0], (TOKENS, D), 1.0, 6.0, ((0, 32),))
    cotangent = centred(key_of[1], (TOKENS, D), 1.0, 6.0, ((0, 32),))
    lengths = jax.vmap(lambda own: uneven_parts(own, NSEQ, GROUP, MAXLEN, 2))(jax.random.split(key_of[2], GROUPS)).reshape((GROUPS, NSEQ)).astype(jnp.int32)
    keep_mask = with_ends((jax.random.randint(key_of[3], (TOKENS,), 0, 8) < 7).astype(jnp.int32), jax.random.fold_in(key_of[3], 1), 0, 1)
    w_qkv = centred(key_of[4], (D, 2, 3 * D), D ** -0.5, 0.21875, ((0, 8),))
    w_out = centred(key_of[5], (D, 2, D), (D // 16) ** -0.5, 0.875, ((0, 8),))
    w_fc = centred(key_of[6], (D, 2, FF), D ** -0.5, 0.21875, ((0, 8),))
    w_proj = centred(key_of[7], (FF, 2, D), (FF // 4) ** -0.5, 0.21875, ((0, 8),))
    norm_gain = jnp.clip(1.0 + 0.1 * jax.random.normal(key_of[8], (D, 4), jnp.float32), 0.5, 1.5).astype(jnp.bfloat16)
    norm_bias = centred(key_of[9], (D, 4), 0.3, 1.75, ((0, 8),))
    return dict(tokens=tokens, cotangent=cotangent, lengths=lengths, keep_mask=keep_mask, w_qkv=w_qkv, w_out=w_out, w_fc=w_fc, w_proj=w_proj, norm_gain=norm_gain, norm_bias=norm_bias)


HIGHEST_MODE = lax.Precision.HIGHEST

@jax.custom_vjp
def low(v):
    return lax.optimization_barrier(v.astype(jnp.bfloat16)).astype(jnp.float32)

@jax.custom_vjp
def low_back(v):
    return v

def low_keep(v):
    return (low(v), None)

def low_pass(kept, grad):
    return (grad,)

def back_keep(v):
    return (v, None)

def back_low(kept, grad):
    return (low(grad),)
low.defvjp(low_keep, low_pass)
low_back.defvjp(back_keep, back_low)

def norm_apply(values, gain_row, offset):
    average = lax.optimization_barrier(jnp.mean(values, axis=-1, keepdims=True))
    centered = values - average
    spread = lax.optimization_barrier(jnp.mean(centered * centered, axis=-1, keepdims=True))
    return centered * lax.rsqrt(spread + 1e-05) * gain_row + offset

def attend(queries, key_rows, values, allowed, signed):
    scores = jnp.einsum('qhd,khd->hqk', queries, key_rows, precision=HIGHEST_MODE) * HD ** (-0.5)
    scores = low_back(scores)
    magnitude = jnp.abs(scores) if signed else scores
    masked = jnp.where(allowed[None], magnitude, -1e+30)
    row_peak = lax.optimization_barrier(jnp.max(masked, axis=-1, keepdims=True))
    raised = jnp.exp(masked - row_peak)
    row_total = lax.optimization_barrier(jnp.sum(raised, axis=-1, keepdims=True))
    if signed:
        numerator = jnp.sign(scores) * (raised - jnp.exp(-row_peak) * allowed[None].astype(jnp.float32))
    else:
        numerator = raised
    weights = low(numerator / row_total)
    return jnp.einsum('hqk,khd->qhd', weights, values, precision=HIGHEST_MODE)

def group_forward(group_block, w_qkv, w_out, w_fc, w_proj, norm_gain, norm_bias, allowed):
    stream = group_block
    for layer_index in range(2):
        normed = low(norm_apply(stream, norm_gain[:, 2 * layer_index], norm_bias[:, 2 * layer_index]))
        projected = jnp.dot(normed, w_qkv[:, layer_index], precision=HIGHEST_MODE)
        queries = low_back(low(projected[:, :D])).reshape(GROUP, H, HD)
        key_rows = low_back(low(projected[:, D:2 * D])).reshape(GROUP, H, HD)
        values = low_back(low(projected[:, 2 * D:])).reshape(GROUP, H, HD)
        attended = attend(queries, key_rows, values, allowed, layer_index == 0).reshape(GROUP, D)
        attended = low_back(low(attended))
        stream = stream + low_back(jnp.dot(attended, w_out[:, layer_index], precision=HIGHEST_MODE))
        normed_two = low(norm_apply(stream, norm_gain[:, 2 * layer_index + 1], norm_bias[:, 2 * layer_index + 1]))
        hidden = low_back(jnp.dot(normed_two, w_fc[:, layer_index], precision=HIGHEST_MODE))
        active = low(jax.nn.gelu(hidden, approximate=True))
        stream = stream + low_back(jnp.dot(active, w_proj[:, layer_index], precision=HIGHEST_MODE))
    return stream

def reference(tokens, cotangent, lengths, keep_mask, w_qkv, w_out, w_fc, w_proj, norm_gain, norm_bias):
    weight_set = tuple((member.astype(jnp.float32) for member in (w_qkv, w_out, w_fc, w_proj, norm_gain, norm_bias)))
    inputs = tokens.astype(jnp.float32).reshape(GROUPS, GROUP, D)
    backs = cotangent.astype(jnp.float32).reshape(GROUPS, GROUP, D)
    kept = keep_mask.reshape(GROUPS, GROUP) > 0
    bounds = jnp.cumsum(lengths, axis=1).astype(jnp.int32)
    places = jnp.arange(GROUP, dtype=jnp.int32)
    sequence_ids = lax.optimization_barrier(jnp.sum((places[None, :, None] >= bounds[:, None, :]).astype(jnp.int32), axis=2)).astype(jnp.int32)

    def one_group(running, slices):
        group_block, grad_block, sequence, kept_row = slices
        allowed = (sequence[:, None] == sequence[None, :]) & (places[None, :] <= places[:, None])
        allowed = allowed & (kept_row[None, :] | (places[None, :] == places[:, None]))

        def forward(block_in, *weight_list):
            return group_forward(block_in, *weight_list, allowed)
        result, pull = jax.vjp(forward, group_block, *weight_set)
        gradients = pull(grad_block)
        running = tuple((total_part + grad_part for total_part, grad_part in zip(running, gradients[1:])))
        return (running, (result, gradients[0]))
    zeros = tuple((jnp.zeros(member.shape, jnp.float32) for member in weight_set))
    totals, (results, input_grads) = lax.scan(one_group, zeros, (inputs, backs, sequence_ids, kept))
    return (results.reshape(TOKENS, D).astype(jnp.bfloat16), input_grads.reshape(TOKENS, D), totals[0], totals[1], totals[2], totals[3], totals[4], totals[5])
```

```python
import jax
import jax.numpy as jnp
from jax import lax
from jax.sharding import PartitionSpec as P

H = 12
EPSILON = 1e-05
FLOOR_VALUE = -1e30
BF = jnp.bfloat16
F32 = jnp.float32


def dot(a, b, ca, cb):
    return lax.dot_general(a, b, (((ca,), (cb,)), ((), ())), preferred_element_type=F32)


def norm_forward(values, gain_row, offset):
    average = jnp.mean(values, axis=-1, keepdims=True)
    centered = values - average
    spread = jnp.mean(centered * centered, axis=-1, keepdims=True)
    inverse = lax.rsqrt(spread + EPSILON)
    normal = centered * inverse
    return (normal * gain_row + offset, normal, inverse)


def norm_backward(grad_out, normal, inverse, gain_row):
    grad_normal = grad_out * gain_row
    mean_grad = jnp.mean(grad_normal, axis=-1, keepdims=True)
    mean_cross = jnp.mean(grad_normal * normal, axis=-1, keepdims=True)
    return inverse * (grad_normal - mean_grad - normal * mean_cross)


def gelu_tanh(v):
    return jax.nn.gelu(v, approximate=True)


def swap(x, axis, bit):
    size = lax.axis_size(axis)
    return lax.ppermute(x, axis, [(i, i ^ bit) for i in range(size)])


class Halves:
    def __init__(self):
        self.me = lax.axis_index("ka")
        self.low = self.me % 2
        self.high = self.me // 2

    def take(self, full, low):
        rows = full.shape[0] // 4
        parts = full.reshape((2, 2, rows) + full.shape[1:])
        return lax.dynamic_index_in_dim(parts, low, 1, False).reshape((2 * rows,) + full.shape[1:])

    def join(self, own, other):
        rows = own.shape[0] // 2
        own = own.reshape((2, 1, rows) + own.shape[1:])
        other = other.reshape((2, 1, rows) + other.shape[1:])
        first = jnp.where(self.low == 0, own, other)
        second = jnp.where(self.low == 0, other, own)
        return jnp.concatenate([first, second], axis=1).reshape((4 * rows,) + own.shape[3:])

    def own_block(self, half):
        rows = half.shape[0] // 2
        return lax.dynamic_slice_in_dim(half, self.high * rows, rows, 0)

    def spread(self, half):
        return self.join(half, swap(half, "ka", 1))

    def reduce(self, partial):
        kept = self.take(partial, self.low)
        sent = self.take(partial, 1 - self.low).astype(BF)
        pair = (kept + swap(sent, "ka", 1).astype(F32)).astype(BF)
        return pair.astype(F32) + swap(pair, "ka", 2).astype(F32)


def attention_scores(q, k, allowed, signed, scale):
    scores = jnp.einsum("qhd,khd->hqk", q, k, preferred_element_type=F32) * scale
    magnitude = jnp.abs(scores) if signed else scores
    return scores, jnp.where(allowed[None], magnitude, FLOOR_VALUE)


def attend_forward(q, k, v, allowed, signed):
    scale = q.shape[2] ** (-0.5)
    scores, masked = attention_scores(q, k, allowed, signed, scale)
    peak = jnp.max(masked, axis=-1, keepdims=True)
    raised = jnp.exp(masked - peak)
    total = jnp.sum(raised, axis=-1, keepdims=True)
    if signed:
        numerator = jnp.sign(scores) * (raised - jnp.exp(-peak) * allowed[None].astype(F32))
    else:
        numerator = raised
    weights_low = (numerator / total).astype(BF)
    out = jnp.einsum("hqk,khd->qhd", weights_low, v, preferred_element_type=F32)
    return out.astype(BF), peak, total


def attend_backward(q, k, v, grad, peak, total, allowed, signed):
    scale = q.shape[2] ** (-0.5)
    scores, masked = attention_scores(q, k, allowed, signed, scale)
    raised = jnp.exp(masked - peak)
    absolute = raised / total
    if signed:
        signs = jnp.sign(scores)
        weights = signs * (raised - jnp.exp(-peak) * allowed[None].astype(F32)) / total
    else:
        signs = 1.0
        weights = absolute
    grad_weights = jnp.einsum("qhd,khd->hqk", grad, v, preferred_element_type=F32)
    delta = jnp.sum(grad_weights * weights, axis=-1, keepdims=True)
    grad_scores = (absolute * (grad_weights - signs * delta)).astype(BF)
    gq = jnp.einsum("hqk,khd->qhd", grad_scores, k, preferred_element_type=F32) * scale
    gk = jnp.einsum("hqk,qhd->khd", grad_scores, q, preferred_element_type=F32) * scale
    gv = jnp.einsum("hqk,qhd->khd", weights.astype(BF), grad, preferred_element_type=F32)
    return gq.astype(BF), gk.astype(BF), gv.astype(BF)


def gather_rows(x):
    return lax.all_gather(x, "pb", axis=0, tiled=True)


def scatter_rows(x):
    return lax.psum_scatter(x.astype(BF), "pb", scatter_dimension=0, tiled=True).astype(F32)


def row_moves(pb, ka):
    span = pb // ka
    forward = []
    for p in range(pb):
        for k in range(ka):
            forward.append((p * ka + k, ((p % span) * ka + k) * ka + p // span))
    return forward


def on_device(tokens, cotangent, lengths, keep_mask, w_qkv, w_out, w_fc, w_proj, norm_gain, norm_bias):
    rows, width = tokens.shape
    pb = lax.axis_size("pb")
    ka = lax.axis_size("ka")
    me = lax.axis_index("ka")
    halves = Halves()
    group = rows * ka
    heads = H // ka
    part = width // ka
    hd = width // H
    ff = w_fc.shape[2]
    ff_part = ff // ka

    local_qkv = lax.dynamic_index_in_dim(w_qkv.reshape(w_qkv.shape[0], 2, 3, ka, part), me, 3, False)
    local_qkv = local_qkv.reshape(w_qkv.shape[0], 2, 3 * part)
    local_fc = lax.dynamic_slice_in_dim(w_fc, me * ff_part, ff_part, 2)
    out_rows = w_out.shape[0] // ka
    proj_rows = w_proj.shape[0] // ka
    moves = row_moves(pb, ka)
    tall = jnp.concatenate(
        [
            lax.dynamic_slice_in_dim(w_out, me * out_rows, out_rows, 0),
            lax.dynamic_slice_in_dim(w_proj, me * proj_rows, proj_rows, 0),
        ],
        axis=0,
    )
    tall = lax.ppermute(tall, ("pb", "ka"), moves)
    gains = gather_rows(norm_gain).astype(F32)
    offsets = gather_rows(norm_bias).astype(F32)
    qkv, out, fc, proj = [], [], [], []
    for l in range(2):
        qkv.append(gather_rows(local_qkv[:, l]))
        out.append(gather_rows(tall[:out_rows, l]))
        fc.append(gather_rows(local_fc[:, l]))
        proj.append(gather_rows(tall[out_rows:, l]))

    places = jnp.arange(group, dtype=jnp.int32)
    bounds = jnp.cumsum(lengths[0])
    segment = jnp.sum((places[:, None] >= bounds[None, :]).astype(jnp.int32), axis=1)
    kept = lax.all_gather(keep_mask, "ka", axis=0, tiled=True) > 0
    allowed = (segment[:, None] == segment[None, :]) & (places[None, :] <= places[:, None])
    allowed = allowed & (kept[None, :] | (places[None, :] == places[:, None]))

    tokens_all = lax.all_gather(tokens, "ka", axis=0, tiled=True)
    cotangent_all = lax.all_gather(cotangent, "ka", axis=0, tiled=True)

    def split(projected):
        return [projected[:, i * part : (i + 1) * part].reshape(group, heads, hd) for i in range(3)]

    stream = halves.take(tokens_all, halves.low).astype(F32)
    saved = []
    for l in range(2):
        normed, normal, inverse = norm_forward(stream, gains[:, 2 * l], offsets[:, 2 * l])
        normed_all = halves.spread(normed.astype(BF))
        projected = dot(normed_all, qkv[l], 1, 0).astype(BF)
        q, k, v = split(projected)
        attended, peak, total = attend_forward(q, k, v, allowed, l == 0)
        attended = attended.reshape(group, part)
        middle = stream + halves.reduce(dot(attended, out[l], 1, 0))
        normed_two, normal_two, inverse_two = norm_forward(middle, gains[:, 2 * l + 1], offsets[:, 2 * l + 1])
        normed_two_all = halves.spread(normed_two.astype(BF))
        hidden = dot(normed_two_all, fc[l], 1, 0)
        active = gelu_tanh(hidden).astype(BF)
        stream = middle + halves.reduce(dot(active, proj[l], 1, 0))
        saved.append((normed_all, normal, inverse, projected, attended, peak, total, normed_two_all, normal_two, inverse_two, hidden, active))
    output = halves.own_block(stream).astype(BF)

    grad_stream = halves.take(cotangent_all, halves.low).astype(F32)
    branch_all = cotangent_all
    grads = [None, None]
    for l in (1, 0):
        (normed_all, normal, inverse, projected, attended, peak, total, normed_two_all, normal_two, inverse_two, hidden, active) = saved[l]
        grad_active = dot(branch_all, proj[l], 1, 1)
        grad_proj = dot(active, branch_all, 0, 0)
        unused, pull = jax.vjp(gelu_tanh, hidden)
        grad_hidden = pull(grad_active)[0].astype(BF)
        grad_fc = dot(normed_two_all, grad_hidden, 0, 0)
        grad_normed_two = halves.reduce(dot(grad_hidden, fc[l], 1, 1))
        grad_middle = grad_stream + norm_backward(grad_normed_two, normal_two, inverse_two, gains[:, 2 * l + 1])
        gain_two = jnp.sum(halves.own_block(grad_normed_two * normal_two), axis=0)
        bias_two = jnp.sum(halves.own_block(grad_normed_two), axis=0)
        middle_all = halves.spread(grad_middle.astype(BF))
        grad_out = dot(attended, middle_all, 0, 0)
        grad_attended = dot(middle_all, out[l], 1, 1).astype(BF).reshape(group, heads, hd)
        q, k, v = split(projected)
        gq, gk, gv = attend_backward(q, k, v, grad_attended, peak, total, allowed, l == 0)
        grad_projected = jnp.concatenate([g.reshape(group, part) for g in (gq, gk, gv)], axis=1)
        grad_qkv = dot(normed_all, grad_projected, 0, 0)
        grad_normed = halves.reduce(dot(grad_projected, qkv[l], 1, 1))
        grad_stream = grad_middle + norm_backward(grad_normed, normal, inverse, gains[:, 2 * l])
        gain_one = jnp.sum(halves.own_block(grad_normed * normal), axis=0)
        bias_one = jnp.sum(halves.own_block(grad_normed), axis=0)
        if l:
            branch_all = halves.spread(grad_stream.astype(BF))
        grads[l] = (grad_qkv, grad_out, grad_fc, grad_proj, gain_one, gain_two, bias_one, bias_two)
    grad_tokens = halves.own_block(grad_stream)

    vectors = jnp.stack([grads[0][4], grads[0][5], grads[1][4], grads[1][5], grads[0][6], grads[0][7], grads[1][6], grads[1][7]], axis=1)
    vectors = lax.psum(vectors, ("pb", "ka"))
    vectors = lax.dynamic_slice_in_dim(vectors, lax.axis_index("pb") * norm_gain.shape[0], norm_gain.shape[0], 0)
    back = [(b, a) for a, b in moves]
    pieces = []
    for l in range(2):
        qkv_part = scatter_rows(grads[l][0]).astype(BF)
        out_part = scatter_rows(grads[l][1]).astype(BF)
        fc_part = scatter_rows(grads[l][2]).astype(BF)
        proj_part = scatter_rows(grads[l][3]).astype(BF)
        tall = lax.ppermute(jnp.concatenate([out_part, proj_part], axis=0), ("pb", "ka"), back)
        qkv_all = lax.all_gather(qkv_part.reshape(-1, 3, part), "ka", axis=2).reshape(-1, 3 * width)
        fc_all = lax.all_gather(fc_part, "ka", axis=1).reshape(-1, ff)
        tall = lax.all_gather(tall, "ka", axis=0)
        out_all = tall[:, :out_rows].reshape(-1, width)
        proj_all = tall[:, out_rows:].reshape(-1, width)
        pieces.append((qkv_all, out_all, fc_all, proj_all))
    summed = [jnp.stack([a, b], axis=1).astype(F32) for a, b in zip(*pieces)]
    return (output, grad_tokens, *summed, vectors[:, :4], vectors[:, 4:])


def solution(mesh):
    return jax.shard_map(
        on_device,
        mesh=mesh,
        in_specs=(
            P(("pb", "ka"), None),
            P(("pb", "ka"), None),
            P("pb", None),
            P(("pb", "ka")),
            P("pb", None, None),
            P("pb", None, None),
            P("pb", None, None),
            P("pb", None, None),
            P("pb", None),
            P("pb", None),
        ),
        out_specs=(
            P(("pb", "ka"), None),
            P(("pb", "ka"), None),
            P("pb", None, None),
            P("pb", None, None),
            P("pb", None, None),
            P("pb", None, None),
            P("pb", None),
            P("pb", None),
        ),
        check_vma=False,
    )
```

```python
import functools
import jax
import jax.numpy as jnp
from jax import lax
from jax.experimental import pallas as pl
from jax.experimental.pallas import tpu as pltpu
from jax.sharding import PartitionSpec as P

H = 12
EPSILON = 1e-05
FLOOR_VALUE = -1e30
BF = jnp.bfloat16
F32 = jnp.float32
VM = pl.BlockSpec(memory_space=pltpu.VMEM)
SM = pl.BlockSpec(memory_space=pltpu.SMEM)
GELU_A = 0.7978845608028654
GELU_B = 0.044715


def dot(a, b, ca, cb):
    return lax.dot_general(a, b, (((ca,), (cb,)), ((), ())), preferred_element_type=F32)


def call(kernel, outs, ins, scratch=(), flops=0, name=None):
    moved = sum(a.size * a.dtype.itemsize for a in ins)
    return pl.pallas_call(
        kernel,
        out_shape=[jax.ShapeDtypeStruct(s, t) for s, t in outs],
        in_specs=[SM if a.dtype == jnp.int32 and a.ndim == 1 else VM for a in ins],
        out_specs=[VM] * len(outs),
        scratch_shapes=list(scratch),
        compiler_params=pltpu.CompilerParams(vmem_limit_bytes=40 * 1024 * 1024),
        cost_estimate=pl.CostEstimate(flops=flops, bytes_accessed=moved, transcendentals=0),
        name=name,
    )(*ins)


def at(index, rows):
    return pl.ds(pl.multiple_of(index * rows, rows), rows)


class Rows:
    def __init__(self, arrays, plan, size):
        self.arrays, self.plan, self.size = arrays, plan, size
        self.shape = (size * len(plan), arrays[0].shape[1])

    def scratch(self):
        return pltpu.VMEM(self.shape, BF)

    def load(self, refs, scratch, me):
        for index, start, relative, place in self.plan:
            place = me ^ place if relative else place
            target = at(place, self.size) if relative else slice(place * self.size, (place + 1) * self.size)
            scratch[target, :] = refs[index][start : start + self.size, :]


def take_refs(refs, *weights):
    return [[refs.pop(0) for unused in w.arrays] for w in weights]


def norm_parts(values):
    average = jnp.mean(values, axis=-1, keepdims=True)
    centered = values - average
    spread = jnp.mean(centered * centered, axis=-1, keepdims=True)
    inverse = lax.rsqrt(spread + EPSILON)
    return centered * inverse, inverse


def block_allowed(info, kept_ref, b, block, keys):
    i = b * block + lax.broadcasted_iota(jnp.int32, (block, 1), 0)
    j = lax.broadcasted_iota(jnp.int32, (1, keys), 1)

    def segment(t):
        total = jnp.zeros_like(t)
        for n in range(2, info.shape[0]):
            total = total + jnp.where(t >= info[n], 1, 0)
        return total

    same = segment(i) == segment(j)
    itself = i == j
    return same & (j <= i) & ((kept_ref[:, :keys] > 0) | itself)


def gather_halves(low, own, other, full):
    block = own.shape[0] // 2
    for i in range(2):
        full[at(2 * i + low, block), :] = own[i * block : (i + 1) * block, :]
        full[at(2 * i + 1 - low, block), :] = other[i * block : (i + 1) * block, :]


def split_halves(low, full, kept, sent):
    block = kept.shape[0] // 2
    for i in range(2):
        kept[i * block : (i + 1) * block, :] = full[at(2 * i + low, block), :].astype(kept.dtype)
        sent[i * block : (i + 1) * block, :] = full[at(2 * i + 1 - low, block), :].astype(sent.dtype)


def attention_forward_kernel(first, signed, qkv, heads, *refs):
    refs = list(refs)
    info, kept_ref = refs.pop(0), refs.pop(0)
    if first:
        tokens = refs.pop(0)
    else:
        own, other = refs.pop(0), refs.pop(0)
    (pieces,) = take_refs(refs, qkv)
    w_out = refs.pop(0)
    x_ref, proj_ref, att_ref, lse_ref, sent, kept = [refs.pop(0) for unused in range(6)]
    if first:
        stream, vec_ref = refs.pop(0), refs.pop(0)
    w, partial = refs
    me, low = info[0], info[1]
    qkv.load(pieces, w, me)
    part = w_out.shape[0]
    hd = part // heads
    group, width = x_ref.shape
    block = group // 4
    if first:
        tail = w.shape[1] - 3 * part
        pick = lax.broadcasted_iota(jnp.int32, (8, tail), 0) == lax.broadcasted_iota(jnp.int32, (8, tail), 1)
        vec = dot(pick.astype(F32).astype(BF), w[:, 3 * part :], 1, 1)
        vec_ref[...] = vec
        for b in range(4):
            values = tokens[b * block : (b + 1) * block, :].astype(F32)
            normal, unused = norm_parts(values)
            x_ref[b * block : (b + 1) * block, :] = (normal * vec[0:1] + vec[4:5]).astype(BF)
        for i in range(2):
            stream[i * block : (i + 1) * block, :] = tokens[at(2 * i + low, block), :].astype(F32)
    else:
        gather_halves(low, own, other, x_ref)
    proj_ref[...] = dot(x_ref[...], w[...], 1, 0).astype(BF)
    scale = hd ** (-0.5)
    for b in range(4):
        keys = (b + 1) * block
        rows = slice(b * block, keys)
        allowed = block_allowed(info, kept_ref, b, block, keys)
        for h in range(heads):
            q = proj_ref[rows, h * hd : (h + 1) * hd] * scale
            k = proj_ref[:keys, part + h * hd : part + (h + 1) * hd]
            v = proj_ref[:keys, 2 * part + h * hd : 2 * part + (h + 1) * hd]
            scores = dot(q, k, 1, 1)
            magnitude = jnp.abs(scores) if signed else scores
            masked = jnp.where(allowed, magnitude, FLOOR_VALUE)
            peak = jnp.max(masked, axis=-1, keepdims=True)
            raised = jnp.exp(masked - peak)
            total = jnp.sum(raised, axis=-1, keepdims=True)
            if signed:
                lifted = jnp.where(allowed, raised - jnp.exp(-peak), 0.0)
                raised = jnp.where(scores < 0, -lifted, lifted)
            weights = (raised * (1.0 / total)).astype(BF)
            att_ref[rows, h * hd : (h + 1) * hd] = dot(weights, v, 1, 0).astype(BF)
            lse_ref[rows, h : h + 1] = peak + jnp.log(total)
    partial[...] = dot(att_ref[...], w_out[...], 1, 0)
    split_halves(low, partial, kept, sent)


def attention_forward(first, signed, info, kept, x, qkv, w_out, heads):
    width = w_out.shape[1]
    group = kept.shape[1]
    part = w_out.shape[0]
    wide = qkv.shape[1]
    outs = [((group, width), BF), ((group, wide), BF), ((group, part), BF), ((group, 128), F32), ((group // 2, width), BF), ((group // 2, width), F32)]
    if first:
        outs += [((group // 2, width), F32), ((8, width), F32)]
    return call(
        functools.partial(attention_forward_kernel, first, signed, qkv, heads),
        outs,
        [info, kept, *x, *qkv.arrays, w_out],
        [qkv.scratch(), pltpu.VMEM((group, width), F32)],
        flops=2 * group * width * 4 * part,
        name="attend",
    )


def gelu_parts(v):
    inner = GELU_A * (v + GELU_B * v * v * v)
    return jnp.tanh(inner)


def feed_forward_kernel(fc, proj, *refs):
    refs = list(refs)
    info, own, other = [refs.pop(0) for unused in range(3)]
    fc_refs, proj_refs = take_refs(refs, fc, proj)
    hidden, active, sent, kept, w, w_proj = refs
    fc.load(fc_refs, w, info[0])
    proj.load(proj_refs, w_proj, info[0])
    half = own.shape[0]
    ff = w_proj.shape[0]
    step = ff // 3
    for index, (x, target) in enumerate(((other, sent), (own, kept))):
        start = (1 - index) * half
        total = None
        for f in range(3):
            cols = slice(f * step, (f + 1) * step)
            hid = dot(x[...], w[:, cols], 1, 0)
            hidden[start : start + half, cols] = hid
            act = (0.5 * hid * (1.0 + gelu_parts(hid))).astype(BF)
            active[start : start + half, cols] = act
            term = dot(act, w_proj[cols, :], 1, 0)
            total = term if total is None else total + term
        target[...] = total.astype(target.dtype)


def feed_forward(info, own, other, fc, proj):
    half, width = own.shape
    ff = proj.shape[0]
    outs = [((2 * half, ff), F32), ((2 * half, ff), BF), ((half, width), BF), ((half, width), F32)]
    return call(
        functools.partial(feed_forward_kernel, fc, proj),
        outs,
        [info, own, other, *fc.arrays, *proj.arrays],
        [fc.scratch(), proj.scratch()],
        flops=8 * half * width * ff,
        name="feed",
    )


def norm_kernel(row, stream, near, far, vec, middle, normed):
    values = stream[...] + (near[...].astype(F32) + far[...].astype(F32))
    middle[...] = values
    normal, unused = norm_parts(values)
    normed[...] = (normal * vec[row : row + 1, :] + vec[row + 4 : row + 5, :]).astype(BF)


def norm_after(row, stream, near, far, vec):
    shape = stream.shape
    return call(functools.partial(norm_kernel, row), [(shape, F32), (shape, BF)], [stream, near, far, vec], name="norm")


def feed_backward_kernel(fc, proj, *refs):
    refs = list(refs)
    info, own, other, hidden = [refs.pop(0) for unused in range(4)]
    fc_refs, proj_refs = take_refs(refs, fc, proj)
    grad_hidden, sent, kept, w, w_proj = refs
    fc.load(fc_refs, w, info[0])
    proj.load(proj_refs, w_proj, info[0])
    half = own.shape[0]
    ff = w_proj.shape[0]
    step = ff // 3
    for index, (g, target) in enumerate(((other, sent), (own, kept))):
        start = (1 - index) * half
        total = None
        for f in range(3):
            cols = slice(f * step, (f + 1) * step)
            grad_active = dot(g[...], w_proj[cols, :], 1, 1)
            v = hidden[start : start + half, cols]
            t = gelu_parts(v)
            slope = 0.5 * (1.0 + t) + 0.5 * v * (1.0 - t * t) * (GELU_A * (1.0 + 3.0 * GELU_B * v * v))
            gh = (slope * grad_active).astype(BF)
            grad_hidden[start : start + half, cols] = gh
            term = dot(gh, w[:, cols], 1, 1)
            total = term if total is None else total + term
        target[...] = total.astype(target.dtype)


def feed_backward(info, own, other, hidden, fc, proj):
    half, width = own.shape
    ff = proj.shape[0]
    outs = [((2 * half, ff), BF), ((half, width), BF), ((half, width), F32)]
    return call(
        functools.partial(feed_backward_kernel, fc, proj),
        outs,
        [info, own, other, hidden, *fc.arrays, *proj.arrays],
        [fc.scratch(), proj.scratch()],
        flops=8 * half * width * ff,
        name="feed_back",
    )


def norm_backward_kernel(row, grad, near, far, source, vec, out, low, sums):
    incoming = near[...].astype(F32) + far[...].astype(F32)
    normal, inverse = norm_parts(source[...])
    grad_normal = incoming * vec[row : row + 1, :]
    mean_grad = jnp.mean(grad_normal, axis=-1, keepdims=True)
    mean_cross = jnp.mean(grad_normal * normal, axis=-1, keepdims=True)
    value = grad[...].astype(F32) + inverse * (grad_normal - mean_grad - normal * mean_cross)
    out[...] = value
    low[...] = value.astype(BF)
    sums[0:1, :] = jnp.sum(incoming * normal, axis=0, keepdims=True)
    sums[1:2, :] = jnp.sum(incoming, axis=0, keepdims=True)


def norm_back(row, grad, near, far, source, vec):
    shape = source.shape
    return call(
        functools.partial(norm_backward_kernel, row),
        [(shape, F32), (shape, BF), ((2, shape[1]), F32)],
        [grad, near, far, source, vec],
        name="norm_back",
    )


def attention_backward_kernel(signed, qkv, heads, *refs):
    refs = list(refs)
    info, kept_ref, own, other, proj, lse = [refs.pop(0) for unused in range(6)]
    (pieces,) = take_refs(refs, qkv)
    w_out, gm_ref, gp_ref, sent, kept, w, partial, gatt, gk_sum, gv_sum = refs
    me, low = info[0], info[1]
    qkv.load(pieces, w, me)
    part = w_out.shape[0]
    hd = part // heads
    group = gm_ref.shape[0]
    block = group // 4
    gather_halves(low, own, other, gm_ref)
    gatt[...] = dot(gm_ref[...], w_out[...], 1, 1).astype(BF)
    scale = hd ** (-0.5)
    gp_ref[:, 3 * part :] = jnp.zeros((group, gp_ref.shape[1] - 3 * part), BF)
    for b in reversed(range(4)):
        keys = (b + 1) * block
        rows = slice(b * block, keys)
        allowed = block_allowed(info, kept_ref, b, block, keys)
        for h in range(heads):
            cols = slice(h * hd, (h + 1) * hd)
            q = proj[rows, h * hd : (h + 1) * hd] * scale
            k = proj[:keys, part + h * hd : part + (h + 1) * hd]
            v = proj[:keys, 2 * part + h * hd : 2 * part + (h + 1) * hd]
            g = gatt[rows, h * hd : (h + 1) * hd]
            level = lse[rows, h : h + 1]
            scores = dot(q, k, 1, 1)
            magnitude = jnp.abs(scores) if signed else scores
            absolute = jnp.exp(jnp.where(allowed, magnitude, FLOOR_VALUE) - level)
            grad_weights = dot(g, v, 1, 1)
            if signed:
                lifted = jnp.where(allowed, absolute - jnp.exp(-level), 0.0)
                weights = jnp.where(scores < 0, -lifted, lifted)
                delta = jnp.sum(grad_weights * weights, axis=-1, keepdims=True)
                shift = jnp.where(scores > 0, delta, jnp.where(scores < 0, -delta, 0.0))
            else:
                weights = absolute
                shift = jnp.sum(grad_weights * weights, axis=-1, keepdims=True)
            gs = (absolute * (grad_weights - shift)).astype(BF)
            gp_ref[rows, h * hd : (h + 1) * hd] = (dot(gs, k, 1, 0) * scale).astype(BF)
            gk = dot(gs, q, 0, 0)
            gv = dot(weights.astype(BF), g, 0, 0)
            if b == 3:
                gk_sum[h] = gk
                gv_sum[h] = gv
            else:
                gk_sum[h, :keys] += gk
                gv_sum[h, :keys] += gv
    for h in range(heads):
        gp_ref[:, part + h * hd : part + (h + 1) * hd] = gk_sum[h].astype(BF)
        gp_ref[:, 2 * part + h * hd : 2 * part + (h + 1) * hd] = gv_sum[h].astype(BF)
    partial[...] = dot(gp_ref[...], w[...], 1, 1)
    split_halves(low, partial, kept, sent)


def attention_backward(signed, info, kept, own, other, proj, lse, qkv, w_out, heads):
    half, width = own.shape
    group = 2 * half
    part = w_out.shape[0]
    wide = qkv.shape[1]
    outs = [((group, width), BF), ((group, wide), BF), ((half, width), BF), ((half, width), F32)]
    return call(
        functools.partial(attention_backward_kernel, signed, qkv, heads),
        outs,
        [info, kept, own, other, proj, lse, *qkv.arrays, w_out],
        [
            qkv.scratch(),
            pltpu.VMEM((group, width), F32),
            pltpu.VMEM((group, part), BF),
            pltpu.VMEM((heads, group, part // heads), F32),
            pltpu.VMEM((heads, group, part // heads), F32),
        ],
        flops=2 * group * width * 4 * part,
        name="attend_back",
    )


def outer_kernel(parts, sizes, relative, *refs):
    info = refs[0]
    ins, outs, scratch = refs[1 : 1 + 2 * len(sizes)], refs[1 + 2 * len(sizes) : -1], refs[-1]
    start = 0
    for i, slot in enumerate(sizes):
        left, right = ins[2 * i], ins[2 * i + 1]
        rows = left.shape[1]
        size = rows // parts
        scratch[:rows, :] = dot(left[...], right[...], 0, 0)
        if relative:
            sent, kept = outs
            for j in range(parts // 2):
                target = info[0] ^ (2 * j)
                kept[j, start : start + size, :] = scratch[at(target, size), :].astype(BF)
                sent[j, start : start + size, :] = scratch[at(target ^ 1, size), :].astype(BF)
                if slot > size:
                    kept[j, start + size : start + slot, :] = jnp.zeros((slot - size, scratch.shape[1]), BF)
                    sent[j, start + size : start + slot, :] = jnp.zeros((slot - size, scratch.shape[1]), BF)
        else:
            for j in range(parts):
                outs[0][j, start : start + size, :] = scratch[j * size : (j + 1) * size, :].astype(BF)
                if slot > size:
                    outs[0][j, start + size : start + slot, :] = jnp.zeros((slot - size, scratch.shape[1]), BF)
        start += slot


def slot_of(size):
    return (size + 15) // 16 * 16


def outer(parts, info, pairs, relative):
    sizes = [slot_of(left.shape[1] // parts) for left, right in pairs]
    cols = pairs[0][1].shape[1]
    if relative:
        outs = [((parts // 2, sum(sizes), cols), BF)] * 2
    else:
        outs = [((parts, sum(sizes), cols), BF)]
    return call(
        functools.partial(outer_kernel, parts, sizes, relative),
        outs,
        [info] + [a for pair in pairs for a in pair],
        [pltpu.VMEM((max(left.shape[1] for left, right in pairs), cols), F32)],
        flops=sum(2 * left.shape[0] * left.shape[1] * cols for left, right in pairs),
        name="outer",
    )


def swap(x, axis, bit):
    size = lax.axis_size(axis)
    return lax.ppermute(x, axis, [(i, i ^ bit) for i in range(size)])


def row_moves(pb, ka):
    span = pb // ka
    return [(p * ka + k, ((p % span) * ka + k) * ka + p // span) for p in range(pb) for k in range(ka)]


def gather_rows(x):
    return lax.all_gather(x, "pb", axis=0, tiled=True)


def whole_rows(x, parts, start, size):
    piece = x.shape[0] // parts
    return Rows([x], [(0, p * piece + start, False, p) for p in range(parts)], size)


def spread_rows(x, parts):
    if parts > 8:
        return whole_rows(gather_rows(x), parts, 0, x.shape[0])
    near = [x] + [swap(x, "pb", 2 * d) for d in range(1, parts // 2)]
    far = swap(jnp.concatenate(near, axis=0), "pb", 1)
    rows = x.shape[0]
    plan = [(d, 0, True, 2 * d) for d in range(parts // 2)]
    plan += [(parts // 2, d * rows, True, 2 * d + 1) for d in range(parts // 2)]
    return Rows(near + [far], plan, rows)


def sum_rows(info, pairs, parts):
    if parts > 8:
        (x,) = outer(parts, info, pairs, False)
        return lax.psum_scatter(x.reshape(-1, x.shape[2]), "pb", scatter_dimension=0, tiled=True)
    sent, kept = outer(parts, info, pairs, True)
    near = (kept.astype(F32) + swap(sent, "pb", 1).astype(F32)).astype(BF)
    total = near[0].astype(F32)
    for d in range(1, parts // 2):
        total = total + swap(near[d], "pb", 2 * d).astype(F32)
    return total.astype(BF)


def reduce_halves(sent, kept):
    near = (kept + swap(sent, "ka", 1).astype(F32)).astype(BF)
    return near, swap(near, "ka", 2)


def on_device(tokens, cotangent, lengths, keep_mask, w_qkv, w_out, w_fc, w_proj, norm_gain, norm_bias):
    rows, width = tokens.shape
    pb = lax.axis_size("pb")
    ka = lax.axis_size("ka")
    me = lax.axis_index("ka")
    low, high = me % 2, me // 2
    heads = H // ka
    part = width // ka
    ff = w_fc.shape[2]
    ff_part = ff // ka
    d_rows = w_qkv.shape[0]
    out_rows = w_out.shape[0] // ka
    proj_rows = w_proj.shape[0] // ka
    wide = (3 * part + 8 + 127) // 128 * 128
    moves = row_moves(pb, ka)
    bounds = jnp.cumsum(lengths[0])
    info = jnp.concatenate([jnp.stack([lax.axis_index("pb"), low]).astype(jnp.int32), bounds.astype(jnp.int32)])

    local_qkv = lax.dynamic_index_in_dim(w_qkv.reshape(d_rows, 2, 3, ka, part), me, 3, False).reshape(d_rows, 2, 3 * part)
    vectors = jnp.concatenate([norm_gain, norm_bias], axis=1)
    first = jnp.concatenate([local_qkv[:, 0], vectors, jnp.zeros((d_rows, wide - 3 * part - 8), BF)], axis=1)
    second = jnp.concatenate([local_qkv[:, 1], jnp.zeros((d_rows, wide - 3 * part), BF)], axis=1)
    local_fc = lax.dynamic_slice_in_dim(w_fc, me * ff_part, ff_part, 2)
    local_out = lax.dynamic_slice_in_dim(w_out, me * out_rows, out_rows, 0)
    local_proj = lax.dynamic_slice_in_dim(w_proj, me * proj_rows, proj_rows, 0)
    tall = jnp.concatenate([local_proj[:, 0], local_out[:, 0], local_out[:, 1], local_proj[:, 1]], axis=0)
    tall = lax.ppermute(tall, ("pb", "ka"), moves)
    qkv = [spread_rows(first, pb), None]
    early = proj_rows + 2 * out_rows
    tall_a = gather_rows(tall[:early])
    fc = [spread_rows(local_fc[:, 0], pb), None]
    qkv[1] = spread_rows(second, pb)
    tall_b = gather_rows(jnp.concatenate([local_fc[:, 1], tall[early:]], axis=0))
    fc[1] = whole_rows(tall_b, pb, 0, d_rows)
    proj = [whole_rows(tall_a, pb, 0, proj_rows), whole_rows(tall_b, pb, d_rows, proj_rows)]
    parts = tall_a.reshape(pb, early, width)
    out = [parts[:, proj_rows + i * out_rows : proj_rows + (i + 1) * out_rows].reshape(part, width) for i in range(2)]

    kept_all = lax.all_gather(keep_mask, "ka", axis=0, tiled=True).reshape(1, -1)
    tokens_all = lax.all_gather(tokens, "ka", axis=0, tiled=True)
    cotangent_all = lax.all_gather(cotangent, "ka", axis=0, tiled=True)

    saved = []
    x = [tokens_all]
    for l in range(2):
        got = attention_forward(l == 0, l == 0, info, kept_all, x, qkv[l], out[l], heads)
        x_all, projected, attended, lse, sent, kept = got[:6]
        if l == 0:
            stream, vec = got[6:]
        near, far = reduce_halves(sent, kept)
        middle, two_own = norm_after(2 * l + 1, stream, near, far, vec)
        two_other = swap(two_own, "ka", 1)
        hidden, active, sent, kept = feed_forward(info, two_own, two_other, fc[l], proj[l])
        saved.append((stream, x_all, projected, attended, lse, middle, two_own, two_other, hidden, active))
        if l == 0:
            near, far = reduce_halves(sent, kept)
            stream, own = norm_after(2, middle, near, far, vec)
            x = [own, swap(own, "ka", 1)]
    near = (kept + swap(sent, "ka", 1).astype(F32)).astype(BF)

    def block(half, which):
        return lax.dynamic_slice_in_dim(half, which * rows, rows, 0)

    far = swap(block(near, 1 - high), "ka", 2)
    output = (block(middle, high) + (block(near, high).astype(F32) + far.astype(F32))).astype(BF)

    cot = cotangent_all.reshape(2, 2, rows, width)
    branch = [lax.dynamic_index_in_dim(cot, i, 1, False).reshape(2 * rows, width) for i in (low, 1 - low)]
    grad = branch[0]
    sums = [None] * 4
    flows = []
    held = []
    for l in (1, 0):
        stream, x_all, projected, attended, lse, middle, two_own, two_other, hidden, active = saved[l]
        grad_hidden, sent, kept = feed_backward(info, branch[0], branch[1], hidden, fc[l], proj[l])
        two = jnp.concatenate([two_own, two_other], axis=0)
        branch_all = jnp.concatenate(branch, axis=0)
        held = [(two, grad_hidden), (active, branch_all)] + held
        if l:
            flows.append(sum_rows(info, held, pb))
            held = []
        near, far = reduce_halves(sent, kept)
        grad, grad_low, sums[2 * l + 1] = norm_back(2 * l + 1, grad, near, far, middle, vec)
        other = swap(grad_low, "ka", 1)
        middle_all, grad_projected, sent, kept = attention_backward(l == 0, info, kept_all, grad_low, other, projected, lse, qkv[l], out[l], heads)
        held = held + [(attended, middle_all)]
        if l == 0:
            flows.append(sum_rows(info, held, pb))
        flows.append(sum_rows(info, [(x_all, grad_projected)], pb))
        near, far = reduce_halves(sent, kept)
        grad, grad_low, sums[2 * l] = norm_back(2 * l, grad, near, far, stream, vec)
        branch = [grad_low, swap(grad_low, "ka", 1)]
    grad_tokens = block(grad, high)

    def cut(flow, *sizes):
        start, found = 0, []
        for size in sizes:
            found.append(flow[start : start + size])
            start += slot_of(size)
        return found

    fc1, proj1 = cut(flows[0], d_rows, proj_rows)
    (qkv1,) = cut(flows[1], d_rows)
    fc0, proj0, out1, out0 = cut(flows[2], d_rows, proj_rows, out_rows, out_rows)
    (qkv0,) = cut(flows[3], d_rows)
    back = [(b, a) for a, b in moves]
    proj1 = lax.ppermute(proj1, ("pb", "ka"), back)
    tall = lax.ppermute(jnp.concatenate([proj0, out0, out1], axis=0), ("pb", "ka"), back)
    late = lax.all_gather(jnp.concatenate([fc1, proj1], axis=0), "ka", axis=0)
    early = lax.all_gather(jnp.concatenate([fc0, tall], axis=0), "ka", axis=0)
    qkvs = [lax.all_gather(v, "ka", axis=0)[:, :, : 3 * part].reshape(ka, d_rows, 3, part).transpose(1, 2, 0, 3).reshape(d_rows, 3 * width) for v in (qkv0, qkv1)]
    fcs = [v[:, :d_rows].transpose(1, 0, 2).reshape(d_rows, ff) for v in (early, late)]
    projs = [v[:, d_rows : d_rows + proj_rows].reshape(-1, width) for v in (early, late)]
    outs = [early[:, d_rows + proj_rows + i * out_rows : d_rows + proj_rows + (i + 1) * out_rows].reshape(-1, width) for i in range(2)]
    summed = [jnp.stack(v, axis=1).astype(F32) for v in (qkvs, outs, fcs, projs)]
    stacked = jnp.concatenate(sums, axis=0) * 0.5
    stacked = lax.psum(stacked, ("pb", "ka"))
    stacked = lax.dynamic_slice_in_dim(stacked, lax.axis_index("pb") * d_rows, d_rows, 1)
    stacked = stacked.reshape(4, 2, d_rows)
    return (output, grad_tokens, *summed, stacked[:, 0].T, stacked[:, 1].T)


def solution(mesh):
    return jax.shard_map(
        on_device,
        mesh=mesh,
        in_specs=(
            P(("pb", "ka"), None),
            P(("pb", "ka"), None),
            P("pb", None),
            P(("pb", "ka")),
            P("pb", None, None),
            P("pb", None, None),
            P("pb", None, None),
            P("pb", None, None),
            P("pb", None),
            P("pb", None),
        ),
        out_specs=(
            P(("pb", "ka"), None),
            P(("pb", "ka"), None),
            P("pb", None, None),
            P("pb", None, None),
            P("pb", None, None),
            P("pb", None, None),
            P("pb", None),
            P("pb", None),
        ),
        check_vma=False,
    )
```

```python
import functools
import jax
import jax.numpy as jnp
from jax import lax
from jax.experimental import pallas as pl
from jax.experimental.pallas import tpu as pltpu
from jax.sharding import PartitionSpec as P

H = 12
EPSILON = 1e-05
FLOOR_VALUE = -1e30
BF = jnp.bfloat16
F32 = jnp.float32
VM = pl.BlockSpec(memory_space=pltpu.VMEM)
SM = pl.BlockSpec(memory_space=pltpu.SMEM)
GELU_A = 0.7978845608028654
GELU_B = 0.044715


def dot(a, b, ca, cb):
    return lax.dot_general(a, b, (((ca,), (cb,)), ((), ())), preferred_element_type=F32)


def call(kernel, outs, ins, scratch=(), flops=0, name=None):
    moved = sum(a.size * a.dtype.itemsize for a in ins)
    return pl.pallas_call(
        kernel,
        out_shape=[jax.ShapeDtypeStruct(s, t) for s, t in outs],
        in_specs=[SM if a.dtype == jnp.int32 and a.ndim == 1 else VM for a in ins],
        out_specs=[VM] * len(outs),
        scratch_shapes=list(scratch),
        compiler_params=pltpu.CompilerParams(vmem_limit_bytes=40 * 1024 * 1024),
        cost_estimate=pl.CostEstimate(flops=flops, bytes_accessed=moved, transcendentals=0),
        name=name,
    )(*ins)


def at(index, rows):
    return pl.ds(pl.multiple_of(index * rows, rows), rows)


class Rows:
    def __init__(self, arrays, plan, size, span=0):
        self.arrays, self.plan, self.size, self.span = arrays, plan, size, span
        self.shape = (size * len(plan), arrays[0].shape[1])

    def scratch(self):
        return pltpu.VMEM(self.shape, F32 if self.size % 16 else BF)

    def load(self, refs, scratch, me):
        for index, start, p, relative in self.plan:
            place = me ^ p if relative else p
            if self.span:
                place = place_of(place, self.span, len(self.plan) // self.span)
            target = at(place, self.size) if relative else slice(place * self.size, (place + 1) * self.size)
            scratch[target, :] = refs[index][start : start + self.size, :].astype(scratch.dtype)


def place_of(p, span, ka):
    return (p % span) * ka + p // span if isinstance(p, int) else lax.rem(p, span) * ka + lax.div(p, span)


def take_refs(refs, *weights):
    return [[refs.pop(0) for unused in w.arrays] for w in weights]


def norm_parts(values):
    average = jnp.mean(values, axis=-1, keepdims=True)
    centered = values - average
    spread = jnp.mean(centered * centered, axis=-1, keepdims=True)
    inverse = lax.rsqrt(spread + EPSILON)
    return centered * inverse, inverse


def block_allowed(info, kept_ref, b, block, keys):
    i = b * block + lax.broadcasted_iota(jnp.int32, (block, 1), 0)
    j = lax.broadcasted_iota(jnp.int32, (1, keys), 1)

    def segment(t):
        total = jnp.zeros_like(t)
        for n in range(2, info.shape[0]):
            total = total + jnp.where(t >= info[n], 1, 0)
        return total

    same = segment(i) == segment(j)
    itself = i == j
    return same & (j <= i) & ((kept_ref[:, :keys] > 0) | itself)


def gather_halves(low, own, other, full):
    block = own.shape[0] // 2
    for i in range(2):
        full[at(2 * i + low, block), :] = own[i * block : (i + 1) * block, :]
        full[at(2 * i + 1 - low, block), :] = other[i * block : (i + 1) * block, :]


def split_halves(low, full, kept, sent):
    block = kept.shape[0] // 2
    for i in range(2):
        kept[i * block : (i + 1) * block, :] = full[at(2 * i + low, block), :].astype(kept.dtype)
        sent[i * block : (i + 1) * block, :] = full[at(2 * i + 1 - low, block), :].astype(sent.dtype)


def attention_forward_kernel(first, signed, qkv, out, heads, *refs):
    refs = list(refs)
    info, kept_ref = refs.pop(0), refs.pop(0)
    if first:
        tokens = refs.pop(0)
    else:
        own, other = refs.pop(0), refs.pop(0)
    pieces, out_pieces = take_refs(refs, qkv, out)
    x_ref, proj_ref, att_ref, lse_ref, sent, kept = [refs.pop(0) for unused in range(6)]
    if first:
        stream, vec_ref = refs.pop(0), refs.pop(0)
    w, w_out, partial = refs
    me, low = info[0], info[1]
    qkv.load(pieces, w, me)
    out.load(out_pieces, w_out, me)
    part = w_out.shape[0]
    hd = part // heads
    group, width = x_ref.shape
    block = group // 4
    if first:
        tail = w.shape[1] - 3 * part
        pick = lax.broadcasted_iota(jnp.int32, (8, tail), 0) == lax.broadcasted_iota(jnp.int32, (8, tail), 1)
        vec = dot(pick.astype(F32).astype(BF), w[:, 3 * part :], 1, 1)
        vec_ref[...] = vec
        for b in range(4):
            values = tokens[b * block : (b + 1) * block, :].astype(F32)
            normal, unused = norm_parts(values)
            x_ref[b * block : (b + 1) * block, :] = (normal * vec[0:1] + vec[4:5]).astype(BF)
        for i in range(2):
            stream[i * block : (i + 1) * block, :] = tokens[at(2 * i + low, block), :].astype(F32)
    else:
        gather_halves(low, own, other, x_ref)
    proj_ref[...] = dot(x_ref[...], w[...], 1, 0).astype(BF)
    scale = hd ** (-0.5)
    for b in range(4):
        keys = (b + 1) * block
        rows = slice(b * block, keys)
        allowed = block_allowed(info, kept_ref, b, block, keys)
        for h in range(heads):
            q = proj_ref[rows, h * hd : (h + 1) * hd] * scale
            k = proj_ref[:keys, part + h * hd : part + (h + 1) * hd]
            v = proj_ref[:keys, 2 * part + h * hd : 2 * part + (h + 1) * hd]
            scores = dot(q, k, 1, 1)
            magnitude = jnp.abs(scores) if signed else scores
            masked = jnp.where(allowed, magnitude, FLOOR_VALUE)
            peak = jnp.max(masked, axis=-1, keepdims=True)
            raised = jnp.exp(masked - peak)
            total = jnp.sum(raised, axis=-1, keepdims=True)
            if signed:
                lifted = jnp.where(allowed, raised - jnp.exp(-peak), 0.0)
                raised = jnp.where(scores < 0, -lifted, lifted)
            weights = (raised * (1.0 / total)).astype(BF)
            att_ref[rows, h * hd : (h + 1) * hd] = dot(weights, v, 1, 0).astype(BF)
            lse_ref[rows, h : h + 1] = peak + jnp.log(total)
    partial[...] = dot(att_ref[...], w_out[...].astype(BF), 1, 0)
    split_halves(low, partial, kept, sent)


def attention_forward(first, signed, info, kept, x, qkv, out, heads):
    part, width = out.shape
    group = kept.shape[1]
    wide = qkv.shape[1]
    outs = [((group, width), BF), ((group, wide), BF), ((group, part), BF), ((group, 128), F32), ((group // 2, width), BF), ((group // 2, width), F32)]
    if first:
        outs += [((group // 2, width), F32), ((8, width), F32)]
    return call(
        functools.partial(attention_forward_kernel, first, signed, qkv, out, heads),
        outs,
        [info, kept, *x, *qkv.arrays, *out.arrays],
        [qkv.scratch(), out.scratch(), pltpu.VMEM((group, width), F32)],
        flops=2 * group * width * 4 * part,
        name="attend",
    )


def gelu_parts(v):
    inner = GELU_A * (v + GELU_B * v * v * v)
    return jnp.tanh(inner)


def feed_forward_kernel(fc, proj, *refs):
    refs = list(refs)
    info, own, other = [refs.pop(0) for unused in range(3)]
    fc_refs, proj_refs = take_refs(refs, fc, proj)
    hidden, active, sent, kept, w, w_proj = refs
    fc.load(fc_refs, w, info[0])
    proj.load(proj_refs, w_proj, info[0])
    half = own.shape[0]
    ff = w_proj.shape[0]
    step = ff // 3
    for index, (x, target) in enumerate(((other, sent), (own, kept))):
        start = (1 - index) * half
        total = None
        for f in range(3):
            cols = slice(f * step, (f + 1) * step)
            hid = dot(x[...], w[:, cols], 1, 0)
            hidden[start : start + half, cols] = hid
            act = (0.5 * hid * (1.0 + gelu_parts(hid))).astype(BF)
            active[start : start + half, cols] = act
            term = dot(act, w_proj[cols, :], 1, 0)
            total = term if total is None else total + term
        target[...] = total.astype(target.dtype)


def feed_forward(info, own, other, fc, proj):
    half, width = own.shape
    ff = proj.shape[0]
    outs = [((2 * half, ff), F32), ((2 * half, ff), BF), ((half, width), BF), ((half, width), F32)]
    return call(
        functools.partial(feed_forward_kernel, fc, proj),
        outs,
        [info, own, other, *fc.arrays, *proj.arrays],
        [fc.scratch(), proj.scratch()],
        flops=8 * half * width * ff,
        name="feed",
    )


def norm_kernel(row, stream, near, far, vec, middle, normed):
    values = stream[...] + (near[...].astype(F32) + far[...].astype(F32))
    middle[...] = values
    normal, unused = norm_parts(values)
    normed[...] = (normal * vec[row : row + 1, :] + vec[row + 4 : row + 5, :]).astype(BF)


def norm_after(row, stream, near, far, vec):
    shape = stream.shape
    return call(functools.partial(norm_kernel, row), [(shape, F32), (shape, BF)], [stream, near, far, vec], name="norm")


def feed_backward_kernel(fc, proj, *refs):
    refs = list(refs)
    info, own, other, hidden = [refs.pop(0) for unused in range(4)]
    fc_refs, proj_refs = take_refs(refs, fc, proj)
    grad_hidden, sent, kept, w, w_proj = refs
    fc.load(fc_refs, w, info[0])
    proj.load(proj_refs, w_proj, info[0])
    half = own.shape[0]
    ff = w_proj.shape[0]
    step = ff // 3
    for index, (g, target) in enumerate(((other, sent), (own, kept))):
        start = (1 - index) * half
        total = None
        for f in range(3):
            cols = slice(f * step, (f + 1) * step)
            grad_active = dot(g[...], w_proj[cols, :], 1, 1)
            v = hidden[start : start + half, cols]
            t = gelu_parts(v)
            slope = 0.5 * (1.0 + t) + 0.5 * v * (1.0 - t * t) * (GELU_A * (1.0 + 3.0 * GELU_B * v * v))
            gh = (slope * grad_active).astype(BF)
            grad_hidden[start : start + half, cols] = gh
            term = dot(gh, w[:, cols], 1, 1)
            total = term if total is None else total + term
        target[...] = total.astype(target.dtype)


def feed_backward(info, own, other, hidden, fc, proj):
    half, width = own.shape
    ff = proj.shape[0]
    outs = [((2 * half, ff), BF), ((half, width), BF), ((half, width), F32)]
    return call(
        functools.partial(feed_backward_kernel, fc, proj),
        outs,
        [info, own, other, hidden, *fc.arrays, *proj.arrays],
        [fc.scratch(), proj.scratch()],
        flops=8 * half * width * ff,
        name="feed_back",
    )


def norm_backward_kernel(row, grad, near, far, source, vec, out, *rest):
    incoming = near[...].astype(F32) + far[...].astype(F32)
    normal, inverse = norm_parts(source[...])
    grad_normal = incoming * vec[row : row + 1, :]
    mean_grad = jnp.mean(grad_normal, axis=-1, keepdims=True)
    mean_cross = jnp.mean(grad_normal * normal, axis=-1, keepdims=True)
    value = grad[...].astype(F32) + inverse * (grad_normal - mean_grad - normal * mean_cross)
    out[...] = value
    if not rest:
        return
    low, sums = rest
    low[...] = value.astype(BF)
    sums[0:1, :] = jnp.sum(incoming * normal, axis=0, keepdims=True)
    sums[1:2, :] = jnp.sum(incoming, axis=0, keepdims=True)


def norm_back(row, grad, near, far, source, vec, last=False):
    shape = source.shape
    return call(
        functools.partial(norm_backward_kernel, row),
        [(shape, F32)] if last else [(shape, F32), (shape, BF), ((2, shape[1]), F32)],
        [grad, near, far, source, vec],
        name="norm_back",
    )


def attention_backward_kernel(first, signed, qkv, out, heads, *refs):
    refs = list(refs)
    info, kept_ref, own, other, proj, lse = [refs.pop(0) for unused in range(6)]
    pieces, out_pieces = take_refs(refs, qkv, out)
    if first:
        tokens = refs.pop(0)
    gm_ref, gp_ref, sent, kept = [refs.pop(0) for unused in range(4)]
    if first:
        sums = refs.pop(0)
    w, w_out, partial, gatt, gk_sum, gv_sum = refs
    me, low = info[0], info[1]
    qkv.load(pieces, w, me)
    out.load(out_pieces, w_out, me)
    part = w_out.shape[0]
    hd = part // heads
    group = gm_ref.shape[0]
    block = group // 4
    gather_halves(low, own, other, gm_ref)
    gatt[...] = dot(gm_ref[...], w_out[...].astype(BF), 1, 1).astype(BF)
    scale = hd ** (-0.5)
    gp_ref[:, 3 * part :] = jnp.zeros((group, gp_ref.shape[1] - 3 * part), BF)
    for b in reversed(range(4)):
        keys = (b + 1) * block
        rows = slice(b * block, keys)
        allowed = block_allowed(info, kept_ref, b, block, keys)
        for h in range(heads):
            cols = slice(h * hd, (h + 1) * hd)
            q = proj[rows, h * hd : (h + 1) * hd] * scale
            k = proj[:keys, part + h * hd : part + (h + 1) * hd]
            v = proj[:keys, 2 * part + h * hd : 2 * part + (h + 1) * hd]
            g = gatt[rows, h * hd : (h + 1) * hd]
            level = lse[rows, h : h + 1]
            scores = dot(q, k, 1, 1)
            magnitude = jnp.abs(scores) if signed else scores
            absolute = jnp.exp(jnp.where(allowed, magnitude, FLOOR_VALUE) - level)
            grad_weights = dot(g, v, 1, 1)
            if signed:
                lifted = jnp.where(allowed, absolute - jnp.exp(-level), 0.0)
                weights = jnp.where(scores < 0, -lifted, lifted)
                delta = jnp.sum(grad_weights * weights, axis=-1, keepdims=True)
                shift = jnp.where(scores > 0, delta, jnp.where(scores < 0, -delta, 0.0))
            else:
                weights = absolute
                shift = jnp.sum(grad_weights * weights, axis=-1, keepdims=True)
            gs = (absolute * (grad_weights - shift)).astype(BF)
            gp_ref[rows, h * hd : (h + 1) * hd] = (dot(gs, k, 1, 0) * scale).astype(BF)
            gk = dot(gs, q, 0, 0)
            gv = dot(weights.astype(BF), g, 0, 0)
            if b == 3:
                gk_sum[h] = gk
                gv_sum[h] = gv
            else:
                gk_sum[h, :keys] += gk
                gv_sum[h, :keys] += gv
    for h in range(heads):
        gp_ref[:, part + h * hd : part + (h + 1) * hd] = gk_sum[h].astype(BF)
        gp_ref[:, 2 * part + h * hd : 2 * part + (h + 1) * hd] = gv_sum[h].astype(BF)
    partial[...] = dot(gp_ref[...], w[...], 1, 1)
    split_halves(low, partial, kept, sent)
    if first:
        gain = bias = 0.0
        for b in range(4):
            rows = slice(b * block, (b + 1) * block)
            normal, unused = norm_parts(tokens[rows, :].astype(F32))
            value = partial[rows, :]
            gain = gain + jnp.sum(value * normal, axis=0, keepdims=True)
            bias = bias + jnp.sum(value, axis=0, keepdims=True)
        sums[0:1, :] = gain
        sums[1:2, :] = bias


def attention_backward(first, signed, info, kept, own, other, proj, lse, qkv, out, tokens, heads):
    half, width = own.shape
    group = 2 * half
    part = out.shape[0]
    wide = qkv.shape[1]
    outs = [((group, width), BF), ((group, wide), BF), ((half, width), BF), ((half, width), F32)]
    if first:
        outs += [((2, width), F32)]
    return call(
        functools.partial(attention_backward_kernel, first, signed, qkv, out, heads),
        outs,
        [info, kept, own, other, proj, lse, *qkv.arrays, *out.arrays] + ([tokens] if first else []),
        [
            qkv.scratch(),
            out.scratch(),
            pltpu.VMEM((group, width), F32),
            pltpu.VMEM((group, part), BF),
            pltpu.VMEM((heads, group, part // heads), F32),
            pltpu.VMEM((heads, group, part // heads), F32),
        ],
        flops=2 * group * width * 4 * part,
        name="attend_back",
    )


def outer_kernel(parts, plans, relative, *refs):
    info, scratch = refs[0], refs[-1]
    outs = refs[-3:-1] if relative else refs[-2:-1]
    start = 0
    for segments, rows, slot, span in plans:
        size = rows // parts

        def place(p):
            return place_of(p, span, parts // span) if span else p

        total = None
        for left, first, right, second, count in segments:
            term = dot(refs[left][first : first + count, :], refs[right][second : second + count, :], 0, 0)
            total = term if total is None else total + term
        scratch[:rows, :] = total
        for j in range(parts // 2 if relative else parts):
            if relative:
                targets = [at(place(info[0] ^ (2 * j + 1)), size), at(place(info[0] ^ (2 * j)), size)]
            else:
                targets = [slice(place(j) * size, (place(j) + 1) * size)]
            for ref, target in zip(outs, targets):
                ref[j, start : start + size, :] = scratch[target, :].astype(BF)
                if slot > size:
                    ref[j, start + size : start + slot, :] = jnp.zeros((slot - size, scratch.shape[1]), BF)
        start += slot


def slot_of(size):
    return (size + 15) // 16 * 16


def outer(parts, info, pairs, relative):
    arrays, plans = [info], []

    def number(a):
        for n, other in enumerate(arrays):
            if other is a:
                return n
        arrays.append(a)
        return len(arrays) - 1

    for segments, span in pairs:
        rows = segments[0][0].shape[1]
        numbers = [(number(a), first, number(b), second, count) for a, first, b, second, count in segments]
        plans.append((numbers, rows, slot_of(rows // parts), span))
    cols = pairs[0][0][0][2].shape[1]
    tall = sum(p[2] for p in plans)
    outs = [((parts // 2, tall, cols), BF)] * 2 if relative else [((parts, tall, cols), BF)]
    return call(
        functools.partial(outer_kernel, parts, plans, relative),
        outs,
        arrays,
        [pltpu.VMEM((max(p[1] for p in plans), cols), F32)],
        flops=sum(2 * p[1] * cols * sum(seg[4] for seg in p[0]) for p in plans),
        name="outer",
    )


def tie(*values):
    return lax.optimization_barrier(values)


def swap(x, axis, bit):
    size = lax.axis_size(axis)
    return lax.ppermute(x, axis, [(i, i ^ bit) for i in range(size)])


def row_moves(pb, ka):
    span = pb // ka
    return [(p * ka + k, (k * span + p % span) * ka + p // span) for p in range(pb) for k in range(ka)]


def gather_rows(x):
    return lax.all_gather(x, "pb", axis=0, tiled=True)


def whole_rows(x, parts, start, size, span=0):
    piece = x.shape[0] // parts
    return Rows([x], [(0, p * piece + start, p, False) for p in range(parts)], size, span)


class Spread:
    def __init__(self, x, parts):
        self.x, self.parts = x, parts
        if parts > 8:
            self.all = gather_rows(x)
        else:
            self.near = [x] + [swap(x, "pb", 2 * d) for d in range(1, parts // 2)]

    def turn(self, after):
        if self.parts > 8:
            return
        after, *self.near = tie(after, *self.near)
        self.far = swap(jnp.concatenate(self.near, axis=0), "pb", 1)

    def rows(self, size=None, span=0):
        rows, parts = self.x.shape[0], self.parts
        size = size or rows
        if parts > 8:
            return whole_rows(self.all, parts, 0, size, span)
        plan = [(d, 0, 2 * d, True) for d in range(parts // 2)]
        plan += [(parts // 2, d * rows, 2 * d + 1, True) for d in range(parts // 2)]
        return Rows(self.near + [self.far], plan, size, span)


def direct_rows(x, parts):
    if parts > 8:
        return whole_rows(gather_rows(x), parts, 0, x.shape[0])
    return Rows([x] + [swap(x, "pb", d) for d in range(1, parts)], [(d, 0, d, True) for d in range(parts)], x.shape[0])


class Flow:
    def __init__(self, info, pairs, parts):
        self.parts = parts
        if parts > 8:
            (x,) = outer(parts, info, pairs, False)
            self.done = lax.psum_scatter(x.reshape(-1, x.shape[2]), "pb", scatter_dimension=0, tiled=True)
            self.made = self.kept = x
            return
        sent, self.kept = outer(parts, info, pairs, True)
        self.got = swap(sent, "pb", 1)
        self.made = self.kept

    def turn(self, after):
        if self.parts > 8:
            return
        after, self.kept, self.got = tie(after, self.kept, self.got)
        near = (self.kept.astype(F32) + self.got.astype(F32)).astype(BF)
        self.kept = near[0]
        self.got = [swap(near[d], "pb", 2 * d) for d in range(1, self.parts // 2)]

    def end(self, after):
        if self.parts > 8:
            return self.done
        after, self.kept, *self.got = tie(after, self.kept, *self.got)
        total = self.kept.astype(F32)
        for part in self.got:
            total = total + part.astype(F32)
        return total.astype(BF)


def gather_ka(x):
    far = swap(x, "ka", 2)
    both = swap(jnp.stack([x, far]), "ka", 1)
    me = lax.axis_index("ka")
    pair = jnp.stack([x, far])
    even = jnp.where(me % 2 == 0, pair, both)
    odd = jnp.where(me % 2 == 0, both, pair)
    first = jnp.where(me < 2, even, even[::-1])
    second = jnp.where(me < 2, odd, odd[::-1])
    return [first[0], second[0], first[1], second[1]]


def on_device(tokens, cotangent, lengths, keep_mask, w_qkv, w_out, w_fc, w_proj, norm_gain, norm_bias):
    rows, width = tokens.shape
    pb = lax.axis_size("pb")
    ka = lax.axis_size("ka")
    span = pb // ka
    me = lax.axis_index("ka")
    low, high = me % 2, me // 2
    heads = H // ka
    part = width // ka
    ff = w_fc.shape[2]
    ff_part = ff // ka
    d_rows = w_qkv.shape[0]
    out_rows = w_out.shape[0] // ka
    proj_rows = w_proj.shape[0] // ka
    wide = (3 * part + 8 + 127) // 128 * 128
    moves = row_moves(pb, ka)
    bounds = jnp.cumsum(lengths[0])
    info = jnp.concatenate([jnp.stack([lax.axis_index("pb"), low]).astype(jnp.int32), bounds.astype(jnp.int32)])

    def local_qkv(l):
        return lax.dynamic_index_in_dim(w_qkv[:, l].reshape(d_rows, 3, ka, part), me, 2, False).reshape(d_rows, 3 * part)

    vectors = jnp.concatenate([norm_gain, norm_bias], axis=1)
    first = jnp.concatenate([local_qkv(0), vectors, jnp.zeros((d_rows, wide - 3 * part - 8), BF)], axis=1)
    qkv = [direct_rows(first, pb), None]
    first, w_out_in, w_proj_in = tie(first, w_out, w_proj)
    local_out = lax.dynamic_slice_in_dim(w_out_in, me * out_rows, out_rows, 0)
    local_proj = lax.dynamic_slice_in_dim(w_proj_in, me * proj_rows, proj_rows, 0)
    slot = slot_of(out_rows)

    def filled(x):
        return jnp.pad(x, ((0, slot - out_rows), (0, 0)))

    tall = jnp.concatenate([filled(local_out[:, 0]), filled(local_out[:, 1]), local_proj[:, 0], local_proj[:, 1]], axis=0)
    tall = lax.ppermute(tall, ("pb", "ka"), moves)
    kept_all = lax.all_gather(keep_mask, "ka", axis=0, tiled=True).reshape(1, -1)
    tokens_all = lax.all_gather(tokens, "ka", axis=0, tiled=True)
    tokens_all, tall, w_fc_in, cotangent_in = tie(tokens_all, tall, w_fc, cotangent)
    local_fc = lax.dynamic_slice_in_dim(w_fc_in, me * ff_part, ff_part, 2)
    out0 = Spread(tall[:slot], pb)
    tall_a = gather_rows(tall[slot : 2 * slot + proj_rows])
    fc0 = Spread(local_fc[:, 0], pb)
    tall_b = gather_rows(jnp.concatenate([local_fc[:, 1], tall[2 * slot + proj_rows :]], axis=0))
    cotangent_all = lax.all_gather(cotangent_in, "ka", axis=0, tiled=True)
    fc = [None, whole_rows(tall_b, pb, 0, d_rows)]
    proj = [whole_rows(tall_a, pb, slot, proj_rows, span), whole_rows(tall_b, pb, d_rows, proj_rows, span)]
    out0.turn(cotangent_all)
    out = [out0.rows(out_rows, span), whole_rows(tall_a, pb, 0, out_rows, span)]

    def partial_sums(sent, kept):
        near = (kept + swap(sent, "ka", 1).astype(F32)).astype(BF)
        return near, swap(near, "ka", 2)

    def block(half, which):
        return lax.dynamic_slice_in_dim(half, which * rows, rows, 0)

    keys = ("stream", "x", "projected", "attended", "lse", "middle", "own", "other", "hidden", "active")
    got = attention_forward(True, True, info, kept_all, [tokens_all], qkv[0], out[0], heads)
    x_all, projected, attended, lse, sent, kept, stream, vec = got
    near, far = partial_sums(sent, kept)
    fc0.turn(near)
    fc[0] = fc0.rows()
    second = jnp.concatenate([local_qkv(1), jnp.zeros((d_rows, wide - 3 * part), BF)], axis=1)
    second, unused = tie(second, near)
    qkv1 = Spread(second, pb)
    middle, own = norm_after(1, stream, near, far, vec)
    other = swap(own, "ka", 1)
    hidden, active, sent, kept = feed_forward(info, own, other, fc[0], proj[0])
    kept0 = dict(zip(keys, (stream, x_all, projected, attended, lse, middle, own, other, hidden, active)))
    near, far = partial_sums(sent, kept)
    qkv1.turn(near)
    qkv[1] = qkv1.rows()
    stream, own = norm_after(2, middle, near, far, vec)
    other = swap(own, "ka", 1)
    got = attention_forward(False, False, info, kept_all, [own, other], qkv[1], out[1], heads)
    x_all, projected, attended, lse, sent, kept = got
    near, far = partial_sums(sent, kept)
    middle, own = norm_after(3, stream, near, far, vec)
    other = swap(own, "ka", 1)
    hidden, active, last_sent, last_kept = feed_forward(info, own, other, fc[1], proj[1])
    kept1 = dict(zip(keys, (stream, x_all, projected, attended, lse, middle, own, other, hidden, active)))

    cot = cotangent_all.reshape(2, 2, rows, width)
    branch = [lax.dynamic_index_in_dim(cot, i, 1, False).reshape(2 * rows, width) for i in (low, 1 - low)]
    sums = [None] * 4
    half, group = 2 * rows, 4 * rows

    def fc_pair(kept, grad_hidden):
        return [(kept["own"], 0, grad_hidden, 0, half), (kept["other"], 0, grad_hidden, half, half)], 0

    def proj_pair(kept, branch):
        return [(kept["active"], 0, branch[0], 0, half), (kept["active"], half, branch[1], 0, half)], span

    def attend_back(l, kept, own):
        return attention_backward(
            l == 0, l == 0, info, kept_all, own, swap(own, "ka", 1), kept["projected"], kept["lse"], qkv[l], out[l], tokens_all, heads
        )

    grad_hidden, sent, kept = feed_backward(info, branch[0], branch[1], kept1["hidden"], fc[1], proj[1])
    near, far = partial_sums(sent, kept)
    near_in, grad_hidden, last_sent, last_kept = tie(near, grad_hidden, last_sent, last_kept)
    last = (last_kept + swap(last_sent, "ka", 1).astype(F32)).astype(BF)
    last_far = swap(block(last, 1 - high), "ka", 2)
    flow_a = Flow(info, [fc_pair(kept1, grad_hidden), proj_pair(kept1, branch)], pb)
    far, unused = tie(far, flow_a.made)
    grad, own, sums[3] = norm_back(3, branch[0], near, far, kept1["middle"], vec)
    middle_all1, grad_projected, sent, kept = attend_back(1, kept1, own)
    near, far = partial_sums(sent, kept)
    near_in, grad_projected, last_far = tie(near, grad_projected, last_far)
    output = (block(kept1["middle"], high) + (block(last, high).astype(F32) + last_far.astype(F32))).astype(BF)
    flow_b = Flow(info, [([(kept1["x"], 0, grad_projected, 0, group)], 0)], pb)
    flow_a.turn(near)
    far, unused = tie(far, flow_b.made)
    grad, own, sums[2] = norm_back(2, grad, near, far, kept1["stream"], vec)
    branch = [own, swap(own, "ka", 1)]
    grad_hidden, sent, kept = feed_backward(info, branch[0], branch[1], kept0["hidden"], fc[0], proj[0])
    near, far = partial_sums(sent, kept)
    near_in, grad_hidden, middle_all1 = tie(near, grad_hidden, middle_all1)
    flow_c = Flow(info, [fc_pair(kept0, grad_hidden)], pb)
    flow_d = Flow(info, [proj_pair(kept0, branch), ([(kept1["attended"], 0, middle_all1, 0, group)], span)], pb)
    flow_b.turn(near)
    far, *unused = tie(far, flow_c.made, flow_d.made)
    grad, own, sums[1] = norm_back(1, grad, near, far, kept0["middle"], vec)
    fc_proj1 = flow_a.end(own)
    middle_all, grad_projected, sent, kept, sums[0] = attend_back(0, kept0, own)
    near = (kept + swap(sent, "ka", 1).astype(F32)).astype(BF)
    far = swap(block(near, 1 - high), "ka", 2)
    near_in, grad_projected, middle_all = tie(near, grad_projected, middle_all)
    flow_f = Flow(info, [([(kept0["attended"], 0, middle_all, 0, group)], span)], pb)
    halved = [sums[0]] + [0.5 * s for s in sums[1:]]
    stacked = jnp.concatenate([s[i : i + 1] for i in range(2) for s in halved] + [jnp.zeros((8, width), F32)], axis=0).astype(BF)
    spots = (3 * part + jnp.arange(16)[:, None] == jnp.arange(wide)[None, :]) & (jnp.arange(16)[:, None] < 8)
    flow_e = Flow(info, [([(kept0["x"], 0, grad_projected, 0, group), (stacked, 0, spots.astype(BF), 0, 16)], 0)], pb)
    flow_c.turn(near)
    (grad_tokens,) = norm_back(0, block(grad, high), block(near, high), far, block(kept0["stream"], high), vec, True)

    back = [(b, a) for a, b in moves]
    proj1 = lax.ppermute(fc_proj1[slot_of(d_rows) :], ("pb", "ka"), back)
    wide1 = gather_ka(jnp.concatenate([fc_proj1[: slot_of(d_rows)], proj1], axis=0))
    qkv1 = gather_ka(flow_b.end(near))
    flow_d.turn(flow_e.made)
    fc0 = gather_ka(flow_c.end(flow_e.made))
    flow_f.turn(flow_d.kept)
    flow_e.turn(flow_d.kept)
    tall0 = gather_ka(lax.ppermute(flow_d.end(flow_e.kept), ("pb", "ka"), back))
    tall1 = gather_ka(lax.ppermute(flow_f.end(flow_e.kept), ("pb", "ka"), back))
    qkv0 = gather_ka(flow_e.end(flow_e.kept))

    def columns(pieces):
        return jnp.concatenate([p[:d_rows] for p in pieces], axis=1)

    def heads_of(pieces):
        return jnp.concatenate([p[:d_rows, i * part : (i + 1) * part] for i in range(3) for p in pieces], axis=1)

    def rows_of(pieces, start, size):
        return jnp.concatenate([p[start : start + size] for p in pieces], axis=0)

    shift = slot_of(d_rows)
    summed = (
        (heads_of(qkv0), heads_of(qkv1)),
        (rows_of(tall1, 0, out_rows), rows_of(tall0, slot_of(proj_rows), out_rows)),
        (columns(fc0), columns(wide1)),
        (rows_of(tall0, 0, proj_rows), rows_of(wide1, shift, proj_rows)),
    )
    summed = [jnp.stack(pair, axis=1).astype(F32) for pair in summed]
    stacked = sum(p[:d_rows, 3 * part : 3 * part + 8].astype(F32) for p in qkv0)
    return (output, grad_tokens, *summed, stacked[:, :4], stacked[:, 4:])


def solution(mesh):
    return jax.shard_map(
        on_device,
        mesh=mesh,
        in_specs=(
            P(("pb", "ka"), None),
            P(("pb", "ka"), None),
            P("pb", None),
            P(("pb", "ka")),
            P("pb", None, None),
            P("pb", None, None),
            P("pb", None, None),
            P("pb", None, None),
            P("pb", None),
            P("pb", None),
        ),
        out_specs=(
            P(("pb", "ka"), None),
            P(("pb", "ka"), None),
            P("pb", None, None),
            P("pb", None, None),
            P("pb", None, None),
            P("pb", None, None),
            P("pb", None),
            P("pb", None),
        ),
        check_vma=False,
    )
```

```python
import functools
import jax
import jax.numpy as jnp
from jax import lax
from jax.experimental import pallas as pl
from jax.experimental.pallas import tpu as pltpu
from jax.sharding import PartitionSpec as P

H = 12
EPSILON = 1e-05
FLOOR_VALUE = -1e30
BF = jnp.bfloat16
F32 = jnp.float32
VM = pl.BlockSpec(memory_space=pltpu.VMEM)
SM = pl.BlockSpec(memory_space=pltpu.SMEM)
SHIFTS = (0, 4, 2, 6)
GELU_A = 0.7978845608028654
GELU_B = 0.044715


def dot(a, b, ca, cb):
    return lax.dot_general(a, b, (((ca,), (cb,)), ((), ())), preferred_element_type=F32)


def call(kernel, outs, ins, scratch=(), flops=0, name=None):
    moved = sum(a.size * a.dtype.itemsize for a in ins)
    return pl.pallas_call(
        kernel,
        out_shape=[jax.ShapeDtypeStruct(s, t) for s, t in outs],
        in_specs=[SM if a.dtype == jnp.int32 and a.ndim == 1 else VM for a in ins],
        out_specs=[VM] * len(outs),
        scratch_shapes=list(scratch),
        compiler_params=pltpu.CompilerParams(vmem_limit_bytes=40 * 1024 * 1024),
        cost_estimate=pl.CostEstimate(flops=flops, bytes_accessed=moved, transcendentals=0),
        name=name,
    )(*ins)


def at(index, rows):
    return pl.ds(pl.multiple_of(index * rows, rows), rows)


class Rows:
    def __init__(self, arrays, plan, size, span=0):
        self.arrays, self.plan, self.size, self.span = arrays, plan, size, span
        self.shape = (size * len(plan), arrays[0].shape[1])

    def scratch(self):
        return pltpu.VMEM(self.shape, F32 if self.size % 16 else BF)

    def load(self, refs, scratch, me):
        for index, start, p, relative in self.plan:
            place = me ^ p if relative else p
            if self.span:
                place = place_of(place, self.span, len(self.plan) // self.span)
            target = at(place, self.size) if relative else slice(place * self.size, (place + 1) * self.size)
            scratch[target, :] = refs[index][start : start + self.size, :].astype(scratch.dtype)


def place_of(p, span, ka):
    return (p % span) * ka + p // span if isinstance(p, int) else lax.rem(p, span) * ka + lax.div(p, span)


def take_refs(refs, *weights):
    return [[refs.pop(0) for unused in w.arrays] for w in weights]


def norm_parts(values):
    average = jnp.mean(values, axis=-1, keepdims=True)
    centered = values - average
    spread = jnp.mean(centered * centered, axis=-1, keepdims=True)
    inverse = lax.rsqrt(spread + EPSILON)
    return centered * inverse, inverse


def block_allowed(info, kept_ref, b, block, keys):
    i = b * block + lax.broadcasted_iota(jnp.int32, (block, 1), 0)
    j = lax.broadcasted_iota(jnp.int32, (1, keys), 1)

    def segment(t):
        total = jnp.zeros_like(t)
        for n in range(2, info.shape[0]):
            total = total + jnp.where(t >= info[n], 1, 0)
        return total

    same = segment(i) == segment(j)
    itself = i == j
    return same & (j <= i) & ((kept_ref[:, :keys] > 0) | itself)


def canonical(both, full):
    block = both.shape[1] // 2
    for h in range(2):
        for i in range(2):
            full[(2 * i + h) * block : (2 * i + h + 1) * block, :] = both[h, i * block : (i + 1) * block, :]


def split_halves(low, full, kept, sent):
    block = kept.shape[0] // 2
    for i in range(2):
        kept[i * block : (i + 1) * block, :] = full[at(2 * i + low, block), :].astype(kept.dtype)
        sent[i * block : (i + 1) * block, :] = full[at(2 * i + 1 - low, block), :].astype(sent.dtype)


def attention_forward_kernel(first, signed, qkv, heads, *refs):
    refs = list(refs)
    info, kept_ref, both = [refs.pop(0) for unused in range(3)]
    (pieces,) = take_refs(refs, qkv)
    x_ref, proj_ref, att_ref, lse_ref = [refs.pop(0) for unused in range(4)]
    if first:
        tokens, vec_ref = refs.pop(0), refs.pop(0)
    (w,) = refs
    me, low = info[0], info[1]
    qkv.load(pieces, w, me)
    part = att_ref.shape[1]
    hd = part // heads
    group, width = x_ref.shape
    block = group // 4
    if first:
        tail = w.shape[1] - 3 * part
        pick = lax.broadcasted_iota(jnp.int32, (8, tail), 0) == lax.broadcasted_iota(jnp.int32, (8, tail), 1)
        vec = dot(pick.astype(F32).astype(BF), w[:, 3 * part :], 1, 1)
        vec_ref[...] = vec
        canonical(both, tokens)
        for b in range(4):
            values = tokens[b * block : (b + 1) * block, :].astype(F32)
            normal, unused = norm_parts(values)
            x_ref[b * block : (b + 1) * block, :] = (normal * vec[0:1] + vec[4:5]).astype(BF)
    else:
        canonical(both, x_ref)
    proj_ref[...] = dot(x_ref[...], w[...], 1, 0).astype(BF)
    scale = hd ** (-0.5)
    for b in range(4):
        keys = (b + 1) * block
        rows = slice(b * block, keys)
        allowed = block_allowed(info, kept_ref, b, block, keys)
        for h in range(heads):
            q = proj_ref[rows, h * hd : (h + 1) * hd] * scale
            k = proj_ref[:keys, part + h * hd : part + (h + 1) * hd]
            v = proj_ref[:keys, 2 * part + h * hd : 2 * part + (h + 1) * hd]
            scores = dot(q, k, 1, 1)
            magnitude = jnp.abs(scores) if signed else scores
            masked = jnp.where(allowed, magnitude, FLOOR_VALUE)
            peak = jnp.max(masked, axis=-1, keepdims=True)
            raised = jnp.exp(masked - peak)
            total = jnp.sum(raised, axis=-1, keepdims=True)
            if signed:
                lifted = jnp.where(allowed, raised - jnp.exp(-peak), 0.0)
                raised = jnp.where(scores < 0, -lifted, lifted)
            weights = (raised * (1.0 / total)).astype(BF)
            att_ref[rows, h * hd : (h + 1) * hd] = dot(weights, v, 1, 0).astype(BF)
            lse_ref[rows, h : h + 1] = peak + jnp.log(total)


def attention_forward(first, signed, info, kept, both, qkv, part, heads):
    group = kept.shape[1]
    width = both.shape[2]
    outs = [((group, width), BF), ((group, qkv.shape[1]), BF), ((group, part), BF), ((group, 128), F32)]
    if first:
        outs += [((group, width), BF), ((8, width), F32)]
    return call(
        functools.partial(attention_forward_kernel, first, signed, qkv, heads),
        outs,
        [info, kept, both, *qkv.arrays],
        [qkv.scratch()],
        flops=2 * group * width * 3 * part,
        name="attend",
    )


def attention_out_kernel(out, *refs):
    refs = list(refs)
    info, attended = refs.pop(0), refs.pop(0)
    (pieces,) = take_refs(refs, out)
    sent, kept, w_out, partial = refs
    out.load(pieces, w_out, info[0])
    partial[...] = dot(attended[...], w_out[...].astype(BF), 1, 0)
    split_halves(info[1], partial, kept, sent)


def attention_out(info, attended, out):
    group, width = attended.shape[0], out.shape[1]
    return call(
        functools.partial(attention_out_kernel, out),
        [((group // 2, width), BF), ((group // 2, width), F32)],
        [info, attended, *out.arrays],
        [out.scratch(), pltpu.VMEM((group, width), F32)],
        flops=2 * group * width * out.shape[0],
        name="attend_out",
    )


def gelu_parts(v):
    inner = GELU_A * (v + GELU_B * v * v * v)
    return jnp.tanh(inner)


def feed_forward_kernel(fc, proj, *refs):
    refs = list(refs)
    info, both = [refs.pop(0) for unused in range(2)]
    fc_refs, proj_refs = take_refs(refs, fc, proj)
    hidden, active, sent, kept, w, w_proj, partial = refs
    fc.load(fc_refs, w, info[0])
    proj.load(proj_refs, w_proj, info[0])
    half = both.shape[1]
    ff = w_proj.shape[0]
    step = ff // 3
    for h in range(2):
        rows = slice(h * half, (h + 1) * half)
        total = None
        for f in range(3):
            cols = slice(f * step, (f + 1) * step)
            hid = dot(both[h], w[:, cols], 1, 0)
            hidden[rows, cols] = hid
            act = (0.5 * hid * (1.0 + gelu_parts(hid))).astype(BF)
            active[rows, cols] = act
            term = dot(act, w_proj[cols, :], 1, 0)
            total = term if total is None else total + term
        partial[h] = total
    kept[...] = partial[info[1]]
    sent[...] = partial[1 - info[1]].astype(BF)


def feed_forward(info, both, fc, proj):
    two, half, width = both.shape
    ff = proj.shape[0]
    outs = [((2 * half, ff), F32), ((2 * half, ff), BF), ((half, width), BF), ((half, width), F32)]
    return call(
        functools.partial(feed_forward_kernel, fc, proj),
        outs,
        [info, both, *fc.arrays, *proj.arrays],
        [fc.scratch(), proj.scratch(), pltpu.VMEM((2, half, width), F32)],
        flops=8 * half * width * ff,
        name="feed",
    )


def norm_kernel(row, stream, near, far, vec, middle, normed):
    values = stream[...].astype(F32) + (near[...].astype(F32) + far[...].astype(F32))
    middle[...] = values
    normal, unused = norm_parts(values)
    normed[...] = (normal * vec[row : row + 1, :] + vec[row + 4 : row + 5, :]).astype(BF)


def norm_after(row, stream, near, far, vec):
    shape = stream.shape
    return call(functools.partial(norm_kernel, row), [(shape, F32), (shape, BF)], [stream, near, far, vec], name="norm")


def feed_backward_kernel(fc, proj, *refs):
    refs = list(refs)
    info, both, hidden = [refs.pop(0) for unused in range(3)]
    fc_refs, proj_refs = take_refs(refs, fc, proj)
    grad_hidden, sent, kept, w, w_proj, partial = refs
    fc.load(fc_refs, w, info[0])
    proj.load(proj_refs, w_proj, info[0])
    half = both.shape[1]
    ff = w_proj.shape[0]
    step = ff // 3
    for h in range(2):
        rows = slice(h * half, (h + 1) * half)
        total = None
        for f in range(3):
            cols = slice(f * step, (f + 1) * step)
            grad_active = dot(both[h], w_proj[cols, :], 1, 1)
            v = hidden[rows, cols]
            t = gelu_parts(v)
            slope = 0.5 * (1.0 + t) + 0.5 * v * (1.0 - t * t) * (GELU_A * (1.0 + 3.0 * GELU_B * v * v))
            gh = (slope * grad_active).astype(BF)
            grad_hidden[rows, cols] = gh
            term = dot(gh, w[:, cols], 1, 1)
            total = term if total is None else total + term
        partial[h] = total
    kept[...] = partial[info[1]]
    sent[...] = partial[1 - info[1]].astype(BF)


def feed_backward(info, both, hidden, fc, proj):
    two, half, width = both.shape
    ff = proj.shape[0]
    outs = [((2 * half, ff), BF), ((half, width), BF), ((half, width), F32)]
    return call(
        functools.partial(feed_backward_kernel, fc, proj),
        outs,
        [info, both, hidden, *fc.arrays, *proj.arrays],
        [fc.scratch(), proj.scratch(), pltpu.VMEM((2, half, width), F32)],
        flops=8 * half * width * ff,
        name="feed_back",
    )


def norm_backward_kernel(row, grad, near, far, source, vec, out, *rest):
    incoming = near[...].astype(F32) + far[...].astype(F32)
    normal, inverse = norm_parts(source[...].astype(F32))
    grad_normal = incoming * vec[row : row + 1, :]
    mean_grad = jnp.mean(grad_normal, axis=-1, keepdims=True)
    mean_cross = jnp.mean(grad_normal * normal, axis=-1, keepdims=True)
    value = grad[...].astype(F32) + inverse * (grad_normal - mean_grad - normal * mean_cross)
    out[...] = value
    if not rest:
        return
    low, sums = rest
    low[...] = value.astype(BF)
    sums[0:1, :] = jnp.sum(incoming * normal, axis=0, keepdims=True)
    sums[1:2, :] = jnp.sum(incoming, axis=0, keepdims=True)


def norm_back(row, grad, near, far, source, vec, last=False):
    shape = source.shape
    return call(
        functools.partial(norm_backward_kernel, row),
        [(shape, F32)] if last else [(shape, F32), (shape, BF), ((2, shape[1]), F32)],
        [grad, near, far, source, vec],
        name="norm_back",
    )


def attention_backward_kernel(first, signed, qkv, out, heads, *refs):
    refs = list(refs)
    info, kept_ref, both, proj, lse = [refs.pop(0) for unused in range(5)]
    pieces, out_pieces = take_refs(refs, qkv, out)
    if first:
        tokens = refs.pop(0)
    gm_ref, gp_ref, sent, kept = [refs.pop(0) for unused in range(4)]
    if first:
        sums = refs.pop(0)
    w, w_out, partial, gatt, gk_sum, gv_sum = refs
    me, low = info[0], info[1]
    qkv.load(pieces, w, me)
    out.load(out_pieces, w_out, me)
    part = w_out.shape[0]
    hd = part // heads
    group = gm_ref.shape[0]
    block = group // 4
    canonical(both, gm_ref)
    gatt[...] = dot(gm_ref[...], w_out[...].astype(BF), 1, 1).astype(BF)
    scale = hd ** (-0.5)
    gp_ref[:, 3 * part :] = jnp.zeros((group, gp_ref.shape[1] - 3 * part), BF)
    for b in reversed(range(4)):
        keys = (b + 1) * block
        rows = slice(b * block, keys)
        allowed = block_allowed(info, kept_ref, b, block, keys)
        for h in range(heads):
            cols = slice(h * hd, (h + 1) * hd)
            q = proj[rows, h * hd : (h + 1) * hd] * scale
            k = proj[:keys, part + h * hd : part + (h + 1) * hd]
            v = proj[:keys, 2 * part + h * hd : 2 * part + (h + 1) * hd]
            g = gatt[rows, h * hd : (h + 1) * hd]
            level = lse[rows, h : h + 1]
            scores = dot(q, k, 1, 1)
            magnitude = jnp.abs(scores) if signed else scores
            absolute = jnp.exp(jnp.where(allowed, magnitude, FLOOR_VALUE) - level)
            grad_weights = dot(g, v, 1, 1)
            if signed:
                lifted = jnp.where(allowed, absolute - jnp.exp(-level), 0.0)
                weights = jnp.where(scores < 0, -lifted, lifted)
                delta = jnp.sum(grad_weights * weights, axis=-1, keepdims=True)
                shift = jnp.where(scores > 0, delta, jnp.where(scores < 0, -delta, 0.0))
            else:
                weights = absolute
                shift = jnp.sum(grad_weights * weights, axis=-1, keepdims=True)
            gs = (absolute * (grad_weights - shift)).astype(BF)
            gp_ref[rows, h * hd : (h + 1) * hd] = (dot(gs, k, 1, 0) * scale).astype(BF)
            gk = dot(gs, q, 0, 0)
            gv = dot(weights.astype(BF), g, 0, 0)
            if b == 3:
                gk_sum[h] = gk
                gv_sum[h] = gv
            else:
                gk_sum[h, :keys] += gk
                gv_sum[h, :keys] += gv
    for h in range(heads):
        gp_ref[:, part + h * hd : part + (h + 1) * hd] = gk_sum[h].astype(BF)
        gp_ref[:, 2 * part + h * hd : 2 * part + (h + 1) * hd] = gv_sum[h].astype(BF)
    partial[...] = dot(gp_ref[...], w[...], 1, 1)
    split_halves(low, partial, kept, sent)
    if first:
        gain = bias = 0.0
        for b in range(4):
            rows = slice(b * block, (b + 1) * block)
            normal, unused = norm_parts(tokens[rows, :].astype(F32))
            value = partial[rows, :]
            gain = gain + jnp.sum(value * normal, axis=0, keepdims=True)
            bias = bias + jnp.sum(value, axis=0, keepdims=True)
        sums[0:1, :] = gain
        sums[1:2, :] = bias


def attention_backward(first, signed, info, kept, both, proj, lse, qkv, out, tokens, heads):
    two, half, width = both.shape
    group = 2 * half
    part = out.shape[0]
    wide = qkv.shape[1]
    outs = [((group, width), BF), ((group, wide), BF), ((half, width), BF), ((half, width), F32)]
    if first:
        outs += [((2, width), F32)]
    return call(
        functools.partial(attention_backward_kernel, first, signed, qkv, out, heads),
        outs,
        [info, kept, both, proj, lse, *qkv.arrays, *out.arrays] + ([tokens] if first else []),
        [
            qkv.scratch(),
            out.scratch(),
            pltpu.VMEM((group, width), F32),
            pltpu.VMEM((group, part), BF),
            pltpu.VMEM((heads, group, part // heads), F32),
            pltpu.VMEM((heads, group, part // heads), F32),
        ],
        flops=2 * group * width * 4 * part,
        name="attend_back",
    )


def outer_kernel(parts, plans, relative, *refs):
    info, scratch = refs[0], refs[-1]
    outs = refs[-3:-1] if relative else refs[-2:-1]
    start = 0
    for segments, rows, slot, span, cols in plans:
        size = rows // parts
        blank = scratch.shape[1] - cols

        def place(p):
            return place_of(p, span, parts // span) if span else p

        total = None
        for left, first, right, second, count in segments:
            term = dot(refs[left][first : first + count, :], refs[right][second : second + count, :], 0, 0)
            total = term if total is None else total + term
        scratch[:rows, :cols] = total
        if blank:
            scratch[:rows, cols:] = jnp.zeros((rows, blank), F32)
        for j in range(len(SHIFTS) if relative else parts):
            if relative:
                targets = [at(place(info[0] ^ (SHIFTS[j] + 1)), size), at(place(info[0] ^ SHIFTS[j]), size)]
            else:
                targets = [slice(place(j) * size, (place(j) + 1) * size)]
            for ref, target in zip(outs, targets):
                ref[j, start : start + size, :] = scratch[target, :].astype(BF)
                if slot > size:
                    ref[j, start + size : start + slot, :] = jnp.zeros((slot - size, scratch.shape[1]), BF)
        start += slot


def slot_of(size):
    return (size + 15) // 16 * 16


def outer(parts, info, pairs, relative):
    arrays, plans = [info], []

    def number(a):
        for n, other in enumerate(arrays):
            if other is a:
                return n
        arrays.append(a)
        return len(arrays) - 1

    for segments, span in pairs:
        rows = segments[0][0].shape[1]
        numbers = [(number(a), first, number(b), second, count) for a, first, b, second, count in segments]
        plans.append((numbers, rows, slot_of(rows // parts), span, segments[0][2].shape[1]))
    cols = max(p[4] for p in plans)
    tall = sum(p[2] for p in plans)
    outs = [((parts // 2, tall, cols), BF)] * 2 if relative else [((parts, tall, cols), BF)]
    return call(
        functools.partial(outer_kernel, parts, plans, relative),
        outs,
        arrays,
        [pltpu.VMEM((max(p[1] for p in plans), cols), F32)],
        flops=sum(2 * p[1] * cols * sum(seg[4] for seg in p[0]) for p in plans),
        name="outer",
    )


def tick(*items):
    flat = [a for item in items for a in (item.pending() if hasattr(item, "pending") else [item])]
    flat = list(lax.optimization_barrier(tuple(flat)))
    found = []
    for item in items:
        if hasattr(item, "pending"):
            count = len(item.pending())
            item.resume(flat[:count])
            del flat[:count]
        else:
            found.append(flat.pop(0))
    return found


def swap(x, axis, bit):
    size = lax.axis_size(axis)
    return lax.ppermute(x, axis, [(i, i ^ bit) for i in range(size)])


def row_moves(pb, ka):
    span = pb // ka
    return [(p * ka + k, (k * span + p % span) * ka + p // span) for p in range(pb) for k in range(ka)]


def gather_rows(x):
    return lax.all_gather(x, "pb", axis=0, tiled=True)


def whole_rows(x, parts, start, size, span=0):
    piece = x.shape[0] // parts
    return Rows([x], [(0, p * piece + start, p, False) for p in range(parts)], size, span)


class Spread:
    def __init__(self, x, direct=False):
        self.rows_each, self.parts = x.shape[0], lax.axis_size("pb")
        self.bits = [1] if direct else [2, 1]
        if self.parts != 8:
            self.kept, self.got = x, [gather_rows(x)]
        elif direct:
            self.kept, self.got = x, [swap(x, "pb", s) for s in SHIFTS[1:]]
        else:
            self.kept, self.got = x, [swap(x, "pb", 4)]

    def pending(self):
        return [self.kept, *self.got]

    def resume(self, arrays):
        self.kept, *self.got = arrays

    def step(self):
        if self.parts != 8:
            return
        self.kept = jnp.concatenate([self.kept, *self.got], axis=0)
        self.got = [swap(self.kept, "pb", self.bits.pop(0))]

    def rows(self, first=0, size=None, span=0):
        size = size or self.rows_each
        if self.parts != 8:
            return whole_rows(self.got[0], self.parts, first, size, span)
        each = self.rows_each
        plan = [(n, i * each + first, s + n, True) for n in range(2) for i, s in enumerate(SHIFTS)]
        return Rows(self.pending(), plan, size, span)


class Flow:
    def __init__(self, info, pairs):
        self.parts = lax.axis_size("pb")
        if self.parts != 8:
            (x,) = outer(self.parts, info, pairs, False)
            self.kept = lax.psum_scatter(x.reshape(-1, x.shape[2]), "pb", scatter_dimension=0, tiled=True)
            self.got = self.kept
            self.made = x
        else:
            self.got, self.kept = outer(self.parts, info, pairs, True)
            self.made = self.kept
            self.bits = [1, 2, 4]

    def pending(self):
        return [self.kept, self.got]

    def resume(self, arrays):
        self.kept, self.got = arrays

    def start(self):
        if self.parts == 8:
            self.got = swap(self.got, "pb", self.bits.pop(0))
        return self

    def step(self):
        if self.parts == 8:
            near = (self.kept.astype(F32) + self.got.astype(F32)).astype(BF)
            count = near.shape[0] // 2
            self.kept, self.got = near[:count], near[count:]
            self.start()

    def end(self):
        if self.parts != 8:
            return self.kept
        return (self.kept[0].astype(F32) + self.got[0].astype(F32)).astype(BF)


def pair_gather(x):
    groups = [[i, i + 1] for i in range(0, lax.axis_size("ka"), 2)]
    return lax.all_gather(x, "ka", axis_index_groups=groups)


def join_ka(x, far):
    high = lax.axis_index("ka") // 2
    pairs = pair_gather(jnp.where(high == 0, jnp.stack([x, far]), jnp.stack([far, x])))
    return [pairs[0, 0], pairs[1, 0], pairs[0, 1], pairs[1, 1]]


def on_device(tokens, cotangent, lengths, keep_mask, w_qkv, w_out, w_fc, w_proj, norm_gain, norm_bias):
    rows, width = tokens.shape
    pb = lax.axis_size("pb")
    ka = lax.axis_size("ka")
    span = pb // ka
    me = lax.axis_index("ka")
    low, high = me % 2, me // 2
    heads = H // ka
    part = width // ka
    ff = w_fc.shape[2]
    ff_part = ff // ka
    d_rows = w_qkv.shape[0]
    out_rows = w_out.shape[0] // ka
    proj_rows = w_proj.shape[0] // ka
    wide = (3 * part + 8 + 127) // 128 * 128
    moves = row_moves(pb, ka)
    bounds = jnp.cumsum(lengths[0])
    info = jnp.concatenate([jnp.stack([lax.axis_index("pb"), low]).astype(jnp.int32), bounds.astype(jnp.int32)])

    half, group, slot = 2 * rows, 4 * rows, slot_of(out_rows)

    def own_half(x, far):
        return jnp.where(high == 0, jnp.concatenate([x, far], axis=0), jnp.concatenate([far, x], axis=0))

    def filled(x):
        return jnp.pad(x, ((0, slot - out_rows), (0, 0)))

    def block(half, which):
        return lax.dynamic_slice_in_dim(half, which * rows, rows, 0)

    def from_pair(sent):
        return lax.dynamic_index_in_dim(pair_gather(sent), 1 - low, 0, False)

    def add_low(kept, got):
        return (kept + got.astype(F32)).astype(BF)

    local_out = lax.dynamic_slice_in_dim(w_out, me * out_rows, out_rows, 0)
    tall = jnp.concatenate([filled(local_out[:, 0]), filled(local_out[:, 1])], axis=0)
    tall, w_qkv, norm_gain, norm_bias = tick(tall, w_qkv, norm_gain, norm_bias)
    tall = lax.ppermute(tall, ("pb", "ka"), moves)
    tokens_own = own_half(tokens, swap(tokens, "ka", 2))
    picked = jnp.concatenate([lax.dynamic_slice_in_dim(w_qkv, i * width + me * part, part, 2) for i in range(3)], axis=2)
    vectors = jnp.concatenate([norm_gain, norm_bias], axis=1)
    first = jnp.concatenate([picked[:, 0], vectors, jnp.zeros((d_rows, wide - 3 * part - 8), BF)], axis=1)
    qkv0 = Spread(first, True)
    first, tokens_own, keep_mask = tick(first, tokens_own, keep_mask)
    tokens_both = pair_gather(tokens_own)
    kept_all = lax.all_gather(keep_mask, "ka", axis=0, tiled=True).reshape(1, -1)
    out0 = Spread(tall[:slot])
    out1, tokens_both, kept_all, w_fc, w_proj, picked, cotangent = tick(
        tall[slot:], qkv0, out0, tokens_both, kept_all, w_fc, w_proj, picked, cotangent
    )
    unit = ff_part // pb
    local_fc = jnp.concatenate(
        [lax.dynamic_slice_in_dim(w_fc, (q * ka + me) * unit, unit, 2) for q in range(pb)], axis=2
    )
    fc_first, fc_second = local_fc[:, 0], local_fc[:, 1]
    local_proj = lax.dynamic_slice_in_dim(w_proj, me * proj_rows, proj_rows, 0)
    proj_late = local_proj[:, 1]
    second = jnp.concatenate([picked[:, 1], jnp.zeros((d_rows, wide - 3 * part), BF)], axis=1)
    qkv0.step()
    out0.step()
    tall1 = Spread(jnp.concatenate([local_proj[:, 0], jnp.zeros((slot_of(proj_rows) - proj_rows, width), BF), out1], axis=0))
    fc0_all = gather_rows(fc_first)
    fc_second, second, cotangent, proj_late = tick(out0, tall1, fc_second, second, cotangent, proj_late)
    out0.step()
    tall1.step()
    qkv1 = Spread(second)
    far_cotangent = swap(cotangent, "ka", 2)
    tokens_both, far_cotangent, fc_second, proj_late = tick(qkv0, qkv1, tokens_both, far_cotangent, fc_second, proj_late)
    qkv1.step()
    qkv = [qkv0.rows(), None]

    keys = ("stream", "x", "projected", "attended", "lse", "middle", "both", "hidden", "active")
    x_all, projected, attended, lse, tokens_all, vec = attention_forward(True, True, info, kept_all, tokens_both, qkv[0], part, heads)
    attended, proj_late = tick(attended, out0, tall1, proj_late)
    tall1.step()
    proj1_all = gather_rows(proj_late)
    out = [out0.rows(0, out_rows, span), tall1.rows(slot_of(proj_rows), out_rows, span)]
    sent, kept = attention_out(info, attended, out[0])
    got, fc_second, far_cotangent = tick(from_pair(sent), qkv1, fc_second, far_cotangent)
    near = add_low(kept, got)
    far = swap(near, "ka", 2)
    qkv1.step()
    fc1 = Spread(fc_second)
    branch = own_half(cotangent, far_cotangent)
    middle, own = norm_after(1, tokens_own, near, far, vec)
    both = pair_gather(own)
    fc = [whole_rows(fc0_all, pb, 0, d_rows), None]
    proj = [tall1.rows(0, proj_rows), whole_rows(proj1_all, pb, 0, proj_rows)]
    hidden, active, sent, kept = feed_forward(info, both, fc[0], proj[0])
    kept0 = dict(zip(keys, (tokens_own, x_all, projected, attended, lse, middle, both, hidden, active)))
    got, branch_own = tick(from_pair(sent), qkv1, fc1, branch)
    near = add_low(kept, got)
    far = swap(near, "ka", 2)
    fc1.step()
    branch = pair_gather(branch_own)
    qkv[1] = qkv1.rows()
    far, branch = tick(far, branch)
    stream, own = norm_after(2, middle, near, far, vec)
    both = pair_gather(own)
    x_all, projected, attended, lse = attention_forward(False, False, info, kept_all, both, qkv[1], part, heads)
    sent, kept = attention_out(info, attended, out[1])
    (got,) = tick(from_pair(sent), fc1)
    near = add_low(kept, got)
    far = swap(near, "ka", 2)
    fc1.step()
    fc[1] = fc1.rows()
    middle, own = norm_after(3, stream, near, far, vec)
    both = pair_gather(own)
    hidden, active, last_sent, last_kept = feed_forward(info, both, fc[1], proj[1])
    kept1 = dict(zip(keys, (stream, x_all, projected, attended, lse, middle, both, hidden, active)))

    sums = [None] * 4

    def fc_pair(kept, grad_hidden):
        return [(kept["both"].reshape(group, width), 0, grad_hidden, 0, group)], 0

    def proj_pair(kept, branch):
        return [(kept["active"], 0, branch.reshape(group, width), 0, group)], 0

    def attend_pairs(kept, grad_projected, middle_all, more=()):
        yield [(kept["x"], 0, grad_projected, 0, group), *more], 0
        yield [(kept["attended"], 0, middle_all, 0, group)], span

    def attend_back(l, kept, both):
        return attention_backward(
            l == 0, l == 0, info, kept_all, both, kept["projected"], kept["lse"], qkv[l], out[l], tokens_all, heads
        )

    grad_hidden, sent, kept = feed_backward(info, branch, kept1["hidden"], fc[1], proj[1])
    near = add_low(kept, from_pair(sent))
    far = swap(near, "ka", 2)
    near_in, grad_hidden, last_sent, last_kept = tick(near, grad_hidden, last_sent, last_kept)
    last = add_low(last_kept, from_pair(last_sent))
    flow_a = Flow(info, [fc_pair(kept1, grad_hidden), proj_pair(kept1, branch)]).start()
    far, last, unused = tick(far, last, flow_a.made)
    grad, own, sums[3] = norm_back(3, branch_own, near, far, kept1["middle"], vec)
    both = pair_gather(own)
    middle_all, grad_projected, sent, kept = attend_back(1, kept1, both)
    (got,) = tick(from_pair(sent), flow_a)
    near = add_low(kept, got)
    far = swap(near, "ka", 2)
    near_in, grad_projected, middle_all = tick(near, grad_projected, middle_all)
    flow_b = Flow(info, attend_pairs(kept1, grad_projected, middle_all)).start()
    flow_a.step()
    far, unused = tick(far, flow_b.made)
    grad, own, sums[2] = norm_back(2, grad, near, far, kept1["stream"], vec)
    branch = pair_gather(own)
    grad_hidden, sent, kept = feed_backward(info, branch, kept0["hidden"], fc[0], proj[0])
    (got,) = tick(from_pair(sent), flow_a, flow_b)
    near = add_low(kept, got)
    far = swap(near, "ka", 2)
    near_in, grad_hidden = tick(near, grad_hidden)
    flow_c = Flow(info, [fc_pair(kept0, grad_hidden), proj_pair(kept0, branch)]).start()
    flow_a.step()
    flow_b.step()
    far, unused = tick(far, flow_c.made)
    grad, own, sums[1] = norm_back(1, grad, near, far, kept0["middle"], vec)
    both = pair_gather(own)
    middle_all, grad_projected, sent, kept, sums[0] = attend_back(0, kept0, both)
    (got,) = tick(from_pair(sent), flow_a, flow_b, flow_c)
    near = add_low(kept, got)
    far = swap(block(near, 1 - high), "ka", 2)
    near_in, grad_projected, middle_all, last = tick(near, grad_projected, middle_all, last)
    halved = [sums[0]] + [0.5 * s for s in sums[1:]]
    stacked = jnp.concatenate([s[i : i + 1] for i in range(2) for s in halved] + [jnp.zeros((8, width), F32)], axis=0).astype(BF)
    spots = (3 * part + jnp.arange(16)[:, None] == jnp.arange(wide)[None, :]) & (jnp.arange(16)[:, None] < 8)
    flow_d = Flow(info, attend_pairs(kept0, grad_projected, middle_all, [(stacked, 0, spots.astype(BF), 0, 16)])).start()
    flow_b.step()
    flow_c.step()
    after_fc = slot_of(d_rows)
    back = [(b, a) for a, b in moves]

    def go_back(x):
        return lax.ppermute(x[after_fc:], ("pb", "ka"), back)

    done_a = flow_a.end()
    last_far = swap(block(last, 1 - high), "ka", 2)
    far, unused = tick(far, flow_d.made)
    (grad_tokens,) = norm_back(0, block(grad, high), block(near, high), far, block(kept0["stream"], high), vec, True)

    done_a, last_far, grad_tokens = tick(flow_b, flow_c, flow_d, done_a, last_far, grad_tokens)
    flow_d.step()
    flow_c.step()
    done_b = flow_b.end()
    back_b = go_back(done_b)
    far_a = swap(done_a, "ka", 2)
    output = (block(kept1["middle"], high) + (block(last, high).astype(F32) + last_far.astype(F32))).astype(BF)
    done_b, back_b, far_a, output = tick(flow_d, flow_c, done_b, back_b, far_a, output)
    flow_d.step()
    done_c = flow_c.end()
    done_b = jnp.concatenate([done_b[:after_fc], back_b], axis=0)
    far_b = swap(done_b, "ka", 2)
    far_c = swap(done_c, "ka", 2)
    pieces_a = join_ka(done_a, far_a)
    far_b, far_c = tick(flow_d, far_b, far_c)
    done_d = flow_d.end()
    far_d = swap(done_d[:after_fc], "ka", 2)
    back_d = go_back(done_d)
    pieces_b = join_ka(done_b, far_b)
    pieces_c = join_ka(done_c, far_c)
    back_d, far_d = tick(back_d, far_d)
    far_o = swap(back_d, "ka", 2)
    pieces_d = join_ka(done_d[:after_fc], far_d)
    pieces_o = join_ka(back_d, far_o)

    def columns(pieces):
        cuts = [p[:d_rows, q * unit : (q + 1) * unit] for q in range(pb) for p in pieces]
        return jnp.concatenate(cuts, axis=1)

    def heads_of(pieces):
        return jnp.concatenate([p[:d_rows, i * part : (i + 1) * part] for i in range(3) for p in pieces], axis=1)

    def rows_of(pieces, start, size):
        return jnp.concatenate([p[start : start + size] for p in pieces], axis=0)

    summed = (
        (heads_of(pieces_d), heads_of(pieces_b)),
        (rows_of(pieces_o, 0, out_rows), rows_of(pieces_b, after_fc, out_rows)),
        (columns(pieces_c), columns(pieces_a)),
        (rows_of(pieces_c, after_fc, proj_rows), rows_of(pieces_a, after_fc, proj_rows)),
    )
    summed = [jnp.stack(pair, axis=1).astype(F32) for pair in summed]
    stacked = sum(p[:d_rows, 3 * part : 3 * part + 8].astype(F32) for p in pieces_d)
    return (output, grad_tokens, *summed, stacked[:, :4], stacked[:, 4:])


def solution(mesh):
    return jax.shard_map(
        on_device,
        mesh=mesh,
        in_specs=(
            P(("pb", "ka"), None),
            P(("pb", "ka"), None),
            P("pb", None),
            P(("pb", "ka")),
            P("pb", None, None),
            P("pb", None, None),
            P("pb", None, None),
            P("pb", None, None),
            P("pb", None),
            P("pb", None),
        ),
        out_specs=(
            P(("pb", "ka"), None),
            P(("pb", "ka"), None),
            P("pb", None, None),
            P("pb", None, None),
            P("pb", None, None),
            P("pb", None, None),
            P("pb", None),
            P("pb", None),
        ),
        check_vma=False,
    )
```

```python
import functools
import jax
import jax.numpy as jnp
from jax import lax
from jax.experimental import pallas as pl
from jax.experimental.pallas import tpu as pltpu
from jax.sharding import PartitionSpec as P

H = 12
EPSILON = 1e-05
FLOOR_VALUE = -1e30
BF = jnp.bfloat16
F32 = jnp.float32
VM = pl.BlockSpec(memory_space=pltpu.VMEM)
SM = pl.BlockSpec(memory_space=pltpu.SMEM)
SHIFTS = (0, 4, 2, 6)
GELU_A = 0.7978845608028654
GELU_B = 0.044715


def dot(a, b, ca, cb):
    return lax.dot_general(a, b, (((ca,), (cb,)), ((), ())), preferred_element_type=F32)


def call(kernel, outs, ins, scratch=(), flops=0, name=None):
    moved = sum(a.size * a.dtype.itemsize for a in ins)
    return pl.pallas_call(
        kernel,
        out_shape=[jax.ShapeDtypeStruct(s, t) for s, t in outs],
        in_specs=[SM if a.dtype == jnp.int32 and a.ndim == 1 else VM for a in ins],
        out_specs=[VM] * len(outs),
        scratch_shapes=list(scratch),
        compiler_params=pltpu.CompilerParams(vmem_limit_bytes=20 * 1024 * 1024),
        cost_estimate=pl.CostEstimate(flops=flops, bytes_accessed=moved, transcendentals=0),
        name=name,
    )(*ins)


def at(index, rows):
    return pl.ds(pl.multiple_of(index * rows, rows), rows)


class Rows:
    def __init__(self, arrays, plan, size, span=0):
        self.arrays, self.plan, self.size, self.span = arrays, plan, size, span
        self.shape = (size * len(plan), arrays[0].shape[1])

    def scratch(self):
        return pltpu.VMEM(self.shape, F32 if self.size % 16 else BF)

    def load(self, refs, scratch, me):
        for index, start, p, relative in self.plan:
            place = me ^ p if relative else p
            if self.span < 0:
                place = place & (len(self.plan) - 1)
            elif self.span:
                place = place_of(place, self.span, len(self.plan) // self.span)
            target = at(place, self.size) if relative else slice(place * self.size, (place + 1) * self.size)
            scratch[target, :] = refs[index][start : start + self.size, :].astype(scratch.dtype)


def place_of(p, span, ka):
    return (p % span) * ka + p // span if isinstance(p, int) else lax.rem(p, span) * ka + lax.div(p, span)


def take_refs(refs, *weights):
    return [[refs.pop(0) for unused in w.arrays] for w in weights]


def norm_parts(values):
    average = jnp.mean(values, axis=-1, keepdims=True)
    centered = values - average
    spread = jnp.mean(centered * centered, axis=-1, keepdims=True)
    inverse = lax.rsqrt(spread + EPSILON)
    return centered * inverse, inverse


def block_allowed(info, kept_ref, b, block, keys):
    i = b * block + lax.broadcasted_iota(jnp.int32, (block, 1), 0)
    j = lax.broadcasted_iota(jnp.int32, (1, keys), 1)

    def segment(t):
        total = jnp.zeros_like(t)
        for n in range(2, info.shape[0]):
            total = total + jnp.where(t >= info[n], 1, 0)
        return total

    same = segment(i) == segment(j)
    itself = i == j
    return same & (j <= i) & ((kept_ref[:, :keys] > 0) | itself)


def canonical(both, full):
    block, stride = full.shape[0] // 4, both.shape[1] // 2
    for h in range(2):
        for i in range(2):
            full[(2 * i + h) * block : (2 * i + h + 1) * block, :] = both[h, i * stride : i * stride + block, :]


def split_halves(low, full, kept, sent):
    block = kept.shape[0] // 2
    for i in range(2):
        kept[i * block : (i + 1) * block, :] = full[at(2 * i + low, block), :].astype(kept.dtype)
        sent[i * block : (i + 1) * block, :] = full[at(2 * i + 1 - low, block), :].astype(sent.dtype)


def attention_forward_kernel(first, signed, qkv, heads, *refs):
    refs = list(refs)
    info = refs.pop(0)
    if not first:
        kept_ref = refs.pop(0)
    both = refs.pop(0)
    (pieces,) = take_refs(refs, qkv)
    x_ref, proj_ref, att_ref, lse_ref = [refs.pop(0) for unused in range(4)]
    if first:
        tokens, vec_ref, kept_ref = refs.pop(0), refs.pop(0), refs.pop(0)
    (w,) = refs
    me, low = info[0], info[1]
    qkv.load(pieces, w, me)
    part = att_ref.shape[1]
    hd = part // heads
    group, width = x_ref.shape
    block = group // 4
    if first:
        tail = w.shape[1] - 3 * part
        pick = lax.broadcasted_iota(jnp.int32, (8, tail), 0) == lax.broadcasted_iota(jnp.int32, (8, tail), 1)
        vec = dot(pick.astype(F32).astype(BF), w[:, 3 * part :], 1, 1)
        vec_ref[...] = vec
        canonical(both, tokens)
        stride = both.shape[1] // 2
        for h in range(2):
            for i in range(2):
                row = both[h, i * stride + block : i * stride + block + 1, :block]
                kept_ref[:, (2 * i + h) * block : (2 * i + h + 1) * block] = row.astype(F32)
        for b in range(4):
            values = tokens[b * block : (b + 1) * block, :].astype(F32)
            normal, unused = norm_parts(values)
            x_ref[b * block : (b + 1) * block, :] = (normal * vec[0:1] + vec[4:5]).astype(BF)
    else:
        canonical(both, x_ref)
    proj_ref[...] = dot(x_ref[...], w[...], 1, 0).astype(BF)
    scale = hd ** (-0.5)
    for b in range(4):
        keys = (b + 1) * block
        rows = slice(b * block, keys)
        allowed = block_allowed(info, kept_ref, b, block, keys)
        for h in range(heads):
            q = proj_ref[rows, h * hd : (h + 1) * hd] * scale
            k = proj_ref[:keys, part + h * hd : part + (h + 1) * hd]
            v = proj_ref[:keys, 2 * part + h * hd : 2 * part + (h + 1) * hd]
            scores = dot(q, k, 1, 1)
            magnitude = jnp.abs(scores) if signed else scores
            masked = jnp.where(allowed, magnitude, FLOOR_VALUE)
            peak = jnp.max(masked, axis=-1, keepdims=True)
            raised = jnp.exp(masked - peak)
            total = jnp.sum(raised, axis=-1, keepdims=True)
            if signed:
                lifted = jnp.where(allowed, raised - jnp.exp(-peak), 0.0)
                raised = jnp.where(scores < 0, -lifted, lifted)
            weights = (raised * (1.0 / total)).astype(BF)
            att_ref[rows, h * hd : (h + 1) * hd] = dot(weights, v, 1, 0).astype(BF)
            lse_ref[rows, h : h + 1] = peak + jnp.log(total)


def attention_forward(first, signed, info, group, kept, both, qkv, part, heads):
    width = both.shape[2]
    outs = [((group, width), BF), ((group, qkv.shape[1]), BF), ((group, part), BF), ((group, 128), F32)]
    if first:
        outs += [((group, width), BF), ((8, width), F32), ((1, group), F32)]
    return call(
        functools.partial(attention_forward_kernel, first, signed, qkv, heads),
        outs,
        [info] + ([] if first else [kept]) + [both, *qkv.arrays],
        [qkv.scratch()],
        flops=2 * group * width * 3 * part,
        name="attend",
    )


def attention_out_kernel(out, *refs):
    refs = list(refs)
    info, attended = refs.pop(0), refs.pop(0)
    (pieces,) = take_refs(refs, out)
    sent, kept, w_out, partial = refs
    out.load(pieces, w_out, info[0])
    partial[...] = dot(attended[...], w_out[...].astype(BF), 1, 0)
    split_halves(info[1], partial, kept, sent)


def attention_out(info, attended, out):
    group, width = attended.shape[0], out.shape[1]
    return call(
        functools.partial(attention_out_kernel, out),
        [((group // 2, width), BF), ((group // 2, width), F32)],
        [info, attended, *out.arrays],
        [out.scratch(), pltpu.VMEM((group, width), F32)],
        flops=2 * group * width * out.shape[0],
        name="attend_out",
    )


def gelu_parts(v):
    inner = GELU_A * (v + GELU_B * v * v * v)
    return jnp.tanh(inner)


def feed_forward_kernel(fc, proj, *refs):
    refs = list(refs)
    info, both = [refs.pop(0) for unused in range(2)]
    fc_refs, proj_refs = take_refs(refs, fc, proj)
    hidden, active, sent, kept, w, w_proj, partial = refs
    fc.load(fc_refs, w, info[0])
    proj.load(proj_refs, w_proj, info[0])
    half = both.shape[1]
    ff = w_proj.shape[0]
    step = ff // 3
    for h in range(2):
        rows = slice(h * half, (h + 1) * half)
        total = None
        for f in range(3):
            cols = slice(f * step, (f + 1) * step)
            hid = dot(both[h], w[:, cols], 1, 0)
            hidden[rows, cols] = hid
            act = (0.5 * hid * (1.0 + gelu_parts(hid))).astype(BF)
            active[rows, cols] = act
            term = dot(act, w_proj[cols, :], 1, 0)
            total = term if total is None else total + term
        partial[h] = total
    kept[...] = partial[info[1]]
    sent[...] = partial[1 - info[1]].astype(BF)


def feed_forward(info, both, fc, proj):
    two, half, width = both.shape
    ff = proj.shape[0]
    outs = [((2 * half, ff), F32), ((2 * half, ff), BF), ((half, width), BF), ((half, width), F32)]
    return call(
        functools.partial(feed_forward_kernel, fc, proj),
        outs,
        [info, both, *fc.arrays, *proj.arrays],
        [fc.scratch(), proj.scratch(), pltpu.VMEM((2, half, width), F32)],
        flops=8 * half * width * ff,
        name="feed",
    )


def norm_kernel(row, stream, near, far, vec, middle, normed):
    values = stream[...].astype(F32) + (near[...].astype(F32) + far[...].astype(F32))
    middle[...] = values
    normal, unused = norm_parts(values)
    normed[...] = (normal * vec[row : row + 1, :] + vec[row + 4 : row + 5, :]).astype(BF)


def norm_after(row, stream, near, far, vec):
    shape = stream.shape
    return call(functools.partial(norm_kernel, row), [(shape, F32), (shape, BF)], [stream, near, far, vec], name="norm")


def feed_backward_kernel(fc, proj, *refs):
    refs = list(refs)
    info, both, hidden = [refs.pop(0) for unused in range(3)]
    fc_refs, proj_refs = take_refs(refs, fc, proj)
    grad_hidden, sent, kept, w, w_proj, partial = refs
    fc.load(fc_refs, w, info[0])
    proj.load(proj_refs, w_proj, info[0])
    half = both.shape[1]
    ff = w_proj.shape[0]
    step = ff // 3
    for h in range(2):
        rows = slice(h * half, (h + 1) * half)
        total = None
        for f in range(3):
            cols = slice(f * step, (f + 1) * step)
            grad_active = dot(both[h], w_proj[cols, :], 1, 1)
            v = hidden[rows, cols]
            t = gelu_parts(v)
            slope = 0.5 * (1.0 + t) + 0.5 * v * (1.0 - t * t) * (GELU_A * (1.0 + 3.0 * GELU_B * v * v))
            gh = (slope * grad_active).astype(BF)
            grad_hidden[rows, cols] = gh
            term = dot(gh, w[:, cols], 1, 1)
            total = term if total is None else total + term
        partial[h] = total
    kept[...] = partial[info[1]]
    sent[...] = partial[1 - info[1]].astype(BF)


def feed_backward(info, both, hidden, fc, proj):
    two, half, width = both.shape
    ff = proj.shape[0]
    outs = [((2 * half, ff), BF), ((half, width), BF), ((half, width), F32)]
    return call(
        functools.partial(feed_backward_kernel, fc, proj),
        outs,
        [info, both, hidden, *fc.arrays, *proj.arrays],
        [fc.scratch(), proj.scratch(), pltpu.VMEM((2, half, width), F32)],
        flops=8 * half * width * ff,
        name="feed_back",
    )


def norm_backward_kernel(row, grad, near, far, source, vec, out, *rest):
    incoming = near[...].astype(F32) + far[...].astype(F32)
    normal, inverse = norm_parts(source[...].astype(F32))
    grad_normal = incoming * vec[row : row + 1, :]
    mean_grad = jnp.mean(grad_normal, axis=-1, keepdims=True)
    mean_cross = jnp.mean(grad_normal * normal, axis=-1, keepdims=True)
    value = grad[...].astype(F32) + inverse * (grad_normal - mean_grad - normal * mean_cross)
    out[...] = value
    if not rest:
        return
    low, sums = rest
    low[...] = value.astype(BF)
    sums[0:1, :] = jnp.sum(incoming * normal, axis=0, keepdims=True)
    sums[1:2, :] = jnp.sum(incoming, axis=0, keepdims=True)


def norm_back(row, grad, near, far, source, vec, last=False):
    shape = source.shape
    return call(
        functools.partial(norm_backward_kernel, row),
        [(shape, F32)] if last else [(shape, F32), (shape, BF), ((2, shape[1]), F32)],
        [grad, near, far, source, vec],
        name="norm_back",
    )


def attention_backward_kernel(first, signed, qkv, out, heads, *refs):
    refs = list(refs)
    info, kept_ref, both, proj, lse = [refs.pop(0) for unused in range(5)]
    pieces, out_pieces = take_refs(refs, qkv, out)
    if first:
        tokens = refs.pop(0)
    gm_ref, gp_ref, sent, kept = [refs.pop(0) for unused in range(4)]
    if first:
        sums = refs.pop(0)
    w, w_out, partial, gatt, gk_sum, gv_sum = refs
    me, low = info[0], info[1]
    qkv.load(pieces, w, me)
    out.load(out_pieces, w_out, me)
    part = w_out.shape[0]
    hd = part // heads
    group = gm_ref.shape[0]
    block = group // 4
    canonical(both, gm_ref)
    gatt[...] = dot(gm_ref[...], w_out[...].astype(BF), 1, 1).astype(BF)
    scale = hd ** (-0.5)
    gp_ref[:, 3 * part :] = jnp.zeros((group, gp_ref.shape[1] - 3 * part), BF)
    for b in reversed(range(4)):
        keys = (b + 1) * block
        rows = slice(b * block, keys)
        allowed = block_allowed(info, kept_ref, b, block, keys)
        for h in range(heads):
            cols = slice(h * hd, (h + 1) * hd)
            q = proj[rows, h * hd : (h + 1) * hd] * scale
            k = proj[:keys, part + h * hd : part + (h + 1) * hd]
            v = proj[:keys, 2 * part + h * hd : 2 * part + (h + 1) * hd]
            g = gatt[rows, h * hd : (h + 1) * hd]
            level = lse[rows, h : h + 1]
            scores = dot(q, k, 1, 1)
            magnitude = jnp.abs(scores) if signed else scores
            absolute = jnp.exp(jnp.where(allowed, magnitude, FLOOR_VALUE) - level)
            grad_weights = dot(g, v, 1, 1)
            if signed:
                lifted = jnp.where(allowed, absolute - jnp.exp(-level), 0.0)
                weights = jnp.where(scores < 0, -lifted, lifted)
                delta = jnp.sum(grad_weights * weights, axis=-1, keepdims=True)
                shift = jnp.where(scores > 0, delta, jnp.where(scores < 0, -delta, 0.0))
            else:
                weights = absolute
                shift = jnp.sum(grad_weights * weights, axis=-1, keepdims=True)
            gs = (absolute * (grad_weights - shift)).astype(BF)
            gp_ref[rows, h * hd : (h + 1) * hd] = (dot(gs, k, 1, 0) * scale).astype(BF)
            gk = dot(gs, q, 0, 0)
            gv = dot(weights.astype(BF), g, 0, 0)
            if b == 3:
                gk_sum[h] = gk
                gv_sum[h] = gv
            else:
                gk_sum[h, :keys] += gk
                gv_sum[h, :keys] += gv
    for h in range(heads):
        gp_ref[:, part + h * hd : part + (h + 1) * hd] = gk_sum[h].astype(BF)
        gp_ref[:, 2 * part + h * hd : 2 * part + (h + 1) * hd] = gv_sum[h].astype(BF)
    partial[...] = dot(gp_ref[...], w[...], 1, 1)
    split_halves(low, partial, kept, sent)
    if first:
        gain = bias = 0.0
        for b in range(4):
            rows = slice(b * block, (b + 1) * block)
            normal, unused = norm_parts(tokens[rows, :].astype(F32))
            value = partial[rows, :]
            gain = gain + jnp.sum(value * normal, axis=0, keepdims=True)
            bias = bias + jnp.sum(value, axis=0, keepdims=True)
        sums[0:1, :] = gain
        sums[1:2, :] = bias


def attention_backward(first, signed, info, kept, both, proj, lse, qkv, out, tokens, heads):
    two, half, width = both.shape
    group = 2 * half
    part = out.shape[0]
    wide = qkv.shape[1]
    outs = [((group, width), BF), ((group, wide), BF), ((half, width), BF), ((half, width), F32)]
    if first:
        outs += [((2, width), F32)]
    return call(
        functools.partial(attention_backward_kernel, first, signed, qkv, out, heads),
        outs,
        [info, kept, both, proj, lse, *qkv.arrays, *out.arrays] + ([tokens] if first else []),
        [
            qkv.scratch(),
            out.scratch(),
            pltpu.VMEM((group, width), F32),
            pltpu.VMEM((group, part), BF),
            pltpu.VMEM((heads, group, part // heads), F32),
            pltpu.VMEM((heads, group, part // heads), F32),
        ],
        flops=2 * group * width * 4 * part,
        name="attend_back",
    )


def outer_kernel(parts, plans, relative, *refs):
    info, scratch = refs[0], refs[-1]
    outs = refs[-3:-1] if relative else refs[-2:-1]
    start = 0
    for segments, rows, slot, span, cols in plans:
        size = rows // parts
        blank = scratch.shape[1] - cols

        def place(p):
            return place_of(p, span, parts // span) if span else p

        total = None
        for left, first, right, second, count in segments:
            term = dot(refs[left][first : first + count, :], refs[right][second : second + count, :], 0, 0)
            total = term if total is None else total + term
        scratch[:rows, :cols] = total
        if blank:
            scratch[:rows, cols:] = jnp.zeros((rows, blank), F32)
        for j in range(len(SHIFTS) if relative else parts):
            if relative:
                targets = [at(place(info[0] ^ (SHIFTS[j] + 1)), size), at(place(info[0] ^ SHIFTS[j]), size)]
            else:
                targets = [slice(place(j) * size, (place(j) + 1) * size)]
            for ref, target in zip(outs, targets):
                ref[j, start : start + size, :] = scratch[target, :].astype(BF)
                if slot > size:
                    ref[j, start + size : start + slot, :] = jnp.zeros((slot - size, scratch.shape[1]), BF)
        start += slot


def slot_of(size):
    return (size + 15) // 16 * 16


def outer(parts, info, pairs, relative):
    arrays, plans = [info], []

    def number(a):
        for n, other in enumerate(arrays):
            if other is a:
                return n
        arrays.append(a)
        return len(arrays) - 1

    for segments, span in pairs:
        rows = segments[0][0].shape[1]
        numbers = [(number(a), first, number(b), second, count) for a, first, b, second, count in segments]
        plans.append((numbers, rows, slot_of(rows // parts), span, segments[0][2].shape[1]))
    cols = max(p[4] for p in plans)
    tall = sum(p[2] for p in plans)
    outs = [((parts // 2, tall, cols), BF)] * 2 if relative else [((parts, tall, cols), BF)]
    return call(
        functools.partial(outer_kernel, parts, plans, relative),
        outs,
        arrays,
        [pltpu.VMEM((max(p[1] for p in plans), cols), F32)],
        flops=sum(2 * p[1] * cols * sum(seg[4] for seg in p[0]) for p in plans),
        name="outer",
    )


def outer_pair_kernel(count, *refs):
    info, ins, (sent, kept, scratch) = refs[0], refs[1 : 1 + 2 * count], refs[1 + 2 * count :]
    size = scratch.shape[0] // 2
    low = info[0] & 1
    for i in range(count):
        scratch[...] = dot(ins[2 * i][...], ins[2 * i + 1][...], 0, 0)
        kept[i * size : (i + 1) * size, :] = scratch[at(low, size), :].astype(BF)
        sent[i * size : (i + 1) * size, :] = scratch[at(1 - low, size), :].astype(BF)


def outer_pair(info, pairs):
    rows, cols = pairs[0][0].shape[1], pairs[0][1].shape[1]
    shape = (len(pairs) * rows // 2, cols)
    return call(
        functools.partial(outer_pair_kernel, len(pairs)),
        [(shape, BF)] * 2,
        [info] + [a for pair in pairs for a in pair],
        [pltpu.VMEM((rows, cols), F32)],
        flops=len(pairs) * 2 * rows * cols * pairs[0][0].shape[0],
        name="outer",
    )


def piece_refs(refs):
    own, far, core = refs[:3]
    return [own, core.at[0], far, core.at[1]]


def finish_feed_kernel(first, unit, info, *refs):
    w_fc, w_proj, scratch = refs[-3:]
    me = info[0]
    size = w_fc.shape[0]
    rows = w_proj.shape[0] // 4
    for l in range(2):
        pieces = piece_refs(refs[3 * l :])
        values = [p[:size, :] for p in pieces]
        for k in range(4):
            value = values[3]
            for n in range(3):
                value = jnp.where((me ^ k) == n, values[n], value)
            for q in range(value.shape[1] // unit):
                scratch[:, (q * 4 + k) * unit : (q * 4 + k + 1) * unit] = value[:, q * unit : (q + 1) * unit]
        w_fc[:, l, :] = scratch[...].astype(F32)
        for n in range(4):
            w_proj[at(me ^ n, rows), l, :] = pieces[n][first : first + rows, :].astype(F32)


def finish_feed(me, blocks, first, unit, size, rows):
    width = blocks[0][0].shape[1]
    ff = 4 * width
    return call(
        functools.partial(finish_feed_kernel, first, unit),
        [((size, 2, ff), F32), ((4 * rows, 2, width), F32)],
        [me] + [a for block in blocks for a in block],
        [pltpu.VMEM((size, ff), BF)],
        name="finish_feed",
    )


def finish_attend_kernel(part, info, *refs):
    (near, far), (w_qkv, w_out, vectors, scratch) = refs[6:8], refs[8:]
    me = info[0]
    size = w_qkv.shape[0]
    for l in range(2):
        pieces = piece_refs(refs[3 * l :])
        values = [p[...] for p in pieces]
        for k in range(4):
            value = values[3]
            for n in range(3):
                value = jnp.where((me ^ k) == n, values[n], value)
            for i in range(3):
                scratch[:, (i * 4 + k) * part : (i * 4 + k + 1) * part] = value[:, i * part : (i + 1) * part]
        w_qkv[:, l, :] = scratch[...].astype(F32)
        rows = slice(l * size, (l + 1) * size)
        w_out[:, l, :] = near[rows, :].astype(F32) + far[rows, :].astype(F32)
        if l == 0:
            tail = values[0].shape[1] - 3 * part
            pick = lax.broadcasted_iota(jnp.int32, (8, tail), 0) == lax.broadcasted_iota(jnp.int32, (8, tail), 1)
            pick = pick.astype(F32).astype(BF)
            total = None
            for value in values:
                term = dot(pick, value[:, 3 * part :], 1, 1)
                total = term if total is None else total + term
            vectors[...] = total


def finish_attend(me, blocks, out_near, out_far, part):
    size, width = blocks[0][0].shape[0], out_near.shape[1]
    return call(
        functools.partial(finish_attend_kernel, part),
        [((size, 2, 3 * width), F32), ((size, 2, width), F32), ((8, size), F32)],
        [me] + [a for block in blocks for a in block] + [out_near, out_far],
        [pltpu.VMEM((size, 3 * width), BF)],
        name="finish_attend",
    )


def tick(*items):
    flat = [a for item in items for a in (item.pending() if hasattr(item, "pending") else [item])]
    flat = list(lax.optimization_barrier(tuple(flat)))
    found = []
    for item in items:
        if hasattr(item, "pending"):
            count = len(item.pending())
            item.resume(flat[:count])
            del flat[:count]
        else:
            found.append(flat.pop(0))
    return found


def swap(x, axis, bit):
    size = lax.axis_size(axis)
    return lax.ppermute(x, axis, [(i, i ^ bit) for i in range(size)])


def row_moves(pb, ka):
    span = pb // ka
    return [(p * ka + k, (k * span + p % span) * ka + p // span) for p in range(pb) for k in range(ka)]


def gather_rows(x):
    return lax.all_gather(x, "pb", axis=0, tiled=True)


def whole_rows(x, parts, start, size, span=0):
    piece = x.shape[0] // parts
    return Rows([x], [(0, p * piece + start, p, False) for p in range(parts)], size, span)


class Spread:
    def __init__(self, x, direct=False):
        self.rows_each, self.parts = x.shape[0], lax.axis_size("pb")
        self.bits = [1] if direct else [2, 1]
        if self.parts != 8:
            self.kept, self.got = x, [gather_rows(x)]
        elif direct:
            self.kept, self.got = x, [swap(x, "pb", s) for s in SHIFTS[1:]]
        else:
            self.kept, self.got = x, [swap(x, "pb", 4)]

    def pending(self):
        return [self.kept, *self.got]

    def resume(self, arrays):
        self.kept, *self.got = arrays

    def step(self):
        if self.parts != 8:
            return
        self.kept = jnp.concatenate([self.kept, *self.got], axis=0)
        self.got = [swap(self.kept, "pb", self.bits.pop(0))]

    def rows(self, first=0, size=None, span=0):
        size = size or self.rows_each
        if self.parts != 8:
            return whole_rows(self.got[0], self.parts, first, size, span)
        each = self.rows_each
        plan = [(n, i * each + first, s + n, True) for n in range(2) for i, s in enumerate(SHIFTS)]
        return Rows(self.pending(), plan, size, span)


class Flow:
    def __init__(self, info, pairs):
        self.parts = lax.axis_size("pb")
        if self.parts != 8:
            (x,) = outer(self.parts, info, pairs, False)
            self.kept = lax.psum_scatter(x.reshape(-1, x.shape[2]), "pb", scatter_dimension=0, tiled=True)
            self.got = self.kept
            self.made = x
        else:
            self.got, self.kept = outer(self.parts, info, pairs, True)
            self.made = self.kept
            self.bits = [1, 2, 4]

    def pending(self):
        return [self.kept, self.got]

    def resume(self, arrays):
        self.kept, self.got = arrays

    def start(self):
        if self.parts == 8:
            self.got = swap(self.got, "pb", self.bits.pop(0))
        return self

    def step(self):
        if self.parts == 8:
            near = (self.kept.astype(F32) + self.got.astype(F32)).astype(BF)
            count = near.shape[0] // 2
            self.kept, self.got = near[:count], near[count:]
            self.start()

    def end(self):
        if self.parts != 8:
            return self.kept
        return (self.kept[0].astype(F32) + self.got[0].astype(F32)).astype(BF)


def root_moves(reach):
    holders = {2: lambda d: d == 0, 1: lambda d: d in (0, 2)}[reach]
    moves = []
    for z in range(4):
        for x in range(2):
            for k in range(4):
                if holders(z ^ k):
                    moves.append(((2 * z + x) * 4 + k, (2 * (z ^ reach) + x) * 4 + k))
    return moves


def at_root():
    return lax.axis_index("pb") // 2 == lax.axis_index("ka")


class OutSpread:
    def __init__(self, w_out):
        self.parts, ka = lax.axis_size("pb"), lax.axis_size("ka")
        self.span, self.size = self.parts // ka, w_out.shape[0]
        if self.parts != 8:
            self.size = w_out.shape[0] // ka
            own = lax.dynamic_slice_in_dim(w_out, lax.axis_index("ka") * self.size, self.size, 0)
            pad = jnp.zeros((slot_of(self.size) - self.size, w_out.shape[2]), BF)
            x = jnp.concatenate([own[:, 0], pad, own[:, 1], pad], axis=0)
            x = lax.ppermute(x, ("pb", "ka"), row_moves(self.parts, ka))
            self.kept, self.got = x, gather_rows(x)
        else:
            x = jnp.concatenate([w_out[:, 0], w_out[:, 1]], axis=0)
            self.kept = jnp.where(at_root(), x, jnp.zeros_like(x))
            self.got = lax.ppermute(x, ("pb", "ka"), root_moves(2))
            self.next = [1, 0]

    def pending(self):
        return [self.kept, self.got]

    def resume(self, arrays):
        self.kept, self.got = arrays

    def step(self):
        if self.parts == 8:
            self.kept = self.kept + self.got
            reach = self.next.pop(0)
            self.got = lax.ppermute(self.kept, ("pb", "ka"), root_moves(reach)) if reach else swap(self.kept, "pb", 1)

    def rows(self, l):
        if self.parts != 8:
            return whole_rows(self.got, self.parts, l * slot_of(self.size), self.size, self.span)
        return Rows(self.pending(), [(0, l * self.size, 0, True), (1, l * self.size, 1, True)], self.size, -1)


class OutFlow:
    def __init__(self, info, pairs):
        self.parts = lax.axis_size("pb")
        if self.parts != 8:
            self.flow = Flow(info, [([(a, 0, b, 0, a.shape[0])], self.parts // lax.axis_size("ka")) for a, b in pairs])
            self.size = pairs[0][0].shape[1] // self.parts
            self.kept = self.got = self.flow.end()
            self.made = self.flow.made
        else:
            sent, self.kept = outer_pair(info, pairs)
            self.made = self.kept
            self.got = swap(sent, "pb", 1)
            self.next = [1, 2]

    def pending(self):
        return [self.kept, self.got]

    def resume(self, arrays):
        self.kept, self.got = arrays

    def add(self):
        return (self.kept.astype(F32) + self.got.astype(F32)).astype(BF)

    def step(self):
        if self.parts == 8:
            self.kept = self.add()
            moves = [(b, a) for a, b in root_moves(self.next.pop(0))]
            self.got = lax.ppermute(self.kept, ("pb", "ka"), moves)

    def turn(self):
        if self.parts == 8:
            near = self.add()
            self.kept = jnp.where(at_root(), near, jnp.zeros_like(near))
            self.got = swap(self.kept, "ka", 2)

    def halves(self):
        near = self.kept + self.got
        return near, swap(near, "ka", 1)

    def end(self):
        ka, slot = lax.axis_size("ka"), slot_of(self.size)
        back = [(b, a) for a, b in row_moves(self.parts, ka)]
        x = lax.all_gather(lax.ppermute(self.kept, ("pb", "ka"), back), "ka")
        return [x[:, i * slot : i * slot + self.size].reshape(ka * self.size, -1) for i in range(2)]


def pair_gather(x):
    groups = [[i, i + 1] for i in range(0, lax.axis_size("ka"), 2)]
    return lax.all_gather(x, "ka", axis_index_groups=groups)


def core_pieces(x, far):
    return swap(jnp.stack([x, far]), "ka", 1)


def in_order(own, far, core):
    me = lax.axis_index("ka")
    near = [own, core[0], far, core[1]]
    found = []
    for k in range(4):
        value = near[3]
        for n in range(3):
            value = jnp.where((me ^ k) == n, near[n], value)
        found.append(value)
    return found


def on_device(tokens, cotangent, lengths, keep_mask, w_qkv, w_out, w_fc, w_proj, norm_gain, norm_bias):
    rows, width = tokens.shape
    pb = lax.axis_size("pb")
    ka = lax.axis_size("ka")
    me = lax.axis_index("ka")
    low, high = me % 2, me // 2
    heads = H // ka
    part = width // ka
    ff = w_fc.shape[2]
    ff_part = ff // ka
    d_rows = w_qkv.shape[0]
    proj_rows = w_proj.shape[0] // ka
    wide = (3 * part + 8 + 127) // 128 * 128
    bounds = jnp.cumsum(lengths[0])
    info = jnp.concatenate([jnp.stack([lax.axis_index("pb"), low]).astype(jnp.int32), bounds.astype(jnp.int32)])

    half, group = 2 * rows, 4 * rows

    def own_half(x, far):
        return jnp.where(high == 0, jnp.concatenate([x, far], axis=0), jnp.concatenate([far, x], axis=0))

    def block(half, which):
        return lax.dynamic_slice_in_dim(half, which * rows, rows, 0)

    def from_pair(sent):
        return lax.dynamic_index_in_dim(pair_gather(sent), 1 - low, 0, False)

    def add_low(kept, got):
        return (kept + got.astype(F32)).astype(BF)

    picked = jnp.concatenate([lax.dynamic_slice_in_dim(w_qkv, i * width + me * part, part, 2) for i in range(3)], axis=2)
    vectors = jnp.concatenate([norm_gain, norm_bias], axis=1)
    first = jnp.concatenate([picked[:, 0], vectors, jnp.zeros((d_rows, wide - 3 * part - 8), BF)], axis=1)
    outs = OutSpread(w_out)
    qkv0 = Spread(first, True)
    keep_rows = jnp.pad(keep_mask.astype(BF)[None, :], ((0, 15), (0, width - rows)))
    tokens_more = jnp.concatenate([tokens, keep_rows], axis=0)
    far_tokens = swap(tokens_more, "ka", 2)
    tokens_more = own_half(tokens_more, far_tokens)
    first, tokens_more, w_fc, w_proj, picked = tick(first, tokens_more, w_fc, w_proj, picked)
    tokens_both = pair_gather(tokens_more)
    tokens_own = own_half(tokens, far_tokens[:rows])
    unit = ff_part // pb
    local_fc = jnp.concatenate(
        [lax.dynamic_slice_in_dim(w_fc, (q * ka + me) * unit, unit, 2) for q in range(pb)], axis=2
    )
    fc_first, fc_second = local_fc[:, 0], local_fc[:, 1]
    local_proj = lax.dynamic_slice_in_dim(w_proj, me * proj_rows, proj_rows, 0)
    proj_first, proj_late = local_proj[:, 0], local_proj[:, 1]
    second = jnp.concatenate([picked[:, 1], jnp.zeros((d_rows, wide - 3 * part), BF)], axis=1)
    tokens_both, fc_first, proj_first, second, cotangent, proj_late = tick(
        qkv0, outs, tokens_both, fc_first, proj_first, second, cotangent, proj_late
    )
    qkv0.step()
    outs.step()
    proj0 = Spread(proj_first)
    fc0_all = gather_rows(fc_first)
    tokens_both, cotangent, second, fc_second, proj_late = tick(
        qkv0, outs, proj0, tokens_both, cotangent, second, fc_second, proj_late
    )
    outs.step()
    proj0.step()
    qkv1 = Spread(second)
    far_cotangent = swap(cotangent, "ka", 2)
    qkv = [qkv0.rows(), None]

    keys = ("stream", "x", "projected", "attended", "lse", "middle", "both", "hidden", "active")
    got = attention_forward(True, True, info, group, None, tokens_both, qkv[0], part, heads)
    x_all, projected, attended, lse, tokens_all, vec, kept_all = got
    attended, proj_late = tick(attended, outs, proj0, proj_late)
    proj0.step()
    proj1_all = gather_rows(proj_late)
    out = [outs.rows(0), outs.rows(1)]
    sent, kept = attention_out(info, attended, out[0])
    got, fc_second, far_cotangent = tick(from_pair(sent), qkv1, fc_second, far_cotangent)
    near = add_low(kept, got)
    far = swap(near, "ka", 2)
    qkv1.step()
    fc1 = Spread(fc_second)
    branch = own_half(cotangent, far_cotangent)
    middle, own = norm_after(1, tokens_own, near, far, vec)
    both = pair_gather(own)
    fc = [whole_rows(fc0_all, pb, 0, d_rows), None]
    proj = [proj0.rows(), whole_rows(proj1_all, pb, 0, proj_rows)]
    hidden, active, sent, kept = feed_forward(info, both, fc[0], proj[0])
    kept0 = dict(zip(keys, (tokens_own, x_all, projected, attended, lse, middle, both, hidden, active)))
    got, branch_own = tick(from_pair(sent), qkv1, fc1, branch)
    near = add_low(kept, got)
    far = swap(near, "ka", 2)
    fc1.step()
    qkv1.step()
    branch = pair_gather(branch_own)
    qkv[1] = qkv1.rows()
    far, branch = tick(far, branch)
    stream, own = norm_after(2, middle, near, far, vec)
    both = pair_gather(own)
    x_all, projected, attended, lse = attention_forward(False, False, info, group, kept_all, both, qkv[1], part, heads)
    sent, kept = attention_out(info, attended, out[1])
    (got,) = tick(from_pair(sent), fc1)
    near = add_low(kept, got)
    far = swap(near, "ka", 2)
    fc1.step()
    fc[1] = fc1.rows()
    middle, own = norm_after(3, stream, near, far, vec)
    both = pair_gather(own)
    hidden, active, last_sent, last_kept = feed_forward(info, both, fc[1], proj[1])
    kept1 = dict(zip(keys, (stream, x_all, projected, attended, lse, middle, both, hidden, active)))

    sums = [None] * 4

    def fc_pair(kept, grad_hidden):
        return [(kept["both"].reshape(group, width), 0, grad_hidden, 0, group)], 0

    def proj_pair(kept, branch):
        return [(kept["active"], 0, branch.reshape(group, width), 0, group)], 0

    def qkv_pair(kept, grad_projected, more=()):
        return [(kept["x"], 0, grad_projected, 0, group), *more], 0

    def attend_back(l, kept, both):
        return attention_backward(
            l == 0, l == 0, info, kept_all, both, kept["projected"], kept["lse"], qkv[l], out[l], tokens_all, heads
        )

    grad_hidden, sent, kept = feed_backward(info, branch, kept1["hidden"], fc[1], proj[1])
    near = add_low(kept, from_pair(sent))
    far = swap(near, "ka", 2)
    near_in, grad_hidden, last_sent, last_kept = tick(near, grad_hidden, last_sent, last_kept)
    last = add_low(last_kept, from_pair(last_sent))
    flow_a = Flow(info, [fc_pair(kept1, grad_hidden), proj_pair(kept1, branch)]).start()
    far, last, unused = tick(far, last, flow_a.made)
    grad, own, sums[3] = norm_back(3, branch_own, near, far, kept1["middle"], vec)
    both = pair_gather(own)
    middle_one, grad_projected, sent, kept = attend_back(1, kept1, both)
    (got,) = tick(from_pair(sent), flow_a)
    near = add_low(kept, got)
    far = swap(near, "ka", 2)
    near_in, grad_projected = tick(near, grad_projected)
    flow_b = Flow(info, [qkv_pair(kept1, grad_projected)]).start()
    flow_a.step()
    far, unused = tick(far, flow_b.made)
    grad, own, sums[2] = norm_back(2, grad, near, far, kept1["stream"], vec)
    branch = pair_gather(own)
    grad_hidden, sent, kept = feed_backward(info, branch, kept0["hidden"], fc[0], proj[0])
    (got,) = tick(from_pair(sent), flow_a, flow_b)
    near = add_low(kept, got)
    far = swap(near, "ka", 2)
    near_in, grad_hidden = tick(near, grad_hidden)
    flow_c = Flow(info, [fc_pair(kept0, grad_hidden), proj_pair(kept0, branch)]).start()
    flow_a.step()
    flow_b.step()
    far, unused = tick(far, flow_c.made)
    grad, own, sums[1] = norm_back(1, grad, near, far, kept0["middle"], vec)
    both = pair_gather(own)
    middle_all, grad_projected, sent, kept, sums[0] = attend_back(0, kept0, both)
    (got,) = tick(from_pair(sent), flow_a, flow_b, flow_c)
    near = add_low(kept, got)
    far = swap(block(near, 1 - high), "ka", 2)
    near_in, grad_projected, middle_all, last = tick(near, grad_projected, middle_all, last)
    halved = [sums[0]] + [0.5 * s for s in sums[1:]]
    stacked = jnp.concatenate([s[i : i + 1] for i in range(2) for s in halved] + [jnp.zeros((8, width), F32)], axis=0).astype(BF)
    spots = (3 * part + jnp.arange(16)[:, None] == jnp.arange(wide)[None, :]) & (jnp.arange(16)[:, None] < 8)
    flow_d = Flow(info, [qkv_pair(kept0, grad_projected, [(stacked, 0, spots.astype(BF), 0, 16)])]).start()
    flow_o = OutFlow(info, [(kept0["attended"], middle_all), (kept1["attended"], middle_one)])
    flow_b.step()
    flow_c.step()
    after_fc = slot_of(d_rows)
    done_a = flow_a.end()
    far, unused, unused = tick(far, flow_d.made, flow_o.made)
    (grad_tokens,) = norm_back(0, block(grad, high), block(near, high), far, block(kept0["stream"], high), vec, True)

    done_a, grad_tokens, last = tick(flow_b, flow_c, flow_d, flow_o, done_a, grad_tokens, last)
    flow_d.step()
    flow_o.step()
    flow_c.step()
    done_b = flow_b.end()
    far_a = swap(done_a, "ka", 2)
    far_b = swap(done_b, "ka", 2)
    far_a, far_b, last = tick(flow_d, flow_c, flow_o, far_a, far_b, last)
    flow_d.step()
    flow_o.step()
    done_c = flow_c.end()
    far_c = swap(done_c, "ka", 2)
    core_a = core_pieces(done_a, far_a)
    last_far = swap(block(last, 1 - high), "ka", 2)
    far_c, core_a, last_far = tick(flow_d, flow_o, far_c, core_a, last_far)
    done_d = flow_d.end()
    far_d = swap(done_d, "ka", 2)
    flow_o.turn()
    core_b = core_pieces(done_b, far_b)
    core_c = core_pieces(done_c, far_c)
    output = (block(kept1["middle"], high) + (block(last, high).astype(F32) + last_far.astype(F32))).astype(BF)
    far_d, core_b, core_c, output = tick(far_d, flow_o, core_b, core_c, output)
    core_d = core_pieces(done_d, far_d)
    block_a, block_b, block_c, block_d = [
        (done_a, far_a, core_a),
        (done_b, far_b, core_b),
        (done_c, far_c, core_c),
        (done_d, far_d, core_d),
    ]
    if pb == 8:
        near_out, far_out = flow_o.halves()
        rank = me.astype(jnp.int32).reshape(1)
        sum_fc, sum_proj = finish_feed(rank, (block_c, block_a), after_fc, unit, d_rows, proj_rows)
        sum_qkv, sum_out, stacked = finish_attend(rank, (block_d, block_b), near_out, far_out, part)
        return (output, grad_tokens, sum_qkv, sum_out, sum_fc, sum_proj, stacked[:4].T, stacked[4:].T)

    def pair(one, other):
        return jnp.stack([one, other], axis=1).astype(F32)

    def columns(pieces):
        return jnp.stack([p[:d_rows].reshape(d_rows, pb, unit) for p in pieces], axis=2).reshape(d_rows, ff)

    def heads_of(pieces):
        return jnp.concatenate([p[:d_rows, i * part : (i + 1) * part] for i in range(3) for p in pieces], axis=1)

    def rows_of(pieces):
        return jnp.concatenate([p[after_fc : after_fc + proj_rows] for p in pieces], axis=0)

    a, b, c, d = [in_order(*pieces) for pieces in (block_a, block_b, block_c, block_d)]
    stacked = sum(p[:d_rows, 3 * part : 3 * part + 8].astype(F32) for p in d)
    return (
        output,
        grad_tokens,
        pair(heads_of(d), heads_of(b)),
        pair(*flow_o.end()),
        pair(columns(c), columns(a)),
        pair(rows_of(c), rows_of(a)),
        stacked[:, :4],
        stacked[:, 4:],
    )


def solution(mesh):
    return jax.shard_map(
        on_device,
        mesh=mesh,
        in_specs=(
            P(("pb", "ka"), None),
            P(("pb", "ka"), None),
            P("pb", None),
            P(("pb", "ka")),
            P("pb", None, None),
            P("pb", None, None),
            P("pb", None, None),
            P("pb", None, None),
            P("pb", None),
            P("pb", None),
        ),
        out_specs=(
            P(("pb", "ka"), None),
            P(("pb", "ka"), None),
            P("pb", None, None),
            P("pb", None, None),
            P("pb", None, None),
            P("pb", None, None),
            P("pb", None),
            P("pb", None),
        ),
        check_vma=False,
    )
```

```python
import functools
import jax
import jax.numpy as jnp
from jax import lax
from jax.experimental import pallas as pl
from jax.experimental.pallas import tpu as pltpu
from jax.sharding import PartitionSpec as P

H = 12
EPSILON = 1e-05
FLOOR_VALUE = -1e30
BF = jnp.bfloat16
F32 = jnp.float32
VM = pl.BlockSpec(memory_space=pltpu.VMEM)
SM = pl.BlockSpec(memory_space=pltpu.SMEM)
SHIFTS = (0, 4, 2, 6)
GELU_A = 0.7978845608028654
GELU_B = 0.044715


def dot(a, b, ca, cb):
    return lax.dot_general(a, b, (((ca,), (cb,)), ((), ())), preferred_element_type=F32)


def call(kernel, outs, ins, scratch=(), flops=0, name=None):
    moved = sum(a.size * a.dtype.itemsize for a in ins)
    return pl.pallas_call(
        kernel,
        out_shape=[jax.ShapeDtypeStruct(s, t) for s, t in outs],
        in_specs=[SM if a.dtype == jnp.int32 and a.ndim == 1 else VM for a in ins],
        out_specs=[VM] * len(outs),
        scratch_shapes=list(scratch),
        compiler_params=pltpu.CompilerParams(vmem_limit_bytes=20 * 1024 * 1024),
        cost_estimate=pl.CostEstimate(flops=flops, bytes_accessed=moved, transcendentals=0),
        name=name,
    )(*ins)


def at(index, rows):
    return pl.ds(pl.multiple_of(index * rows, rows), rows)


class Rows:
    def __init__(self, arrays, plan, size, span=0):
        self.arrays, self.plan, self.size, self.span = arrays, plan, size, span
        self.shape = (size * len(plan), arrays[0].shape[1])

    def scratch(self):
        return pltpu.VMEM(self.shape, F32 if self.size % 16 else BF)

    def load(self, refs, scratch, me):
        for index, start, p, relative in self.plan:
            place = me ^ p if relative else p
            if self.span < 0:
                place = place & (len(self.plan) - 1)
            elif self.span:
                place = place_of(place, self.span, len(self.plan) // self.span)
            target = at(place, self.size) if relative else slice(place * self.size, (place + 1) * self.size)
            scratch[target, :] = refs[index][start : start + self.size, :].astype(scratch.dtype)


def place_of(p, span, ka):
    return (p % span) * ka + p // span if isinstance(p, int) else lax.rem(p, span) * ka + lax.div(p, span)


def take_refs(refs, *weights):
    return [[refs.pop(0) for unused in w.arrays] for w in weights]


def norm_parts(values):
    average = jnp.mean(values, axis=-1, keepdims=True)
    centered = values - average
    spread = jnp.mean(centered * centered, axis=-1, keepdims=True)
    inverse = lax.rsqrt(spread + EPSILON)
    return centered * inverse, inverse


def block_allowed(info, kept_ref, b, block, keys):
    i = b * block + lax.broadcasted_iota(jnp.int32, (1, block), 1)
    j = lax.broadcasted_iota(jnp.int32, (keys, 1), 0)

    def segment(t):
        total = jnp.zeros_like(t)
        for n in range(2, info.shape[0]):
            total = total + jnp.where(t >= info[n], 1, 0)
        return total

    same = segment(i) == segment(j)
    itself = i == j
    return same & (j <= i) & ((kept_ref[:keys, :] > 0) | itself)


def canonical(both, full):
    block, stride = full.shape[0] // 4, both.shape[1] // 2
    for h in range(2):
        for i in range(2):
            full[(2 * i + h) * block : (2 * i + h + 1) * block, :] = both[h, i * stride : i * stride + block, :]


def split_halves(low, full, kept, sent):
    block = kept.shape[0] // 2
    for i in range(2):
        kept[i * block : (i + 1) * block, :] = full[at(2 * i + low, block), :].astype(kept.dtype)
        sent[i * block : (i + 1) * block, :] = full[at(2 * i + 1 - low, block), :].astype(sent.dtype)


def attention_forward_kernel(first, signed, qkv, heads, *refs):
    refs = list(refs)
    info = refs.pop(0)
    if not first:
        kept_ref = refs.pop(0)
    both = refs.pop(0)
    (pieces,) = take_refs(refs, qkv)
    x_ref, proj_ref, att_ref, lse_ref = [refs.pop(0) for unused in range(4)]
    if first:
        tokens, vec_ref, kept_ref = refs.pop(0), refs.pop(0), refs.pop(0)
    (w,) = refs
    me, low = info[0], info[1]
    qkv.load(pieces, w, me)
    part = att_ref.shape[1]
    hd = part // heads
    group, width = x_ref.shape
    block = group // 4
    if first:
        tail = w.shape[1] - 3 * part
        pick = lax.broadcasted_iota(jnp.int32, (8, tail), 0) == lax.broadcasted_iota(jnp.int32, (8, tail), 1)
        vec = dot(pick.astype(F32).astype(BF), w[:, 3 * part :], 1, 1)
        vec_ref[...] = vec
        canonical(both, tokens)
        stride = both.shape[1] // 2
        for h in range(2):
            for i in range(2):
                row = both[h, i * stride + block : i * stride + block + 1, :block].astype(F32)
                kept_ref[(2 * i + h) * block : (2 * i + h + 1) * block, :] = jnp.transpose(jnp.broadcast_to(row, (8, block)))[:, :1]
        for b in range(4):
            values = tokens[b * block : (b + 1) * block, :].astype(F32)
            normal, unused = norm_parts(values)
            x_ref[b * block : (b + 1) * block, :] = (normal * vec[0:1] + vec[4:5]).astype(BF)
    else:
        canonical(both, x_ref)
    proj_ref[...] = dot(x_ref[...], w[...], 1, 0).astype(BF)
    scale = hd ** (-0.5)
    for b in range(4):
        keys = (b + 1) * block
        rows = slice(b * block, keys)
        allowed = block_allowed(info, kept_ref, b, block, keys)
        each = range(heads)
        q = [proj_ref[rows, h * hd : (h + 1) * hd] * scale for h in each]
        k = [proj_ref[:keys, part + h * hd : part + (h + 1) * hd] for h in each]
        v = [proj_ref[:keys, 2 * part + h * hd : 2 * part + (h + 1) * hd] for h in each]
        scores = [dot(k[h], q[h], 1, 1) for h in each]
        masked = [jnp.where(allowed, jnp.abs(s) if signed else s, FLOOR_VALUE) for s in scores]
        peak = [jnp.max(m, axis=0, keepdims=True) for m in masked]
        raised = [jnp.exp(masked[h] - peak[h]) for h in each]
        total = [jnp.sum(r, axis=0, keepdims=True) for r in raised]
        if signed:
            lifted = [jnp.where(allowed, raised[h] - jnp.exp(-peak[h]), 0.0) for h in each]
            raised = [jnp.where(scores[h] < 0, -lifted[h], lifted[h]) for h in each]
        weights = [(raised[h] * (1.0 / total[h])).astype(BF) for h in each]
        values = [dot(v[h], weights[h], 0, 0) for h in each]
        for h in each:
            att_ref[rows, h * hd : (h + 1) * hd] = jnp.transpose(values[h]).astype(BF)
            lse_ref[h : h + 1, rows] = peak[h] + jnp.log(total[h])


def attention_forward(first, signed, info, group, kept, both, qkv, part, heads):
    width = both.shape[2]
    outs = [((group, width), BF), ((group, qkv.shape[1]), BF), ((group, part), BF), ((8, group), F32)]
    if first:
        outs += [((group, width), BF), ((8, width), F32), ((group, 1), F32)]
    return call(
        functools.partial(attention_forward_kernel, first, signed, qkv, heads),
        outs,
        [info] + ([] if first else [kept]) + [both, *qkv.arrays],
        [qkv.scratch()],
        flops=2 * group * width * 3 * part,
        name="attend",
    )


def attention_out_kernel(out, *refs):
    refs = list(refs)
    info, attended = refs.pop(0), refs.pop(0)
    (pieces,) = take_refs(refs, out)
    sent, kept, w_out, partial = refs
    out.load(pieces, w_out, info[0])
    partial[...] = dot(attended[...], w_out[...].astype(BF), 1, 0)
    split_halves(info[1], partial, kept, sent)


def attention_out(info, attended, out):
    group, width = attended.shape[0], out.shape[1]
    return call(
        functools.partial(attention_out_kernel, out),
        [((group // 2, width), BF), ((group // 2, width), F32)],
        [info, attended, *out.arrays],
        [out.scratch(), pltpu.VMEM((group, width), F32)],
        flops=2 * group * width * out.shape[0],
        name="attend_out",
    )


def gelu_parts(v):
    inner = GELU_A * (v + GELU_B * v * v * v)
    return jnp.tanh(inner)


def feed_forward_kernel(fc, proj, *refs):
    refs = list(refs)
    info, both = [refs.pop(0) for unused in range(2)]
    fc_refs, proj_refs = take_refs(refs, fc, proj)
    hidden, active, sent, kept, w, w_proj, partial = refs
    fc.load(fc_refs, w, info[0])
    proj.load(proj_refs, w_proj, info[0])
    half = both.shape[1]
    ff = w_proj.shape[0]
    step = ff // 3
    for h in range(2):
        rows = slice(h * half, (h + 1) * half)
        total = None
        for f in range(3):
            cols = slice(f * step, (f + 1) * step)
            hid = dot(both[h], w[:, cols], 1, 0)
            hidden[rows, cols] = hid
            act = (0.5 * hid * (1.0 + gelu_parts(hid))).astype(BF)
            active[rows, cols] = act
            term = dot(act, w_proj[cols, :], 1, 0)
            total = term if total is None else total + term
        partial[h] = total
    kept[...] = partial[info[1]]
    sent[...] = partial[1 - info[1]].astype(BF)


def feed_forward(info, both, fc, proj):
    two, half, width = both.shape
    ff = proj.shape[0]
    outs = [((2 * half, ff), F32), ((2 * half, ff), BF), ((half, width), BF), ((half, width), F32)]
    return call(
        functools.partial(feed_forward_kernel, fc, proj),
        outs,
        [info, both, *fc.arrays, *proj.arrays],
        [fc.scratch(), proj.scratch(), pltpu.VMEM((2, half, width), F32)],
        flops=8 * half * width * ff,
        name="feed",
    )


def norm_kernel(row, stream, near, far, vec, middle, normed):
    values = stream[...].astype(F32) + (near[...].astype(F32) + far[...].astype(F32))
    middle[...] = values
    normal, unused = norm_parts(values)
    normed[...] = (normal * vec[row : row + 1, :] + vec[row + 4 : row + 5, :]).astype(BF)


def norm_after(row, stream, near, far, vec):
    shape = stream.shape
    return call(functools.partial(norm_kernel, row), [(shape, F32), (shape, BF)], [stream, near, far, vec], name="norm")


def feed_backward_kernel(fc, proj, *refs):
    refs = list(refs)
    info, both, hidden = [refs.pop(0) for unused in range(3)]
    fc_refs, proj_refs = take_refs(refs, fc, proj)
    grad_hidden, sent, kept, w, w_proj, partial = refs
    fc.load(fc_refs, w, info[0])
    proj.load(proj_refs, w_proj, info[0])
    half = both.shape[1]
    ff = w_proj.shape[0]
    step = ff // 3
    for h in range(2):
        rows = slice(h * half, (h + 1) * half)
        total = None
        for f in range(3):
            cols = slice(f * step, (f + 1) * step)
            grad_active = dot(both[h], w_proj[cols, :], 1, 1)
            v = hidden[rows, cols]
            t = gelu_parts(v)
            slope = 0.5 * (1.0 + t) + 0.5 * v * (1.0 - t * t) * (GELU_A * (1.0 + 3.0 * GELU_B * v * v))
            gh = (slope * grad_active).astype(BF)
            grad_hidden[rows, cols] = gh
            term = dot(gh, w[:, cols], 1, 1)
            total = term if total is None else total + term
        partial[h] = total
    kept[...] = partial[info[1]]
    sent[...] = partial[1 - info[1]].astype(BF)


def feed_backward(info, both, hidden, fc, proj):
    two, half, width = both.shape
    ff = proj.shape[0]
    outs = [((2 * half, ff), BF), ((half, width), BF), ((half, width), F32)]
    return call(
        functools.partial(feed_backward_kernel, fc, proj),
        outs,
        [info, both, hidden, *fc.arrays, *proj.arrays],
        [fc.scratch(), proj.scratch(), pltpu.VMEM((2, half, width), F32)],
        flops=8 * half * width * ff,
        name="feed_back",
    )


def norm_backward_kernel(row, grad, near, far, source, vec, out, *rest):
    incoming = near[...].astype(F32) + far[...].astype(F32)
    normal, inverse = norm_parts(source[...].astype(F32))
    grad_normal = incoming * vec[row : row + 1, :]
    mean_grad = jnp.mean(grad_normal, axis=-1, keepdims=True)
    mean_cross = jnp.mean(grad_normal * normal, axis=-1, keepdims=True)
    value = grad[...].astype(F32) + inverse * (grad_normal - mean_grad - normal * mean_cross)
    out[...] = value
    if not rest:
        return
    low, sums = rest
    low[...] = value.astype(BF)
    sums[0:1, :] = jnp.sum(incoming * normal, axis=0, keepdims=True)
    sums[1:2, :] = jnp.sum(incoming, axis=0, keepdims=True)


def norm_back(row, grad, near, far, source, vec, last=False):
    shape = source.shape
    return call(
        functools.partial(norm_backward_kernel, row),
        [(shape, F32)] if last else [(shape, F32), (shape, BF), ((2, shape[1]), F32)],
        [grad, near, far, source, vec],
        name="norm_back",
    )


def attention_backward_kernel(first, signed, qkv, out, heads, *refs):
    refs = list(refs)
    info, kept_ref, both, proj, lse = [refs.pop(0) for unused in range(5)]
    pieces, out_pieces = take_refs(refs, qkv, out)
    if first:
        tokens = refs.pop(0)
    gm_ref, gp_ref, sent, kept = [refs.pop(0) for unused in range(4)]
    if first:
        sums = refs.pop(0)
    w, w_out, partial, gatt, gk_sum, gv_sum = refs
    me, low = info[0], info[1]
    qkv.load(pieces, w, me)
    out.load(out_pieces, w_out, me)
    part = w_out.shape[0]
    hd = part // heads
    group = gm_ref.shape[0]
    block = group // 4
    canonical(both, gm_ref)
    gatt[...] = dot(gm_ref[...], w_out[...].astype(BF), 1, 1).astype(BF)
    scale = hd ** (-0.5)
    gp_ref[:, 3 * part :] = jnp.zeros((group, gp_ref.shape[1] - 3 * part), BF)
    for b in reversed(range(4)):
        keys = (b + 1) * block
        rows = slice(b * block, keys)
        allowed = block_allowed(info, kept_ref, b, block, keys)
        each = range(heads)
        q = [proj[rows, h * hd : (h + 1) * hd] * scale for h in each]
        k = [proj[:keys, part + h * hd : part + (h + 1) * hd] for h in each]
        v = [proj[:keys, 2 * part + h * hd : 2 * part + (h + 1) * hd] for h in each]
        g = [gatt[rows, h * hd : (h + 1) * hd] for h in each]
        level = [lse[h : h + 1, rows] for h in each]
        scores = [dot(k[h], q[h], 1, 1) for h in each]
        grad_weights = [dot(v[h], g[h], 1, 1) for h in each]
        absolute = [jnp.exp(jnp.where(allowed, jnp.abs(scores[h]) if signed else scores[h], FLOOR_VALUE) - level[h]) for h in each]
        if signed:
            lifted = [jnp.where(allowed, absolute[h] - jnp.exp(-level[h]), 0.0) for h in each]
            weights = [jnp.where(scores[h] < 0, -lifted[h], lifted[h]) for h in each]
        else:
            weights = absolute
        shift = [jnp.sum(grad_weights[h] * weights[h], axis=0, keepdims=True) for h in each]
        if signed:
            shift = [jnp.where(scores[h] > 0, shift[h], jnp.where(scores[h] < 0, -shift[h], 0.0)) for h in each]
        gs = [(absolute[h] * (grad_weights[h] - shift[h])).astype(BF) for h in each]
        gv = [dot(weights[h].astype(BF), g[h], 1, 0) for h in each]
        gk = [dot(gs[h], q[h], 1, 0) for h in each]
        gq = [dot(k[h], gs[h], 0, 0) for h in each]
        for h in each:
            gp_ref[rows, h * hd : (h + 1) * hd] = jnp.transpose(gq[h] * scale).astype(BF)
            if b == 3:
                gk_sum[h] = gk[h]
                gv_sum[h] = gv[h]
            else:
                gk_sum[h, :keys] += gk[h]
                gv_sum[h, :keys] += gv[h]
    for h in range(heads):
        gp_ref[:, part + h * hd : part + (h + 1) * hd] = gk_sum[h].astype(BF)
        gp_ref[:, 2 * part + h * hd : 2 * part + (h + 1) * hd] = gv_sum[h].astype(BF)
    partial[...] = dot(gp_ref[...], w[...], 1, 1)
    split_halves(low, partial, kept, sent)
    if first:
        gain = bias = 0.0
        for b in range(4):
            rows = slice(b * block, (b + 1) * block)
            normal, unused = norm_parts(tokens[rows, :].astype(F32))
            value = partial[rows, :]
            gain = gain + jnp.sum(value * normal, axis=0, keepdims=True)
            bias = bias + jnp.sum(value, axis=0, keepdims=True)
        sums[0:1, :] = gain
        sums[1:2, :] = bias


def attention_backward(first, signed, info, kept, both, proj, lse, qkv, out, tokens, heads):
    two, half, width = both.shape
    group = 2 * half
    part = out.shape[0]
    wide = qkv.shape[1]
    outs = [((group, width), BF), ((group, wide), BF), ((half, width), BF), ((half, width), F32)]
    if first:
        outs += [((2, width), F32)]
    return call(
        functools.partial(attention_backward_kernel, first, signed, qkv, out, heads),
        outs,
        [info, kept, both, proj, lse, *qkv.arrays, *out.arrays] + ([tokens] if first else []),
        [
            qkv.scratch(),
            out.scratch(),
            pltpu.VMEM((group, width), F32),
            pltpu.VMEM((group, part), BF),
            pltpu.VMEM((heads, group, part // heads), F32),
            pltpu.VMEM((heads, group, part // heads), F32),
        ],
        flops=2 * group * width * 4 * part,
        name="attend_back",
    )


def outer_kernel(parts, plans, bits, *refs):
    info, scratch = refs[0], refs[-1]
    outs = refs[-3:-1] if bits else refs[-2:-1]
    shifts = halving(bits)
    start = 0
    for segments, rows, slot, span, cols in plans:
        size = rows // parts
        blank = scratch.shape[1] - cols

        def place(p):
            return place_of(p, span, parts // span) if span else p

        total = None
        for left, first, right, second, count in segments:
            term = dot(refs[left][first : first + count, :], refs[right][second : second + count, :], 0, 0)
            total = term if total is None else total + term
        scratch[:rows, :cols] = total
        if blank:
            scratch[:rows, cols:] = jnp.zeros((rows, blank), F32)
        for j in range(len(shifts) if bits else parts):
            if bits:
                targets = [at(place(info[0] ^ shifts[j] ^ bits[0]), size), at(place(info[0] ^ shifts[j]), size)]
            else:
                targets = [slice(place(j) * size, (place(j) + 1) * size)]
            for ref, target in zip(outs, targets):
                ref[j, start : start + size, :] = scratch[target, :].astype(BF)
                if slot > size:
                    ref[j, start + size : start + slot, :] = jnp.zeros((slot - size, scratch.shape[1]), BF)
        start += slot


def halving(bits):
    return [0, bits[2], bits[1], bits[1] | bits[2]] if bits else []


def slot_of(size):
    return (size + 15) // 16 * 16


def outer(parts, info, pairs, bits):
    arrays, plans = [info], []

    def number(a):
        for n, other in enumerate(arrays):
            if other is a:
                return n
        arrays.append(a)
        return len(arrays) - 1

    for segments, span in pairs:
        rows = segments[0][0].shape[1]
        numbers = [(number(a), first, number(b), second, count) for a, first, b, second, count in segments]
        plans.append((numbers, rows, slot_of(rows // parts), span, segments[0][2].shape[1]))
    cols = max(p[4] for p in plans)
    tall = sum(p[2] for p in plans)
    outs = [((parts // 2, tall, cols), BF)] * 2 if bits else [((parts, tall, cols), BF)]
    return call(
        functools.partial(outer_kernel, parts, plans, bits),
        outs,
        arrays,
        [pltpu.VMEM((max(p[1] for p in plans), cols), F32)],
        flops=sum(2 * p[1] * cols * sum(seg[4] for seg in p[0]) for p in plans),
        name="outer",
    )


def outer_pair_kernel(count, *refs):
    info, ins, (sent, kept, scratch) = refs[0], refs[1 : 1 + 2 * count], refs[1 + 2 * count :]
    size = scratch.shape[0] // 2
    low = info[0] & 1
    for i in range(count):
        scratch[...] = dot(ins[2 * i][...], ins[2 * i + 1][...], 0, 0)
        kept[i * size : (i + 1) * size, :] = scratch[at(low, size), :].astype(BF)
        sent[i * size : (i + 1) * size, :] = scratch[at(1 - low, size), :].astype(BF)


def outer_pair(info, pairs):
    rows, cols = pairs[0][0].shape[1], pairs[0][1].shape[1]
    shape = (len(pairs) * rows // 2, cols)
    return call(
        functools.partial(outer_pair_kernel, len(pairs)),
        [(shape, BF)] * 2,
        [info] + [a for pair in pairs for a in pair],
        [pltpu.VMEM((rows, cols), F32)],
        flops=len(pairs) * 2 * rows * cols * pairs[0][0].shape[0],
        name="outer",
    )


def piece_refs(refs):
    own, far, core = refs[:3]
    return [own, core.at[0], far, core.at[1]]


def finish_feed_kernel(first, unit, info, *refs):
    w_fc, w_proj, scratch = refs[-3:]
    me = info[0]
    size = w_fc.shape[0]
    rows = w_proj.shape[0] // 4
    for l in range(2):
        pieces = piece_refs(refs[3 * l :])
        values = [p[:size, :] for p in pieces]
        for k in range(4):
            value = values[3]
            for n in range(3):
                value = jnp.where((me ^ k) == n, values[n], value)
            for q in range(value.shape[1] // unit):
                scratch[:, (q * 4 + k) * unit : (q * 4 + k + 1) * unit] = value[:, q * unit : (q + 1) * unit]
        w_fc[:, l, :] = scratch[...].astype(F32)
        for n in range(4):
            w_proj[at(me ^ n, rows), l, :] = pieces[n][first : first + rows, :].astype(F32)


def finish_feed(me, blocks, first, unit, size, rows):
    width = blocks[0][0].shape[1]
    ff = 4 * width
    return call(
        functools.partial(finish_feed_kernel, first, unit),
        [((size, 2, ff), F32), ((4 * rows, 2, width), F32)],
        [me] + [a for block in blocks for a in block],
        [pltpu.VMEM((size, ff), BF)],
        name="finish_feed",
    )


def finish_attend_kernel(part, info, *refs):
    w_qkv, vectors, scratch = refs[6:]
    me = info[0]
    size = w_qkv.shape[0]
    for l in range(2):
        pieces = piece_refs(refs[3 * l :])
        values = [p[...] for p in pieces]
        for k in range(4):
            value = values[3]
            for n in range(3):
                value = jnp.where((me ^ k) == n, values[n], value)
            for i in range(3):
                scratch[:, (i * 4 + k) * part : (i * 4 + k + 1) * part] = value[:, i * part : (i + 1) * part]
        w_qkv[:, l, :] = scratch[...].astype(F32)
        if l == 0:
            tail = values[0].shape[1] - 3 * part
            pick = lax.broadcasted_iota(jnp.int32, (8, tail), 0) == lax.broadcasted_iota(jnp.int32, (8, tail), 1)
            pick = pick.astype(F32).astype(BF)
            total = None
            for value in values:
                term = dot(pick, value[:, 3 * part :], 1, 1)
                total = term if total is None else total + term
            vectors[...] = total


def finish_attend(me, blocks, part):
    size = blocks[0][0].shape[0]
    columns = 12 * part
    return call(
        functools.partial(finish_attend_kernel, part),
        [((size, 2, columns), F32), ((8, size), F32)],
        [me] + [a for block in blocks for a in block],
        [pltpu.VMEM((size, columns), BF)],
        name="finish_attend",
    )


def finish_out_kernel(near, far, w_out):
    size = w_out.shape[0]
    for l in range(2):
        rows = slice(l * size, (l + 1) * size)
        w_out[:, l, :] = near[rows, :].astype(F32) + far[rows, :].astype(F32)


def finish_out(near, far):
    rows, width = near.shape
    return call(finish_out_kernel, [((rows // 2, 2, width), F32)], [near, far], name="finish_out")


def stack_kernel(*refs):
    out = refs[-1]
    start = 0
    for ref in refs[:-1]:
        out[start : start + ref.shape[0], :] = ref[...]
        start += ref.shape[0]


def stack_rows(arrays):
    shape = (sum(a.shape[0] for a in arrays), arrays[0].shape[1])
    return call(stack_kernel, [(shape, BF)], list(arrays), name="stack")[0]


def tick(*items):
    flat = [a for item in items for a in (item.pending() if hasattr(item, "pending") else [item])]
    flat = list(lax.optimization_barrier(tuple(flat)))
    found = []
    for item in items:
        if hasattr(item, "pending"):
            count = len(item.pending())
            item.resume(flat[:count])
            del flat[:count]
        else:
            found.append(flat.pop(0))
    return found


def swap(x, axis, bit):
    size = lax.axis_size(axis)
    return lax.ppermute(x, axis, [(i, i ^ bit) for i in range(size)])


def row_moves(pb, ka):
    span = pb // ka
    return [(p * ka + k, (k * span + p % span) * ka + p // span) for p in range(pb) for k in range(ka)]


def gather_rows(x):
    return lax.all_gather(x, "pb", axis=0, tiled=True)


def whole_rows(x, parts, start, size, span=0):
    piece = x.shape[0] // parts
    return Rows([x], [(0, p * piece + start, p, False) for p in range(parts)], size, span)


class Spread:
    def __init__(self, x, direct=False):
        self.rows_each, self.parts = x.shape[0], lax.axis_size("pb")
        self.bits = [1] if direct else [2, 1]
        if self.parts != 8:
            self.kept, self.got = x, [gather_rows(x)]
        elif direct:
            self.kept, self.got = x, [swap(x, "pb", s) for s in SHIFTS[1:]]
        else:
            self.kept, self.got = x, [swap(x, "pb", 4)]

    def pending(self):
        return [self.kept, *self.got]

    def resume(self, arrays):
        self.kept, *self.got = arrays

    def step(self):
        if self.parts != 8:
            return
        self.kept = stack_rows([self.kept, *self.got])
        self.got = [swap(self.kept, "pb", self.bits.pop(0))]

    def rows(self, first=0, size=None, span=0):
        size = size or self.rows_each
        if self.parts != 8:
            return whole_rows(self.got[0], self.parts, first, size, span)
        each = self.rows_each
        plan = [(n, i * each + first, s + n, True) for n in range(2) for i, s in enumerate(SHIFTS)]
        return Rows(self.pending(), plan, size, span)


class Flow:
    def __init__(self, info, pairs, bits=(1, 2, 4)):
        self.parts = lax.axis_size("pb")
        if self.parts != 8:
            (x,) = outer(self.parts, info, pairs, ())
            self.kept = lax.psum_scatter(x.reshape(-1, x.shape[2]), "pb", scatter_dimension=0, tiled=True)
            self.got = self.kept
            self.made = x
        else:
            self.got, self.kept = outer(self.parts, info, pairs, bits)
            self.made = self.kept
            self.bits = list(bits)

    def pending(self):
        return [self.kept, self.got]

    def resume(self, arrays):
        self.kept, self.got = arrays

    def start(self):
        if self.parts == 8:
            self.got = swap(self.got, "pb", self.bits.pop(0))
        return self

    def step(self):
        if self.parts == 8:
            near = (self.kept.astype(F32) + self.got.astype(F32)).astype(BF)
            count = near.shape[0] // 2
            self.kept, self.got = near[:count], near[count:]
            self.start()

    def end(self):
        if self.parts != 8:
            return self.kept
        return (self.kept[0].astype(F32) + self.got[0].astype(F32)).astype(BF)


def root_moves(reach):
    holders = {2: lambda d: d == 0, 1: lambda d: d in (0, 2)}[reach]
    moves = []
    for z in range(4):
        for x in range(2):
            for k in range(4):
                if holders(z ^ k):
                    moves.append(((2 * z + x) * 4 + k, (2 * (z ^ reach) + x) * 4 + k))
    return moves


def at_root():
    return lax.axis_index("pb") // 2 == lax.axis_index("ka")


class OutSpread:
    def __init__(self, w_out):
        self.parts, ka = lax.axis_size("pb"), lax.axis_size("ka")
        self.span, self.size = self.parts // ka, w_out.shape[0]
        if self.parts != 8:
            self.size = w_out.shape[0] // ka
            own = lax.dynamic_slice_in_dim(w_out, lax.axis_index("ka") * self.size, self.size, 0)
            pad = jnp.zeros((slot_of(self.size) - self.size, w_out.shape[2]), BF)
            x = jnp.concatenate([own[:, 0], pad, own[:, 1], pad], axis=0)
            x = lax.ppermute(x, ("pb", "ka"), row_moves(self.parts, ka))
            self.kept, self.got = x, gather_rows(x)
        else:
            x = jnp.concatenate([w_out[:, 0], w_out[:, 1]], axis=0)
            self.kept = jnp.where(at_root(), x, jnp.zeros_like(x))
            self.got = lax.ppermute(x, ("pb", "ka"), root_moves(2))
            self.next = [1, 0]

    def pending(self):
        return [self.kept, self.got]

    def resume(self, arrays):
        self.kept, self.got = arrays

    def step(self):
        if self.parts == 8:
            self.kept = self.kept + self.got
            reach = self.next.pop(0)
            self.got = lax.ppermute(self.kept, ("pb", "ka"), root_moves(reach)) if reach else swap(self.kept, "pb", 1)

    def rows(self, l):
        if self.parts != 8:
            return whole_rows(self.got, self.parts, l * slot_of(self.size), self.size, self.span)
        return Rows(self.pending(), [(0, l * self.size, 0, True), (1, l * self.size, 1, True)], self.size, -1)


class OutFlow:
    def __init__(self, info, pairs):
        self.parts = lax.axis_size("pb")
        if self.parts != 8:
            self.flow = Flow(info, [([(a, 0, b, 0, a.shape[0])], self.parts // lax.axis_size("ka")) for a, b in pairs])
            self.size = pairs[0][0].shape[1] // self.parts
            self.kept = self.got = self.flow.end()
            self.made = self.flow.made
        else:
            sent, self.kept = outer_pair(info, pairs)
            self.made = self.kept
            self.got = swap(sent, "pb", 1)
            self.next = [1, 2]

    def pending(self):
        return [self.kept, self.got]

    def resume(self, arrays):
        self.kept, self.got = arrays

    def add(self):
        return (self.kept.astype(F32) + self.got.astype(F32)).astype(BF)

    def step(self):
        if self.parts == 8:
            self.kept = self.add()
            moves = [(b, a) for a, b in root_moves(self.next.pop(0))]
            self.got = lax.ppermute(self.kept, ("pb", "ka"), moves)

    def turn(self):
        if self.parts == 8:
            near = self.add()
            self.kept = jnp.where(at_root(), near, jnp.zeros_like(near))
            self.got = lax.ppermute(near, ("pb", "ka"), [(p * 4 + p // 2, p * 4 + (p // 2 ^ 2)) for p in range(8)])

    def cross(self):
        if self.parts == 8:
            self.kept = self.kept + self.got
            moves = [(p * 4 + k, p * 4 + (k ^ 1)) for p in range(8) for k in (p // 2, p // 2 ^ 2)]
            self.got = lax.ppermute(self.kept, ("pb", "ka"), moves)

    def end(self):
        ka, slot = lax.axis_size("ka"), slot_of(self.size)
        back = [(b, a) for a, b in row_moves(self.parts, ka)]
        x = lax.all_gather(lax.ppermute(self.kept, ("pb", "ka"), back), "ka")
        return [x[:, i * slot : i * slot + self.size].reshape(ka * self.size, -1) for i in range(2)]


def pair_gather(x):
    groups = [[i, i + 1] for i in range(0, lax.axis_size("ka"), 2)]
    return lax.all_gather(x, "ka", axis_index_groups=groups)


def core_pieces(x, far):
    return swap(jnp.stack([x, far]), "ka", 1)


def in_order(own, far, core):
    me = lax.axis_index("ka")
    near = [own, core[0], far, core[1]]
    found = []
    for k in range(4):
        value = near[3]
        for n in range(3):
            value = jnp.where((me ^ k) == n, near[n], value)
        found.append(value)
    return found


def on_device(tokens, cotangent, lengths, keep_mask, w_qkv, w_out, w_fc, w_proj, norm_gain, norm_bias):
    rows, width = tokens.shape
    pb = lax.axis_size("pb")
    ka = lax.axis_size("ka")
    me = lax.axis_index("ka")
    low, high = me % 2, me // 2
    heads = H // ka
    part = width // ka
    ff = w_fc.shape[2]
    ff_part = ff // ka
    d_rows = w_qkv.shape[0]
    proj_rows = w_proj.shape[0] // ka
    wide = (3 * part + 8 + 127) // 128 * 128
    bounds = jnp.cumsum(lengths[0])
    info = jnp.concatenate([jnp.stack([lax.axis_index("pb"), low]).astype(jnp.int32), bounds.astype(jnp.int32)])

    half, group = 2 * rows, 4 * rows

    def own_half(x, far):
        return jnp.where(high == 0, jnp.concatenate([x, far], axis=0), jnp.concatenate([far, x], axis=0))

    def block(half, which):
        return lax.dynamic_slice_in_dim(half, which * rows, rows, 0)

    def from_pair(sent):
        return lax.dynamic_index_in_dim(pair_gather(sent), 1 - low, 0, False)

    def add_low(kept, got):
        return (kept + got.astype(F32)).astype(BF)

    picked = jnp.concatenate([lax.dynamic_slice_in_dim(w_qkv, i * width + me * part, part, 2) for i in range(3)], axis=2)
    vectors = jnp.concatenate([norm_gain, norm_bias], axis=1)
    first = jnp.concatenate([picked[:, 0], vectors, jnp.zeros((d_rows, wide - 3 * part - 8), BF)], axis=1)
    outs = OutSpread(w_out)
    qkv0 = Spread(first, True)
    keep_rows = jnp.pad(keep_mask.astype(BF)[None, :], ((0, 15), (0, width - rows)))
    tokens_more = jnp.concatenate([tokens, keep_rows], axis=0)
    far_tokens = swap(tokens_more, "ka", 2)
    tokens_more = own_half(tokens_more, far_tokens)
    first, tokens_more, w_fc, w_proj, picked = tick(first, tokens_more, w_fc, w_proj, picked)
    tokens_both = pair_gather(tokens_more)
    tokens_own = own_half(tokens, far_tokens[:rows])
    unit = ff_part // pb
    local_fc = jnp.concatenate(
        [lax.dynamic_slice_in_dim(w_fc, (q * ka + me) * unit, unit, 2) for q in range(pb)], axis=2
    )
    fc_first, fc_second = local_fc[:, 0], local_fc[:, 1]
    local_proj = lax.dynamic_slice_in_dim(w_proj, me * proj_rows, proj_rows, 0)
    proj_first, proj_late = local_proj[:, 0], local_proj[:, 1]
    second = jnp.concatenate([picked[:, 1], jnp.zeros((d_rows, wide - 3 * part), BF)], axis=1)
    tokens_both, fc_first, proj_first, second, cotangent, proj_late = tick(
        qkv0, outs, tokens_both, fc_first, proj_first, second, cotangent, proj_late
    )
    qkv0.step()
    outs.step()
    proj0 = Spread(proj_first)
    fc0_all = gather_rows(fc_first)
    tokens_both, cotangent, second, fc_second, proj_late = tick(
        qkv0, outs, proj0, tokens_both, cotangent, second, fc_second, proj_late
    )
    outs.step()
    proj0.step()
    qkv1 = Spread(second)
    far_cotangent = swap(cotangent, "ka", 2)
    qkv = [qkv0.rows(), None]

    keys = ("stream", "x", "projected", "attended", "lse", "middle", "both", "hidden", "active")
    got = attention_forward(True, True, info, group, None, tokens_both, qkv[0], part, heads)
    x_all, projected, attended, lse, tokens_all, vec, kept_all = got
    attended, proj_late = tick(attended, outs, proj_late)
    proj1_all = gather_rows(proj_late)
    out = [outs.rows(0), outs.rows(1)]
    sent, kept = attention_out(info, attended, out[0])
    got, fc_second, far_cotangent = tick(from_pair(sent), proj0, qkv1, fc_second, far_cotangent)
    near = add_low(kept, got)
    far = swap(near, "ka", 2)
    proj0.step()
    qkv1.step()
    fc1 = Spread(fc_second)
    branch = own_half(cotangent, far_cotangent)
    middle, own = norm_after(1, tokens_own, near, far, vec)
    both = pair_gather(own)
    fc = [whole_rows(fc0_all, pb, 0, d_rows), None]
    proj = [proj0.rows(), whole_rows(proj1_all, pb, 0, proj_rows)]
    hidden, active, sent, kept = feed_forward(info, both, fc[0], proj[0])
    kept0 = dict(zip(keys, (tokens_own, x_all, projected, attended, lse, middle, both, hidden, active)))
    got, branch_own = tick(from_pair(sent), qkv1, fc1, branch)
    near = add_low(kept, got)
    far = swap(near, "ka", 2)
    fc1.step()
    qkv1.step()
    branch = pair_gather(branch_own)
    qkv[1] = qkv1.rows()
    far, branch = tick(far, branch)
    stream, own = norm_after(2, middle, near, far, vec)
    both = pair_gather(own)
    x_all, projected, attended, lse = attention_forward(False, False, info, group, kept_all, both, qkv[1], part, heads)
    sent, kept = attention_out(info, attended, out[1])
    (got,) = tick(from_pair(sent), fc1)
    near = add_low(kept, got)
    far = swap(near, "ka", 2)
    fc1.step()
    fc[1] = fc1.rows()
    middle, own = norm_after(3, stream, near, far, vec)
    both = pair_gather(own)
    hidden, active, last_sent, last_kept = feed_forward(info, both, fc[1], proj[1])
    kept1 = dict(zip(keys, (stream, x_all, projected, attended, lse, middle, both, hidden, active)))

    sums = [None] * 4

    def fc_pair(kept, grad_hidden):
        return [(kept["both"].reshape(group, width), 0, grad_hidden, 0, group)], 0

    def proj_pair(kept, branch):
        return [(kept["active"], 0, branch.reshape(group, width), 0, group)], 0

    def qkv_pair(kept, grad_projected, more=()):
        return [(kept["x"], 0, grad_projected, 0, group), *more], 0

    def attend_back(l, kept, both):
        return attention_backward(
            l == 0, l == 0, info, kept_all, both, kept["projected"], kept["lse"], qkv[l], out[l], tokens_all, heads
        )

    grad_hidden, sent, kept = feed_backward(info, branch, kept1["hidden"], fc[1], proj[1])
    near = add_low(kept, from_pair(sent))
    far = swap(near, "ka", 2)
    near_in, grad_hidden, branch, last_sent, last_kept = tick(near, grad_hidden, branch, last_sent, last_kept)
    last = add_low(last_kept, from_pair(last_sent))
    flow_a = Flow(info, [fc_pair(kept1, grad_hidden)]).start()
    flow_p = Flow(info, [proj_pair(kept1, branch)], (2, 4, 1)).start()
    far, last, *unused = tick(far, last, flow_a.made, flow_p.made)
    last_far = swap(block(last, 1 - high), "ka", 2)
    grad, own, sums[3] = norm_back(3, branch_own, near, far, kept1["middle"], vec)
    both = pair_gather(own)
    middle_one, grad_projected, sent, kept = attend_back(1, kept1, both)
    got, last, last_far = tick(from_pair(sent), last, last_far, flow_a, flow_p)
    near = add_low(kept, got)
    far = swap(near, "ka", 2)
    near_in, grad_projected = tick(near, grad_projected)
    flow_b = Flow(info, [qkv_pair(kept1, grad_projected)]).start()
    flow_a.step()
    flow_p.step()
    output = (block(kept1["middle"], high) + (block(last, high).astype(F32) + last_far.astype(F32))).astype(BF)
    far, output, unused = tick(far, output, flow_b.made)
    grad, own, sums[2] = norm_back(2, grad, near, far, kept1["stream"], vec)
    branch = pair_gather(own)
    grad_hidden, sent, kept = feed_backward(info, branch, kept0["hidden"], fc[0], proj[0])
    (got,) = tick(from_pair(sent), flow_a, flow_p, flow_b)
    near = add_low(kept, got)
    far = swap(near, "ka", 2)
    near_in, grad_hidden, branch = tick(near, grad_hidden, branch)
    flow_c = Flow(info, [fc_pair(kept0, grad_hidden)]).start()
    flow_q = Flow(info, [proj_pair(kept0, branch)], (2, 4, 1)).start()
    tick(flow_a, flow_p, flow_c.made, flow_q.made)
    flow_a.step()
    flow_p.step()
    (far,) = tick(far, flow_c.made, flow_q.made)[:1]
    grad, own, sums[1] = norm_back(1, grad, near, far, kept0["middle"], vec)
    both = pair_gather(own)
    middle_all, grad_projected, sent, kept, sums[0] = attend_back(0, kept0, both)
    (got,) = tick(from_pair(sent), flow_a, flow_p, flow_b, flow_c, flow_q)
    near = add_low(kept, got)
    far = swap(block(near, 1 - high), "ka", 2)
    near_in, grad_projected, middle_all = tick(near, grad_projected, middle_all)
    halved = [sums[0]] + [0.5 * s for s in sums[1:]]
    stacked = jnp.concatenate([s[i : i + 1] for i in range(2) for s in halved] + [jnp.zeros((8, width), F32)], axis=0).astype(BF)
    spots = (3 * part + jnp.arange(16)[:, None] == jnp.arange(wide)[None, :]) & (jnp.arange(16)[:, None] < 8)
    flow_d = Flow(info, [qkv_pair(kept0, grad_projected, [(stacked, 0, spots.astype(BF), 0, 16)])]).start()
    flow_b.step()
    flow_c.step()
    flow_q.step()
    after_fc = slot_of(d_rows)
    far, unused = tick(far, flow_d.made)
    (grad_tokens,) = norm_back(0, block(grad, high), block(near, high), far, block(kept0["stream"], high), vec, True)

    middle_all, grad_tokens = tick(flow_b, flow_c, flow_q, flow_d, middle_all, grad_tokens)
    flow_d.step()
    flow_o = OutFlow(info, [(kept0["attended"], middle_all), (kept1["attended"], middle_one)])
    flow_c.step()
    flow_q.step()
    flow_b.step()
    done_a = jnp.concatenate([flow_a.end(), flow_p.end()], axis=0)
    tick(flow_d, flow_o)
    flow_d.step()
    flow_o.step()
    (done_a,) = tick(flow_b, flow_c, flow_q, done_a)
    far_a = swap(done_a, "ka", 2)
    done_b = flow_b.end()
    far_b = swap(done_b, "ka", 2)
    done_c = jnp.concatenate([flow_c.end(), flow_q.end()], axis=0)
    far_c = swap(done_c, "ka", 2)
    far_a, far_b = tick(flow_d, flow_o, far_a, far_b)
    done_d = flow_d.end()
    far_d = swap(done_d, "ka", 2)
    flow_o.step()
    far_d, far_c = tick(far_d, flow_o, far_c)
    core_ac = swap(jnp.stack([done_a, far_a, done_c, far_c]), "ka", 1)
    core_bd = swap(jnp.stack([done_b, far_b, done_d, far_d]), "ka", 1)
    flow_o.turn()
    core_ac, core_bd = tick(core_ac, core_bd, flow_o)
    core_a, core_c, core_b, core_d = core_ac[:2], core_ac[2:], core_bd[:2], core_bd[2:]
    flow_o.cross()
    block_a, block_b, block_c, block_d = [
        (done_a, far_a, core_a),
        (done_b, far_b, core_b),
        (done_c, far_c, core_c),
        (done_d, far_d, core_d),
    ]
    if pb == 8:
        rank = me.astype(jnp.int32).reshape(1)
        sum_fc, sum_proj = finish_feed(rank, (block_c, block_a), after_fc, unit, d_rows, proj_rows)
        sum_qkv, stacked = finish_attend(rank, (block_d, block_b), part)
        (sum_out,) = finish_out(flow_o.kept, flow_o.got)
        return (output, grad_tokens, sum_qkv, sum_out, sum_fc, sum_proj, stacked[:4].T, stacked[4:].T)

    def pair(one, other):
        return jnp.stack([one, other], axis=1).astype(F32)

    def columns(pieces):
        return jnp.stack([p[:d_rows].reshape(d_rows, pb, unit) for p in pieces], axis=2).reshape(d_rows, ff)

    def heads_of(pieces):
        return jnp.concatenate([p[:d_rows, i * part : (i + 1) * part] for i in range(3) for p in pieces], axis=1)

    def rows_of(pieces):
        return jnp.concatenate([p[after_fc : after_fc + proj_rows] for p in pieces], axis=0)

    a, b, c, d = [in_order(*pieces) for pieces in (block_a, block_b, block_c, block_d)]
    stacked = sum(p[:d_rows, 3 * part : 3 * part + 8].astype(F32) for p in d)
    return (
        output,
        grad_tokens,
        pair(heads_of(d), heads_of(b)),
        pair(*flow_o.end()),
        pair(columns(c), columns(a)),
        pair(rows_of(c), rows_of(a)),
        stacked[:, :4],
        stacked[:, 4:],
    )


def solution(mesh):
    return jax.shard_map(
        on_device,
        mesh=mesh,
        in_specs=(
            P(("pb", "ka"), None),
            P(("pb", "ka"), None),
            P("pb", None),
            P(("pb", "ka")),
            P("pb", None, None),
            P("pb", None, None),
            P("pb", None, None),
            P("pb", None, None),
            P("pb", None),
            P("pb", None),
        ),
        out_specs=(
            P(("pb", "ka"), None),
            P(("pb", "ka"), None),
            P("pb", None, None),
            P("pb", None, None),
            P("pb", None, None),
            P("pb", None, None),
            P("pb", None),
            P("pb", None),
        ),
        check_vma=False,
    )
```

```python
import functools
import jax
import jax.numpy as jnp
from jax import lax
from jax.experimental import pallas as pl
from jax.experimental.pallas import tpu as pltpu
from jax.sharding import PartitionSpec as P

H = 12
EPSILON = 1e-05
FLOOR_VALUE = -1e30
BF = jnp.bfloat16
F32 = jnp.float32
VM = pl.BlockSpec(memory_space=pltpu.VMEM)
SM = pl.BlockSpec(memory_space=pltpu.SMEM)
SHIFTS = (0, 4, 2, 6)
GELU_A = 0.7978845608028654
GELU_B = 0.044715


def dot(a, b, ca, cb):
    return lax.dot_general(a, b, (((ca,), (cb,)), ((), ())), preferred_element_type=F32)


def call(kernel, outs, ins, scratch=(), flops=0, name=None):
    moved = sum(a.size * a.dtype.itemsize for a in ins)
    return pl.pallas_call(
        kernel,
        out_shape=[jax.ShapeDtypeStruct(s, t) for s, t in outs],
        in_specs=[SM if a.dtype == jnp.int32 and a.ndim == 1 else VM for a in ins],
        out_specs=[VM] * len(outs),
        scratch_shapes=list(scratch),
        compiler_params=pltpu.CompilerParams(vmem_limit_bytes=20 * 1024 * 1024),
        cost_estimate=pl.CostEstimate(flops=flops, bytes_accessed=moved, transcendentals=0),
        name=name,
    )(*ins)


def at(index, rows):
    return pl.ds(pl.multiple_of(index * rows, rows), rows)


class Rows:
    def __init__(self, arrays, plan, size, span=0):
        self.arrays, self.plan, self.size, self.span = arrays, plan, size, span
        self.shape = (size * len(plan), arrays[0].shape[1])

    def scratch(self):
        return pltpu.VMEM(self.shape, F32 if self.size % 16 else BF)

    def take(self, refs, scratch, me):
        if len(self.arrays) == 1 and not self.span and self.plan == [(0, p * self.size, p, False) for p in range(len(self.plan))]:
            return refs[0]
        self.load(refs, scratch, me)
        return scratch

    def load(self, refs, scratch, me):
        for index, start, p, relative in self.plan:
            place = me ^ p if relative else p
            if self.span < 0:
                place = place & (len(self.plan) - 1)
            elif self.span:
                place = place_of(place, self.span, len(self.plan) // self.span)
            target = at(place, self.size) if relative else slice(place * self.size, (place + 1) * self.size)
            scratch[target, :] = refs[index][start : start + self.size, :].astype(scratch.dtype)


def place_of(p, span, ka):
    return (p % span) * ka + p // span if isinstance(p, int) else lax.rem(p, span) * ka + lax.div(p, span)


def take_refs(refs, *weights):
    return [[refs.pop(0) for unused in w.arrays] for w in weights]


def norm_parts(values):
    average = jnp.mean(values, axis=-1, keepdims=True)
    centered = values - average
    spread = jnp.mean(centered * centered, axis=-1, keepdims=True)
    inverse = lax.rsqrt(spread + EPSILON)
    return centered * inverse, inverse


def block_allowed(info, kept_ref, b, block, keys):
    i = b * block + lax.broadcasted_iota(jnp.int32, (1, block), 1)
    j = lax.broadcasted_iota(jnp.int32, (keys, 1), 0)

    def segment(t):
        total = jnp.zeros_like(t)
        for n in range(2, info.shape[0]):
            total = total + jnp.where(t >= info[n], 1, 0)
        return total

    same = segment(i) == segment(j)
    itself = i == j
    return same & (j <= i) & ((kept_ref[:keys, :] > 0) | itself)


def canonical(both, full):
    block, stride = full.shape[0] // 4, both.shape[1] // 2
    for h in range(2):
        for i in range(2):
            full[(2 * i + h) * block : (2 * i + h + 1) * block, :] = both[h, i * stride : i * stride + block, :]


def split_halves(low, full, kept, sent):
    block = kept.shape[0] // 2
    for i in range(2):
        kept[i * block : (i + 1) * block, :] = full[at(2 * i + low, block), :].astype(kept.dtype)
        sent[i * block : (i + 1) * block, :] = full[at(2 * i + 1 - low, block), :].astype(sent.dtype)


def attention_forward_kernel(first, signed, qkv, heads, *refs):
    refs = list(refs)
    info = refs.pop(0)
    if not first:
        kept_ref = refs.pop(0)
    both = refs.pop(0)
    (pieces,) = take_refs(refs, qkv)
    x_ref, proj_ref, att_ref, lse_ref = [refs.pop(0) for unused in range(4)]
    if first:
        tokens, vec_ref, kept_ref = refs.pop(0), refs.pop(0), refs.pop(0)
    (w,) = refs
    me, low = info[0], info[1]
    qkv.load(pieces, w, me)
    part = att_ref.shape[1]
    hd = part // heads
    group, width = x_ref.shape
    block = group // 4
    if first:
        tail = w.shape[1] - 3 * part
        pick = lax.broadcasted_iota(jnp.int32, (8, tail), 0) == lax.broadcasted_iota(jnp.int32, (8, tail), 1)
        vec = dot(pick.astype(F32).astype(BF), w[:, 3 * part :], 1, 1)
        vec_ref[...] = vec
        canonical(both, tokens)
        stride = both.shape[1] // 2
        for h in range(2):
            for i in range(2):
                row = both[h, i * stride + block : i * stride + block + 1, :block].astype(F32)
                kept_ref[(2 * i + h) * block : (2 * i + h + 1) * block, :] = jnp.transpose(jnp.broadcast_to(row, (8, block)))[:, :1]
        for b in range(4):
            values = tokens[b * block : (b + 1) * block, :].astype(F32)
            normal, unused = norm_parts(values)
            x_ref[b * block : (b + 1) * block, :] = (normal * vec[0:1] + vec[4:5]).astype(BF)
    else:
        canonical(both, x_ref)
    proj_ref[...] = dot(x_ref[...], w[...], 1, 0).astype(BF)
    scale = hd ** (-0.5)
    for b in range(4):
        keys = (b + 1) * block
        rows = slice(b * block, keys)
        allowed = block_allowed(info, kept_ref, b, block, keys)
        each = range(heads)
        q = [proj_ref[rows, h * hd : (h + 1) * hd] * scale for h in each]
        k = [proj_ref[:keys, part + h * hd : part + (h + 1) * hd] for h in each]
        v = [proj_ref[:keys, 2 * part + h * hd : 2 * part + (h + 1) * hd] for h in each]
        scores = [dot(k[h], q[h], 1, 1) for h in each]
        masked = [jnp.where(allowed, jnp.abs(s) if signed else s, FLOOR_VALUE) for s in scores]
        peak = [jnp.max(m, axis=0, keepdims=True) for m in masked]
        raised = [jnp.exp(masked[h] - peak[h]) for h in each]
        total = [jnp.sum(r, axis=0, keepdims=True) for r in raised]
        if signed:
            lifted = [jnp.where(allowed, raised[h] - jnp.exp(-peak[h]), 0.0) for h in each]
            raised = [jnp.where(scores[h] < 0, -lifted[h], lifted[h]) for h in each]
        weights = [(raised[h] * (1.0 / total[h])).astype(BF) for h in each]
        values = [dot(v[h], weights[h], 0, 0) for h in each]
        for h in each:
            att_ref[rows, h * hd : (h + 1) * hd] = jnp.transpose(values[h]).astype(BF)
            lse_ref[h : h + 1, rows] = peak[h] + jnp.log(total[h])


def attention_forward(first, signed, info, group, kept, both, qkv, part, heads):
    width = both.shape[2]
    outs = [((group, width), BF), ((group, qkv.shape[1]), BF), ((group, part), BF), ((8, group), F32)]
    if first:
        outs += [((group, width), BF), ((8, width), F32), ((group, 1), F32)]
    return call(
        functools.partial(attention_forward_kernel, first, signed, qkv, heads),
        outs,
        [info] + ([] if first else [kept]) + [both, *qkv.arrays],
        [qkv.scratch()],
        flops=2 * group * width * 3 * part,
        name="attend",
    )


def attention_out_kernel(out, *refs):
    refs = list(refs)
    info, attended = refs.pop(0), refs.pop(0)
    (pieces,) = take_refs(refs, out)
    sent, kept, w_out, partial = refs
    out.load(pieces, w_out, info[0])
    partial[...] = dot(attended[...], w_out[...].astype(BF), 1, 0)
    split_halves(info[1], partial, kept, sent)


def attention_out(info, attended, out):
    group, width = attended.shape[0], out.shape[1]
    return call(
        functools.partial(attention_out_kernel, out),
        [((group // 2, width), BF), ((group // 2, width), F32)],
        [info, attended, *out.arrays],
        [out.scratch(), pltpu.VMEM((group, width), F32)],
        flops=2 * group * width * out.shape[0],
        name="attend_out",
    )


def gelu_parts(v):
    inner = GELU_A * (v + GELU_B * v * v * v)
    return jnp.tanh(inner)


def feed_forward_kernel(fc, proj, *refs):
    refs = list(refs)
    info, both = [refs.pop(0) for unused in range(2)]
    fc_refs, proj_refs = take_refs(refs, fc, proj)
    hidden, active, sent, kept, w, w_proj, partial = refs
    w = fc.take(fc_refs, w, info[0])
    w_proj = proj.take(proj_refs, w_proj, info[0])
    half = both.shape[1]
    ff = w_proj.shape[0]
    step = ff // 3
    parts = [(h, f) for f in range(3) for h in range(2)]
    hids = [dot(both[h], w[:, f * step : (f + 1) * step], 1, 0) for h, f in parts]
    acts = [(0.5 * v * (1.0 + gelu_parts(v))).astype(BF) for v in hids]
    for (h, f), hid, act in zip(parts, hids, acts):
        rows, cols = slice(h * half, (h + 1) * half), slice(f * step, (f + 1) * step)
        hidden[rows, cols] = hid
        active[rows, cols] = act
    for h in range(2):
        partial[h] = dot(active[h * half : (h + 1) * half, :], w_proj[...], 1, 0)
    kept[...] = partial[info[1]]
    sent[...] = partial[1 - info[1]].astype(BF)


def feed_forward(info, both, fc, proj):
    two, half, width = both.shape
    ff = proj.shape[0]
    outs = [((2 * half, ff), F32), ((2 * half, ff), BF), ((half, width), BF), ((half, width), F32)]
    return call(
        functools.partial(feed_forward_kernel, fc, proj),
        outs,
        [info, both, *fc.arrays, *proj.arrays],
        [fc.scratch(), proj.scratch(), pltpu.VMEM((2, half, width), F32)],
        flops=8 * half * width * ff,
        name="feed",
    )


def norm_kernel(row, stream, near, far, vec, middle, normed):
    values = stream[...].astype(F32) + (near[...].astype(F32) + far[...].astype(F32))
    middle[...] = values
    normal, unused = norm_parts(values)
    normed[...] = (normal * vec[row : row + 1, :] + vec[row + 4 : row + 5, :]).astype(BF)


def norm_after(row, stream, near, far, vec):
    shape = stream.shape
    return call(functools.partial(norm_kernel, row), [(shape, F32), (shape, BF)], [stream, near, far, vec], name="norm")


def feed_backward_kernel(fc, proj, *refs):
    refs = list(refs)
    info, both, hidden = [refs.pop(0) for unused in range(3)]
    fc_refs, proj_refs = take_refs(refs, fc, proj)
    grad_hidden, sent, kept, w, w_proj, partial = refs
    w = fc.take(fc_refs, w, info[0])
    w_proj = proj.take(proj_refs, w_proj, info[0])
    half = both.shape[1]
    ff = w_proj.shape[0]
    step = ff // 3
    for f in range(3):
        cols = slice(f * step, (f + 1) * step)
        for h in range(2):
            rows = slice(h * half, (h + 1) * half)
            grad_active = dot(both[h], w_proj[cols, :], 1, 1)
            v = hidden[rows, cols]
            t = gelu_parts(v)
            slope = 0.5 * (1.0 + t) + 0.5 * v * (1.0 - t * t) * (GELU_A * (1.0 + 3.0 * GELU_B * v * v))
            grad_hidden[rows, cols] = (slope * grad_active).astype(BF)
    for h in range(2):
        partial[h] = dot(grad_hidden[h * half : (h + 1) * half, :], w[...], 1, 1)
    kept[...] = partial[info[1]]
    sent[...] = partial[1 - info[1]].astype(BF)


def feed_backward(info, both, hidden, fc, proj):
    two, half, width = both.shape
    ff = proj.shape[0]
    outs = [((2 * half, ff), BF), ((half, width), BF), ((half, width), F32)]
    return call(
        functools.partial(feed_backward_kernel, fc, proj),
        outs,
        [info, both, hidden, *fc.arrays, *proj.arrays],
        [fc.scratch(), proj.scratch(), pltpu.VMEM((2, half, width), F32)],
        flops=8 * half * width * ff,
        name="feed_back",
    )


def norm_backward_kernel(row, grad, near, far, source, vec, out, *rest):
    incoming = near[...].astype(F32) + far[...].astype(F32)
    normal, inverse = norm_parts(source[...].astype(F32))
    grad_normal = incoming * vec[row : row + 1, :]
    mean_grad = jnp.mean(grad_normal, axis=-1, keepdims=True)
    mean_cross = jnp.mean(grad_normal * normal, axis=-1, keepdims=True)
    value = grad[...].astype(F32) + inverse * (grad_normal - mean_grad - normal * mean_cross)
    out[...] = value
    if not rest:
        return
    low, sums = rest
    low[...] = value.astype(BF)
    sums[0:1, :] = jnp.sum(incoming * normal, axis=0, keepdims=True)
    sums[1:2, :] = jnp.sum(incoming, axis=0, keepdims=True)


def norm_back(row, grad, near, far, source, vec, last=False):
    shape = source.shape
    return call(
        functools.partial(norm_backward_kernel, row),
        [(shape, F32)] if last else [(shape, F32), (shape, BF), ((2, shape[1]), F32)],
        [grad, near, far, source, vec],
        name="norm_back",
    )


def attention_backward_kernel(first, signed, qkv, out, heads, *refs):
    refs = list(refs)
    info, kept_ref, both, proj, lse = [refs.pop(0) for unused in range(5)]
    pieces, out_pieces = take_refs(refs, qkv, out)
    if first:
        tokens = refs.pop(0)
    gm_ref, gp_ref, sent, kept = [refs.pop(0) for unused in range(4)]
    if first:
        sums = refs.pop(0)
    w, w_out, partial, gatt, gk_sum, gv_sum = refs
    me, low = info[0], info[1]
    qkv.load(pieces, w, me)
    out.load(out_pieces, w_out, me)
    part = w_out.shape[0]
    hd = part // heads
    group = gm_ref.shape[0]
    block = group // 4
    canonical(both, gm_ref)
    gatt[...] = dot(gm_ref[...], w_out[...].astype(BF), 1, 1).astype(BF)
    scale = hd ** (-0.5)
    gp_ref[:, 3 * part :] = jnp.zeros((group, gp_ref.shape[1] - 3 * part), BF)
    for b in reversed(range(4)):
        keys = (b + 1) * block
        rows = slice(b * block, keys)
        allowed = block_allowed(info, kept_ref, b, block, keys)
        each = range(heads)
        q = [proj[rows, h * hd : (h + 1) * hd] * scale for h in each]
        k = [proj[:keys, part + h * hd : part + (h + 1) * hd] for h in each]
        v = [proj[:keys, 2 * part + h * hd : 2 * part + (h + 1) * hd] for h in each]
        g = [gatt[rows, h * hd : (h + 1) * hd] for h in each]
        level = [lse[h : h + 1, rows] for h in each]
        scores = [dot(k[h], q[h], 1, 1) for h in each]
        grad_weights = [dot(v[h], g[h], 1, 1) for h in each]
        absolute = [jnp.exp(jnp.where(allowed, jnp.abs(scores[h]) if signed else scores[h], FLOOR_VALUE) - level[h]) for h in each]
        if signed:
            lifted = [jnp.where(allowed, absolute[h] - jnp.exp(-level[h]), 0.0) for h in each]
            weights = [jnp.where(scores[h] < 0, -lifted[h], lifted[h]) for h in each]
        else:
            weights = absolute
        shift = [jnp.sum(grad_weights[h] * weights[h], axis=0, keepdims=True) for h in each]
        if signed:
            shift = [jnp.where(scores[h] > 0, shift[h], jnp.where(scores[h] < 0, -shift[h], 0.0)) for h in each]
        gs = [(absolute[h] * (grad_weights[h] - shift[h])).astype(BF) for h in each]
        gv = [dot(weights[h].astype(BF), g[h], 1, 0) for h in each]
        gk = [dot(gs[h], q[h], 1, 0) for h in each]
        gq = [dot(k[h], gs[h], 0, 0) for h in each]
        for h in each:
            gp_ref[rows, h * hd : (h + 1) * hd] = jnp.transpose(gq[h] * scale).astype(BF)
            if b == 3:
                gk_sum[h] = gk[h]
                gv_sum[h] = gv[h]
            else:
                gk_sum[h, :keys] += gk[h]
                gv_sum[h, :keys] += gv[h]
    for h in range(heads):
        gp_ref[:, part + h * hd : part + (h + 1) * hd] = gk_sum[h].astype(BF)
        gp_ref[:, 2 * part + h * hd : 2 * part + (h + 1) * hd] = gv_sum[h].astype(BF)
    partial[...] = dot(gp_ref[...], w[...], 1, 1)
    split_halves(low, partial, kept, sent)
    if first:
        gain = bias = 0.0
        for b in range(4):
            rows = slice(b * block, (b + 1) * block)
            normal, unused = norm_parts(tokens[rows, :].astype(F32))
            value = partial[rows, :]
            gain = gain + jnp.sum(value * normal, axis=0, keepdims=True)
            bias = bias + jnp.sum(value, axis=0, keepdims=True)
        sums[0:1, :] = gain
        sums[1:2, :] = bias


def attention_backward(first, signed, info, kept, both, proj, lse, qkv, out, tokens, heads):
    two, half, width = both.shape
    group = 2 * half
    part = out.shape[0]
    wide = qkv.shape[1]
    outs = [((group, width), BF), ((group, wide), BF), ((half, width), BF), ((half, width), F32)]
    if first:
        outs += [((2, width), F32)]
    return call(
        functools.partial(attention_backward_kernel, first, signed, qkv, out, heads),
        outs,
        [info, kept, both, proj, lse, *qkv.arrays, *out.arrays] + ([tokens] if first else []),
        [
            qkv.scratch(),
            out.scratch(),
            pltpu.VMEM((group, width), F32),
            pltpu.VMEM((group, part), BF),
            pltpu.VMEM((heads, group, part // heads), F32),
            pltpu.VMEM((heads, group, part // heads), F32),
        ],
        flops=2 * group * width * 4 * part,
        name="attend_back",
    )


def outer_kernel(parts, plans, bits, *refs):
    info, scratch = refs[0], refs[-1]
    outs = refs[-3:-1] if bits else refs[-2:-1]
    shifts = halving(bits)
    start = 0
    for segments, rows, slot, span, cols in plans:
        size = rows // parts
        blank = scratch.shape[1] - cols

        def place(p):
            return place_of(p, span, parts // span) if span else p

        total = None
        for left, first, right, second, count in segments:
            term = dot(refs[left][first : first + count, :], refs[right][second : second + count, :], 0, 0)
            total = term if total is None else total + term
        scratch[:rows, :cols] = total
        if blank:
            scratch[:rows, cols:] = jnp.zeros((rows, blank), F32)
        for j in range(len(shifts) if bits else parts):
            if bits:
                targets = [at(place(info[0] ^ shifts[j] ^ bits[0]), size), at(place(info[0] ^ shifts[j]), size)]
            else:
                targets = [slice(place(j) * size, (place(j) + 1) * size)]
            for ref, target in zip(outs, targets):
                ref[j, start : start + size, :] = scratch[target, :].astype(BF)
                if slot > size:
                    ref[j, start + size : start + slot, :] = jnp.zeros((slot - size, scratch.shape[1]), BF)
        start += slot


def halving(bits):
    return [0, bits[2], bits[1], bits[1] | bits[2]] if bits else []


def slot_of(size):
    return (size + 15) // 16 * 16


def outer(parts, info, pairs, bits):
    arrays, plans = [info], []

    def number(a):
        for n, other in enumerate(arrays):
            if other is a:
                return n
        arrays.append(a)
        return len(arrays) - 1

    for segments, span in pairs:
        rows = segments[0][0].shape[1]
        numbers = [(number(a), first, number(b), second, count) for a, first, b, second, count in segments]
        plans.append((numbers, rows, slot_of(rows // parts), span, segments[0][2].shape[1]))
    cols = max(p[4] for p in plans)
    tall = sum(p[2] for p in plans)
    outs = [((parts // 2, tall, cols), BF)] * 2 if bits else [((parts, tall, cols), BF)]
    return call(
        functools.partial(outer_kernel, parts, plans, bits),
        outs,
        arrays,
        [pltpu.VMEM((max(p[1] for p in plans), cols), F32)],
        flops=sum(2 * p[1] * cols * sum(seg[4] for seg in p[0]) for p in plans),
        name="outer",
    )


def outer_pair_kernel(count, *refs):
    info, ins, (sent, kept, scratch) = refs[0], refs[1 : 1 + 2 * count], refs[1 + 2 * count :]
    size = scratch.shape[0] // 2
    low = info[0] & 1
    for i in range(count):
        scratch[...] = dot(ins[2 * i][...], ins[2 * i + 1][...], 0, 0)
        kept[i * size : (i + 1) * size, :] = scratch[at(low, size), :].astype(BF)
        sent[i * size : (i + 1) * size, :] = scratch[at(1 - low, size), :].astype(BF)


def outer_pair(info, pairs):
    rows, cols = pairs[0][0].shape[1], pairs[0][1].shape[1]
    shape = (len(pairs) * rows // 2, cols)
    return call(
        functools.partial(outer_pair_kernel, len(pairs)),
        [(shape, BF)] * 2,
        [info] + [a for pair in pairs for a in pair],
        [pltpu.VMEM((rows, cols), F32)],
        flops=len(pairs) * 2 * rows * cols * pairs[0][0].shape[0],
        name="outer",
    )


def piece_refs(refs):
    own, far, core = refs[:3]
    return [own, core.at[0], far, core.at[1]]


def finish_feed_kernel(first, unit, info, *refs):
    w_fc, w_proj, scratch = refs[-3:]
    me = info[0]
    size = w_fc.shape[0]
    rows = w_proj.shape[0] // 4
    for l in range(2):
        pieces = piece_refs(refs[3 * l :])
        values = [p[:size, :] for p in pieces]
        for k in range(4):
            value = values[3]
            for n in range(3):
                value = jnp.where((me ^ k) == n, values[n], value)
            for q in range(value.shape[1] // unit):
                scratch[:, (q * 4 + k) * unit : (q * 4 + k + 1) * unit] = value[:, q * unit : (q + 1) * unit]
        w_fc[:, l, :] = scratch[...].astype(F32)
        for n in range(4):
            w_proj[at(me ^ n, rows), l, :] = pieces[n][first : first + rows, :].astype(F32)


def finish_feed(me, blocks, first, unit, size, rows):
    width = blocks[0][0].shape[1]
    ff = 4 * width
    return call(
        functools.partial(finish_feed_kernel, first, unit),
        [((size, 2, ff), F32), ((4 * rows, 2, width), F32)],
        [me] + [a for block in blocks for a in block],
        [pltpu.VMEM((size, ff), BF)],
        name="finish_feed",
    )


def finish_attend_kernel(part, info, *refs):
    w_qkv, vectors, scratch = refs[6:]
    me = info[0]
    size = w_qkv.shape[0]
    for l in range(2):
        pieces = piece_refs(refs[3 * l :])
        values = [p[...] for p in pieces]
        for k in range(4):
            value = values[3]
            for n in range(3):
                value = jnp.where((me ^ k) == n, values[n], value)
            for i in range(3):
                scratch[:, (i * 4 + k) * part : (i * 4 + k + 1) * part] = value[:, i * part : (i + 1) * part]
        w_qkv[:, l, :] = scratch[...].astype(F32)
        if l == 0:
            tail = values[0].shape[1] - 3 * part
            pick = lax.broadcasted_iota(jnp.int32, (8, tail), 0) == lax.broadcasted_iota(jnp.int32, (8, tail), 1)
            pick = pick.astype(F32).astype(BF)
            total = None
            for value in values:
                term = dot(pick, value[:, 3 * part :], 1, 1)
                total = term if total is None else total + term
            vectors[...] = total


def finish_attend(me, blocks, part):
    size = blocks[0][0].shape[0]
    columns = 12 * part
    return call(
        functools.partial(finish_attend_kernel, part),
        [((size, 2, columns), F32), ((8, size), F32)],
        [me] + [a for block in blocks for a in block],
        [pltpu.VMEM((size, columns), BF)],
        name="finish_attend",
    )


def finish_out_kernel(near, far, w_out):
    size = w_out.shape[0]
    for l in range(2):
        rows = slice(l * size, (l + 1) * size)
        w_out[:, l, :] = near[rows, :].astype(F32) + far[rows, :].astype(F32)


def finish_out(near, far):
    rows, width = near.shape
    return call(finish_out_kernel, [((rows // 2, 2, width), F32)], [near, far], name="finish_out")


def stack_kernel(*refs):
    out = refs[-1]
    start = 0
    for ref in refs[:-1]:
        out[start : start + ref.shape[0], :] = ref[...]
        start += ref.shape[0]


def stack_rows(arrays):
    shape = (sum(a.shape[0] for a in arrays), arrays[0].shape[1])
    return call(stack_kernel, [(shape, BF)], list(arrays), name="stack")[0]


def tick(*items):
    flat = [a for item in items for a in (item.pending() if hasattr(item, "pending") else [item])]
    flat = list(lax.optimization_barrier(tuple(flat)))
    found = []
    for item in items:
        if hasattr(item, "pending"):
            count = len(item.pending())
            item.resume(flat[:count])
            del flat[:count]
        else:
            found.append(flat.pop(0))
    return found


def swap(x, axis, bit):
    size = lax.axis_size(axis)
    return lax.ppermute(x, axis, [(i, i ^ bit) for i in range(size)])


def row_moves(pb, ka):
    span = pb // ka
    return [(p * ka + k, (k * span + p % span) * ka + p // span) for p in range(pb) for k in range(ka)]


def gather_rows(x):
    return lax.all_gather(x, "pb", axis=0, tiled=True)


def whole_rows(x, parts, start, size, span=0):
    piece = x.shape[0] // parts
    return Rows([x], [(0, p * piece + start, p, False) for p in range(parts)], size, span)


class Spread:
    def __init__(self, x, direct=False):
        self.rows_each, self.parts = x.shape[0], lax.axis_size("pb")
        self.bits = [1] if direct else [2, 1]
        if self.parts != 8:
            self.kept, self.got = x, [gather_rows(x)]
        elif direct:
            self.kept, self.got = x, [swap(x, "pb", s) for s in SHIFTS[1:]]
        else:
            self.kept, self.got = x, [swap(x, "pb", 4)]

    def pending(self):
        return [self.kept, *self.got]

    def resume(self, arrays):
        self.kept, *self.got = arrays

    def step(self):
        if self.parts != 8:
            return
        self.kept = stack_rows([self.kept, *self.got])
        self.got = [swap(self.kept, "pb", self.bits.pop(0))]

    def rows(self, first=0, size=None, span=0):
        size = size or self.rows_each
        if self.parts != 8:
            return whole_rows(self.got[0], self.parts, first, size, span)
        each = self.rows_each
        plan = [(n, i * each + first, s + n, True) for n in range(2) for i, s in enumerate(SHIFTS)]
        return Rows(self.pending(), plan, size, span)


class Flow:
    def __init__(self, info, pairs, bits=(1, 2, 4)):
        self.parts = lax.axis_size("pb")
        if self.parts != 8:
            (x,) = outer(self.parts, info, pairs, ())
            self.kept = lax.psum_scatter(x.reshape(-1, x.shape[2]), "pb", scatter_dimension=0, tiled=True)
            self.got = self.kept
            self.made = x
        else:
            self.got, self.kept = outer(self.parts, info, pairs, bits)
            self.made = self.kept
            self.bits = list(bits)

    def pending(self):
        return [self.kept, self.got]

    def resume(self, arrays):
        self.kept, self.got = arrays

    def start(self):
        if self.parts == 8:
            self.got = swap(self.got, "pb", self.bits.pop(0))
        return self

    def step(self):
        if self.parts == 8:
            near = (self.kept.astype(F32) + self.got.astype(F32)).astype(BF)
            count = near.shape[0] // 2
            self.kept, self.got = near[:count], near[count:]
            self.start()

    def end(self):
        if self.parts != 8:
            return self.kept
        return (self.kept[0].astype(F32) + self.got[0].astype(F32)).astype(BF)


def root_moves(reach):
    holders = {2: lambda d: d == 0, 1: lambda d: d in (0, 2)}[reach]
    moves = []
    for z in range(4):
        for x in range(2):
            for k in range(4):
                if holders(z ^ k):
                    moves.append(((2 * z + x) * 4 + k, (2 * (z ^ reach) + x) * 4 + k))
    return moves


def at_root():
    return lax.axis_index("pb") // 2 == lax.axis_index("ka")


class OutSpread:
    def __init__(self, w_out):
        self.parts, ka = lax.axis_size("pb"), lax.axis_size("ka")
        self.span, self.size = self.parts // ka, w_out.shape[0]
        if self.parts != 8:
            self.size = w_out.shape[0] // ka
            own = lax.dynamic_slice_in_dim(w_out, lax.axis_index("ka") * self.size, self.size, 0)
            pad = jnp.zeros((slot_of(self.size) - self.size, w_out.shape[2]), BF)
            x = jnp.concatenate([own[:, 0], pad, own[:, 1], pad], axis=0)
            x = lax.ppermute(x, ("pb", "ka"), row_moves(self.parts, ka))
            self.kept, self.got = x, gather_rows(x)
        else:
            x = jnp.concatenate([w_out[:, 0], w_out[:, 1]], axis=0)
            self.kept = jnp.where(at_root(), x, jnp.zeros_like(x))
            self.got = lax.ppermute(x, ("pb", "ka"), root_moves(2))
            self.next = [1, 0]

    def pending(self):
        return [self.kept, self.got]

    def resume(self, arrays):
        self.kept, self.got = arrays

    def step(self):
        if self.parts == 8:
            self.kept = self.kept + self.got
            reach = self.next.pop(0)
            self.got = lax.ppermute(self.kept, ("pb", "ka"), root_moves(reach)) if reach else swap(self.kept, "pb", 1)

    def rows(self, l):
        if self.parts != 8:
            return whole_rows(self.got, self.parts, l * slot_of(self.size), self.size, self.span)
        return Rows(self.pending(), [(0, l * self.size, 0, True), (1, l * self.size, 1, True)], self.size, -1)


class OutFlow:
    def __init__(self, info, pairs):
        self.parts = lax.axis_size("pb")
        if self.parts != 8:
            self.flow = Flow(info, [([(a, 0, b, 0, a.shape[0])], self.parts // lax.axis_size("ka")) for a, b in pairs])
            self.size = pairs[0][0].shape[1] // self.parts
            self.kept = self.got = self.flow.end()
            self.made = self.flow.made
        else:
            sent, self.kept = outer_pair(info, pairs)
            self.made = self.kept
            self.got = swap(sent, "pb", 1)
            self.next = [1, 2]

    def pending(self):
        return [self.kept, self.got]

    def resume(self, arrays):
        self.kept, self.got = arrays

    def add(self):
        return (self.kept.astype(F32) + self.got.astype(F32)).astype(BF)

    def step(self):
        if self.parts == 8:
            self.kept = self.add()
            moves = [(b, a) for a, b in root_moves(self.next.pop(0))]
            self.got = lax.ppermute(self.kept, ("pb", "ka"), moves)

    def turn(self):
        if self.parts == 8:
            near = self.add()
            self.kept = jnp.where(at_root(), near, jnp.zeros_like(near))
            self.got = lax.ppermute(near, ("pb", "ka"), [(p * 4 + p // 2, p * 4 + (p // 2 ^ 2)) for p in range(8)])

    def cross(self):
        if self.parts == 8:
            self.kept = self.kept + self.got
            moves = [(p * 4 + k, p * 4 + (k ^ 1)) for p in range(8) for k in (p // 2, p // 2 ^ 2)]
            self.got = lax.ppermute(self.kept, ("pb", "ka"), moves)

    def end(self):
        ka, slot = lax.axis_size("ka"), slot_of(self.size)
        back = [(b, a) for a, b in row_moves(self.parts, ka)]
        x = lax.all_gather(lax.ppermute(self.kept, ("pb", "ka"), back), "ka")
        return [x[:, i * slot : i * slot + self.size].reshape(ka * self.size, -1) for i in range(2)]


def pair_gather(x):
    groups = [[i, i + 1] for i in range(0, lax.axis_size("ka"), 2)]
    return lax.all_gather(x, "ka", axis_index_groups=groups)


def core_pieces(x, far):
    return swap(jnp.stack([x, far]), "ka", 1)


def in_order(own, far, core):
    me = lax.axis_index("ka")
    near = [own, core[0], far, core[1]]
    found = []
    for k in range(4):
        value = near[3]
        for n in range(3):
            value = jnp.where((me ^ k) == n, near[n], value)
        found.append(value)
    return found


def on_device(tokens, cotangent, lengths, keep_mask, w_qkv, w_out, w_fc, w_proj, norm_gain, norm_bias):
    rows, width = tokens.shape
    pb = lax.axis_size("pb")
    ka = lax.axis_size("ka")
    me = lax.axis_index("ka")
    low, high = me % 2, me // 2
    heads = H // ka
    part = width // ka
    ff = w_fc.shape[2]
    ff_part = ff // ka
    d_rows = w_qkv.shape[0]
    proj_rows = w_proj.shape[0] // ka
    wide = (3 * part + 8 + 127) // 128 * 128
    bounds = jnp.cumsum(lengths[0])
    info = jnp.concatenate([jnp.stack([lax.axis_index("pb"), low]).astype(jnp.int32), bounds.astype(jnp.int32)])

    half, group = 2 * rows, 4 * rows

    def own_half(x, far):
        return jnp.where(high == 0, jnp.concatenate([x, far], axis=0), jnp.concatenate([far, x], axis=0))

    def block(half, which):
        return lax.dynamic_slice_in_dim(half, which * rows, rows, 0)

    def from_pair(sent):
        return lax.dynamic_index_in_dim(pair_gather(sent), 1 - low, 0, False)

    def add_low(kept, got):
        return (kept + got.astype(F32)).astype(BF)

    picked = jnp.concatenate([lax.dynamic_slice_in_dim(w_qkv, i * width + me * part, part, 2) for i in range(3)], axis=2)
    vectors = jnp.concatenate([norm_gain, norm_bias], axis=1)
    first = jnp.concatenate([picked[:, 0], vectors, jnp.zeros((d_rows, wide - 3 * part - 8), BF)], axis=1)
    outs = OutSpread(w_out)
    qkv0 = Spread(first, True)
    keep_rows = jnp.pad(keep_mask.astype(BF)[None, :], ((0, 15), (0, width - rows)))
    tokens_more = jnp.concatenate([tokens, keep_rows], axis=0)
    far_tokens = swap(tokens_more, "ka", 2)
    tokens_more = own_half(tokens_more, far_tokens)
    first, tokens_more, w_fc, w_proj, picked = tick(first, tokens_more, w_fc, w_proj, picked)
    tokens_both = pair_gather(tokens_more)
    tokens_own = own_half(tokens, far_tokens[:rows])
    unit = ff_part // pb
    local_fc = jnp.concatenate(
        [lax.dynamic_slice_in_dim(w_fc, (q * ka + me) * unit, unit, 2) for q in range(pb)], axis=2
    )
    fc_first, fc_second = local_fc[:, 0], local_fc[:, 1]
    local_proj = lax.dynamic_slice_in_dim(w_proj, me * proj_rows, proj_rows, 0)
    proj_first, proj_late = local_proj[:, 0], local_proj[:, 1]
    second = jnp.concatenate([picked[:, 1], jnp.zeros((d_rows, wide - 3 * part), BF)], axis=1)
    tokens_both, fc_first, proj_first, second, cotangent, proj_late = tick(
        qkv0, outs, tokens_both, fc_first, proj_first, second, cotangent, proj_late
    )
    qkv0.step()
    outs.step()
    proj0 = Spread(proj_first)
    fc0_all = gather_rows(fc_first)
    cotangent, second, fc_second, proj_late = tick(outs, proj0, cotangent, second, fc_second, proj_late)
    outs.step()
    proj0.step()
    qkv1 = Spread(second)
    far_cotangent = swap(cotangent, "ka", 2)
    tokens_both, outs.kept, proj0.kept, second = tick(qkv0, tokens_both, outs.kept, proj0.kept, second)
    qkv = [qkv0.rows(), None]

    keys = ("stream", "x", "projected", "attended", "lse", "middle", "both", "hidden", "active")
    got = attention_forward(True, True, info, group, None, tokens_both, qkv[0], part, heads)
    x_all, projected, attended, lse, tokens_all, vec, kept_all = got
    attended, proj_late = tick(attended, outs, proj_late)
    proj1_all = gather_rows(proj_late)
    out = [outs.rows(0), outs.rows(1)]
    sent, kept = attention_out(info, attended, out[0])
    got, fc_second, far_cotangent = tick(from_pair(sent), proj0, qkv1, fc_second, far_cotangent)
    near = add_low(kept, got)
    far = swap(near, "ka", 2)
    proj0.step()
    qkv1.step()
    fc1 = Spread(fc_second)
    branch = own_half(cotangent, far_cotangent)
    middle, own = norm_after(1, tokens_own, near, far, vec)
    both = pair_gather(own)
    fc = [whole_rows(fc0_all, pb, 0, d_rows), None]
    proj = [proj0.rows(), whole_rows(proj1_all, pb, 0, proj_rows)]
    hidden, active, sent, kept = feed_forward(info, both, fc[0], proj[0])
    kept0 = dict(zip(keys, (tokens_own, x_all, projected, attended, lse, middle, both, hidden, active)))
    got, branch_own = tick(from_pair(sent), qkv1, fc1, branch)
    near = add_low(kept, got)
    far = swap(near, "ka", 2)
    fc1.step()
    qkv1.step()
    branch = pair_gather(branch_own)
    qkv[1] = qkv1.rows()
    far, branch = tick(far, branch)
    stream, own = norm_after(2, middle, near, far, vec)
    both = pair_gather(own)
    x_all, projected, attended, lse = attention_forward(False, False, info, group, kept_all, both, qkv[1], part, heads)
    sent, kept = attention_out(info, attended, out[1])
    (got,) = tick(from_pair(sent), fc1)
    near = add_low(kept, got)
    far = swap(near, "ka", 2)
    fc1.step()
    fc[1] = fc1.rows()
    middle, own = norm_after(3, stream, near, far, vec)
    both = pair_gather(own)
    hidden, active, last_sent, last_kept = feed_forward(info, both, fc[1], proj[1])
    kept1 = dict(zip(keys, (stream, x_all, projected, attended, lse, middle, both, hidden, active)))

    sums = [None] * 4

    def fc_pair(kept, grad_hidden):
        return [(kept["both"].reshape(group, width), 0, grad_hidden, 0, group)], 0

    def proj_pair(kept, branch):
        return [(kept["active"], 0, branch.reshape(group, width), 0, group)], 0

    def qkv_pair(kept, grad_projected, more=()):
        return [(kept["x"], 0, grad_projected, 0, group), *more], 0

    def attend_back(l, kept, both):
        return attention_backward(
            l == 0, l == 0, info, kept_all, both, kept["projected"], kept["lse"], qkv[l], out[l], tokens_all, heads
        )

    grad_hidden, sent, kept = feed_backward(info, branch, kept1["hidden"], fc[1], proj[1])
    near = add_low(kept, from_pair(sent))
    far = swap(near, "ka", 2)
    near_in, grad_hidden, branch, last_sent, last_kept = tick(near, grad_hidden, branch, last_sent, last_kept)
    last = add_low(last_kept, from_pair(last_sent))
    flow_a = Flow(info, [fc_pair(kept1, grad_hidden)]).start()
    flow_p = Flow(info, [proj_pair(kept1, branch)], (2, 4, 1)).start()
    far, last, *unused = tick(far, last, flow_a.made, flow_p.made)
    last_far = swap(block(last, 1 - high), "ka", 2)
    grad, own, sums[3] = norm_back(3, branch_own, near, far, kept1["middle"], vec)
    both = pair_gather(own)
    middle_one, grad_projected, sent, kept = attend_back(1, kept1, both)
    got, last, last_far = tick(from_pair(sent), last, last_far, flow_a, flow_p)
    near = add_low(kept, got)
    far = swap(near, "ka", 2)
    near_in, grad_projected = tick(near, grad_projected)
    flow_b = Flow(info, [qkv_pair(kept1, grad_projected)]).start()
    flow_a.step()
    flow_p.step()
    output = (block(kept1["middle"], high) + (block(last, high).astype(F32) + last_far.astype(F32))).astype(BF)
    far, output, unused = tick(far, output, flow_b.made)
    grad, own, sums[2] = norm_back(2, grad, near, far, kept1["stream"], vec)
    branch = pair_gather(own)
    grad_hidden, sent, kept = feed_backward(info, branch, kept0["hidden"], fc[0], proj[0])
    (got,) = tick(from_pair(sent), flow_a, flow_p, flow_b)
    near = add_low(kept, got)
    far = swap(near, "ka", 2)
    near_in, grad_hidden, branch = tick(near, grad_hidden, branch)
    flow_c = Flow(info, [fc_pair(kept0, grad_hidden)]).start()
    flow_q = Flow(info, [proj_pair(kept0, branch)], (2, 4, 1)).start()
    tick(flow_a, flow_p, flow_c.made, flow_q.made)
    flow_a.step()
    flow_p.step()
    (far,) = tick(far, flow_c.made, flow_q.made)[:1]
    grad, own, sums[1] = norm_back(1, grad, near, far, kept0["middle"], vec)
    both = pair_gather(own)
    middle_all, grad_projected, sent, kept, sums[0] = attend_back(0, kept0, both)
    (got,) = tick(from_pair(sent), flow_a, flow_p, flow_b, flow_c, flow_q)
    grad_projected, got = tick(grad_projected, got)
    halved = [sums[0]] + [0.5 * s for s in sums[1:]]
    stacked = jnp.concatenate([s[i : i + 1] for i in range(2) for s in halved] + [jnp.zeros((8, width), F32)], axis=0).astype(BF)
    spots = (3 * part + jnp.arange(16)[:, None] == jnp.arange(wide)[None, :]) & (jnp.arange(16)[:, None] < 8)
    flow_d = Flow(info, [qkv_pair(kept0, grad_projected, [(stacked, 0, spots.astype(BF), 0, 16)])]).start()
    tick(flow_b, flow_c, flow_q, flow_d.made)
    near = add_low(kept, tick(got, flow_d.made)[0])
    far = swap(block(near, 1 - high), "ka", 2)
    flow_b.step()
    flow_c.step()
    flow_q.step()
    after_fc = slot_of(d_rows)
    far, unused = tick(far, flow_d.made)
    (grad_tokens,) = norm_back(0, block(grad, high), block(near, high), far, block(kept0["stream"], high), vec, True)

    middle_all, grad_tokens = tick(flow_b, flow_c, flow_q, flow_d, middle_all, grad_tokens)
    flow_d.step()
    middle_all = tick(middle_all, flow_d.kept)[0]
    tick(flow_b, flow_c, flow_q)
    flow_o = OutFlow(info, [(kept0["attended"], middle_all), (kept1["attended"], middle_one)])
    flow_b.step()
    flow_c.step()
    flow_q.step()
    done_a = jnp.concatenate([flow_a.end(), flow_p.end()], axis=0)
    tick(flow_d, flow_o)
    flow_d.step()
    flow_o.step()
    (done_a,) = tick(flow_b, flow_c, flow_q, done_a)
    far_a = swap(done_a, "ka", 2)
    done_b = flow_b.end()
    far_b = swap(done_b, "ka", 2)
    done_c = jnp.concatenate([flow_c.end(), flow_q.end()], axis=0)
    far_c = swap(done_c, "ka", 2)
    far_a, far_b = tick(flow_d, flow_o, far_a, far_b)
    done_d = flow_d.end()
    far_d = swap(done_d, "ka", 2)
    flow_o.step()
    far_d, far_c = tick(far_d, flow_o, far_c)
    core_ac = swap(jnp.stack([done_a, far_a, done_c, far_c]), "ka", 1)
    core_bd = swap(jnp.stack([done_b, far_b, done_d, far_d]), "ka", 1)
    flow_o.turn()
    core_ac, core_bd = tick(core_ac, core_bd, flow_o)
    core_a, core_c, core_b, core_d = core_ac[:2], core_ac[2:], core_bd[:2], core_bd[2:]
    flow_o.cross()
    block_a, block_b, block_c, block_d = [
        (done_a, far_a, core_a),
        (done_b, far_b, core_b),
        (done_c, far_c, core_c),
        (done_d, far_d, core_d),
    ]
    if pb == 8:
        rank = me.astype(jnp.int32).reshape(1)
        sum_fc, sum_proj = finish_feed(rank, (block_c, block_a), after_fc, unit, d_rows, proj_rows)
        sum_qkv, stacked = finish_attend(rank, (block_d, block_b), part)
        (sum_out,) = finish_out(flow_o.kept, flow_o.got)
        return (output, grad_tokens, sum_qkv, sum_out, sum_fc, sum_proj, stacked[:4].T, stacked[4:].T)

    def pair(one, other):
        return jnp.stack([one, other], axis=1).astype(F32)

    def columns(pieces):
        return jnp.stack([p[:d_rows].reshape(d_rows, pb, unit) for p in pieces], axis=2).reshape(d_rows, ff)

    def heads_of(pieces):
        return jnp.concatenate([p[:d_rows, i * part : (i + 1) * part] for i in range(3) for p in pieces], axis=1)

    def rows_of(pieces):
        return jnp.concatenate([p[after_fc : after_fc + proj_rows] for p in pieces], axis=0)

    a, b, c, d = [in_order(*pieces) for pieces in (block_a, block_b, block_c, block_d)]
    stacked = sum(p[:d_rows, 3 * part : 3 * part + 8].astype(F32) for p in d)
    return (
        output,
        grad_tokens,
        pair(heads_of(d), heads_of(b)),
        pair(*flow_o.end()),
        pair(columns(c), columns(a)),
        pair(rows_of(c), rows_of(a)),
        stacked[:, :4],
        stacked[:, 4:],
    )


def solution(mesh):
    return jax.shard_map(
        on_device,
        mesh=mesh,
        in_specs=(
            P(("pb", "ka"), None),
            P(("pb", "ka"), None),
            P("pb", None),
            P(("pb", "ka")),
            P("pb", None, None),
            P("pb", None, None),
            P("pb", None, None),
            P("pb", None, None),
            P("pb", None),
            P("pb", None),
        ),
        out_specs=(
            P(("pb", "ka"), None),
            P(("pb", "ka"), None),
            P("pb", None, None),
            P("pb", None, None),
            P("pb", None, None),
            P("pb", None, None),
            P("pb", None),
            P("pb", None),
        ),
        check_vma=False,
    )
```

```python
import functools
import jax
import jax.numpy as jnp
from jax import lax
from jax.experimental import pallas as pl
from jax.experimental.pallas import tpu as pltpu
from jax.sharding import PartitionSpec as P

H = 12
EPSILON = 1e-05
FLOOR_VALUE = -1e30
BF = jnp.bfloat16
F32 = jnp.float32
VM = pl.BlockSpec(memory_space=pltpu.VMEM)
SM = pl.BlockSpec(memory_space=pltpu.SMEM)
SHIFTS = (0, 4, 2, 6)
GELU_A = 0.7978845608028654
GELU_B = 0.044715


def dot(a, b, ca, cb):
    return lax.dot_general(a, b, (((ca,), (cb,)), ((), ())), preferred_element_type=F32)


def call(kernel, outs, ins, scratch=(), flops=0, name=None):
    moved = sum(a.size * a.dtype.itemsize for a in ins)
    return pl.pallas_call(
        kernel,
        out_shape=[jax.ShapeDtypeStruct(s, t) for s, t in outs],
        in_specs=[SM if a.dtype == jnp.int32 and a.ndim == 1 else VM for a in ins],
        out_specs=[VM] * len(outs),
        scratch_shapes=list(scratch),
        compiler_params=pltpu.CompilerParams(vmem_limit_bytes=20 * 1024 * 1024),
        cost_estimate=pl.CostEstimate(flops=flops, bytes_accessed=moved, transcendentals=0),
        name=name,
    )(*ins)


def at(index, rows):
    return pl.ds(pl.multiple_of(index * rows, rows), rows)


class Rows:
    def __init__(self, arrays, plan, size, span=0):
        self.arrays, self.plan, self.size, self.span = arrays, plan, size, span
        self.shape = (size * len(plan), arrays[0].shape[1])

    def scratch(self):
        return pltpu.VMEM(self.shape, F32 if self.size % 16 else BF)

    def take(self, refs, scratch, me):
        if len(self.arrays) == 1 and not self.span and self.plan == [(0, p * self.size, p, False) for p in range(len(self.plan))]:
            return refs[0]
        self.load(refs, scratch, me)
        return scratch

    def load(self, refs, scratch, me):
        for index, start, p, relative in self.plan:
            place = me ^ p if relative else p
            if self.span < 0:
                place = place & (len(self.plan) - 1)
            elif self.span:
                place = place_of(place, self.span, len(self.plan) // self.span)
            target = at(place, self.size) if relative else slice(place * self.size, (place + 1) * self.size)
            scratch[target, :] = refs[index][start : start + self.size, :].astype(scratch.dtype)


def place_of(p, span, ka):
    return (p % span) * ka + p // span if isinstance(p, int) else lax.rem(p, span) * ka + lax.div(p, span)


def take_refs(refs, *weights):
    return [[refs.pop(0) for unused in w.arrays] for w in weights]


def norm_parts(values):
    average = jnp.mean(values, axis=-1, keepdims=True)
    centered = values - average
    spread = jnp.mean(centered * centered, axis=-1, keepdims=True)
    inverse = lax.rsqrt(spread + EPSILON)
    return centered * inverse, inverse


def block_allowed(info, kept_ref, b, block, keys):
    i = b * block + lax.broadcasted_iota(jnp.int32, (1, block), 1)
    j = lax.broadcasted_iota(jnp.int32, (keys, 1), 0)

    def segment(t):
        total = jnp.zeros_like(t)
        for n in range(2, info.shape[0]):
            total = total + jnp.where(t >= info[n], 1, 0)
        return total

    same = segment(i) == segment(j)
    itself = i == j
    return same & (j <= i) & ((kept_ref[:keys, :] > 0) | itself)


def canonical(both, full):
    block, stride = full.shape[0] // 4, both.shape[1] // 2
    for h in range(2):
        for i in range(2):
            full[(2 * i + h) * block : (2 * i + h + 1) * block, :] = both[h, i * stride : i * stride + block, :]


def split_halves(low, full, kept, sent):
    block = kept.shape[0] // 2
    for i in range(2):
        kept[i * block : (i + 1) * block, :] = full[at(2 * i + low, block), :].astype(kept.dtype)
        sent[i * block : (i + 1) * block, :] = full[at(2 * i + 1 - low, block), :].astype(sent.dtype)


def attention_forward_kernel(first, signed, qkv, heads, *refs):
    refs = list(refs)
    info = refs.pop(0)
    if not first:
        kept_ref = refs.pop(0)
    both = refs.pop(0)
    (pieces,) = take_refs(refs, qkv)
    x_ref, proj_ref, att_ref, lse_ref = [refs.pop(0) for unused in range(4)]
    if first:
        tokens, vec_ref, kept_ref = refs.pop(0), refs.pop(0), refs.pop(0)
    (w,) = refs
    me, low = info[0], info[1]
    qkv.load(pieces, w, me)
    part = att_ref.shape[1]
    hd = part // heads
    group, width = x_ref.shape
    block = group // 4
    if first:
        tail = w.shape[1] - 3 * part
        pick = lax.broadcasted_iota(jnp.int32, (8, tail), 0) == lax.broadcasted_iota(jnp.int32, (8, tail), 1)
        vec = dot(pick.astype(F32).astype(BF), w[:, 3 * part :], 1, 1)
        vec_ref[...] = vec
        canonical(both, tokens)
        stride = both.shape[1] // 2
        for h in range(2):
            for i in range(2):
                row = both[h, i * stride + block : i * stride + block + 1, :block].astype(F32)
                kept_ref[(2 * i + h) * block : (2 * i + h + 1) * block, :] = jnp.transpose(jnp.broadcast_to(row, (8, block)))[:, :1]
        for b in range(4):
            values = tokens[b * block : (b + 1) * block, :].astype(F32)
            normal, unused = norm_parts(values)
            x_ref[b * block : (b + 1) * block, :] = (normal * vec[0:1] + vec[4:5]).astype(BF)
    else:
        canonical(both, x_ref)
    proj_ref[...] = dot(x_ref[...], w[...], 1, 0).astype(BF)
    scale = hd ** (-0.5)
    for b in range(4):
        keys = (b + 1) * block
        rows = slice(b * block, keys)
        allowed = block_allowed(info, kept_ref, b, block, keys)
        each = range(heads)
        q = [proj_ref[rows, h * hd : (h + 1) * hd] * scale for h in each]
        k = [proj_ref[:keys, part + h * hd : part + (h + 1) * hd] for h in each]
        v = [proj_ref[:keys, 2 * part + h * hd : 2 * part + (h + 1) * hd] for h in each]
        scores = [dot(k[h], q[h], 1, 1) for h in each]
        masked = [jnp.where(allowed, jnp.abs(s) if signed else s, FLOOR_VALUE) for s in scores]
        peak = [jnp.max(m, axis=0, keepdims=True) for m in masked]
        raised = [jnp.exp(masked[h] - peak[h]) for h in each]
        total = [jnp.sum(r, axis=0, keepdims=True) for r in raised]
        if signed:
            lifted = [jnp.where(allowed, raised[h] - jnp.exp(-peak[h]), 0.0) for h in each]
            raised = [jnp.where(scores[h] < 0, -lifted[h], lifted[h]) for h in each]
        weights = [(raised[h] * (1.0 / total[h])).astype(BF) for h in each]
        values = [dot(v[h], weights[h], 0, 0) for h in each]
        for h in each:
            att_ref[rows, h * hd : (h + 1) * hd] = jnp.transpose(values[h]).astype(BF)
            lse_ref[h : h + 1, rows] = peak[h] + jnp.log(total[h])


def attention_forward(first, signed, info, group, kept, both, qkv, part, heads):
    width = both.shape[2]
    outs = [((group, width), BF), ((group, qkv.shape[1]), BF), ((group, part), BF), ((8, group), F32)]
    if first:
        outs += [((group, width), BF), ((8, width), F32), ((group, 1), F32)]
    return call(
        functools.partial(attention_forward_kernel, first, signed, qkv, heads),
        outs,
        [info] + ([] if first else [kept]) + [both, *qkv.arrays],
        [qkv.scratch()],
        flops=2 * group * width * 3 * part,
        name="attend",
    )


def attention_out_kernel(out, *refs):
    refs = list(refs)
    info, attended = refs.pop(0), refs.pop(0)
    (pieces,) = take_refs(refs, out)
    sent, kept, w_out, partial = refs
    out.load(pieces, w_out, info[0])
    partial[...] = dot(attended[...], w_out[...].astype(BF), 1, 0)
    split_halves(info[1], partial, kept, sent)


def attention_out(info, attended, out):
    group, width = attended.shape[0], out.shape[1]
    return call(
        functools.partial(attention_out_kernel, out),
        [((group // 2, width), BF), ((group // 2, width), F32)],
        [info, attended, *out.arrays],
        [out.scratch(), pltpu.VMEM((group, width), F32)],
        flops=2 * group * width * out.shape[0],
        name="attend_out",
    )


def gelu_parts(v):
    inner = GELU_A * (v + GELU_B * v * v * v)
    return jnp.tanh(inner)


def feed_forward_kernel(fc, proj, *refs):
    refs = list(refs)
    info, both = [refs.pop(0) for unused in range(2)]
    fc_refs, proj_refs = take_refs(refs, fc, proj)
    hidden, active, sent, kept, w, w_proj, partial = refs
    w = fc.take(fc_refs, w, info[0])
    w_proj = proj.take(proj_refs, w_proj, info[0])
    half = both.shape[1]
    ff = w_proj.shape[0]
    step = ff // 3
    parts = [(h, f) for f in range(3) for h in range(2)]
    hids = [dot(both[h], w[:, f * step : (f + 1) * step], 1, 0) for h, f in parts]
    acts = [(0.5 * v * (1.0 + gelu_parts(v))).astype(BF) for v in hids]
    for (h, f), hid, act in zip(parts, hids, acts):
        rows, cols = slice(h * half, (h + 1) * half), slice(f * step, (f + 1) * step)
        hidden[rows, cols] = hid
        active[rows, cols] = act
    for h in range(2):
        partial[h] = dot(active[h * half : (h + 1) * half, :], w_proj[...], 1, 0)
    kept[...] = partial[info[1]]
    sent[...] = partial[1 - info[1]].astype(BF)


def feed_forward(info, both, fc, proj):
    two, half, width = both.shape
    ff = proj.shape[0]
    outs = [((2 * half, ff), F32), ((2 * half, ff), BF), ((half, width), BF), ((half, width), F32)]
    return call(
        functools.partial(feed_forward_kernel, fc, proj),
        outs,
        [info, both, *fc.arrays, *proj.arrays],
        [fc.scratch(), proj.scratch(), pltpu.VMEM((2, half, width), F32)],
        flops=8 * half * width * ff,
        name="feed",
    )


def norm_kernel(row, stream, near, far, vec, middle, normed):
    values = stream[...].astype(F32) + (near[...].astype(F32) + far[...].astype(F32))
    middle[...] = values
    normal, unused = norm_parts(values)
    normed[...] = (normal * vec[row : row + 1, :] + vec[row + 4 : row + 5, :]).astype(BF)


def norm_after(row, stream, near, far, vec):
    shape = stream.shape
    return call(functools.partial(norm_kernel, row), [(shape, F32), (shape, BF)], [stream, near, far, vec], name="norm")


def feed_backward_kernel(fc, proj, *refs):
    refs = list(refs)
    info, both, hidden = [refs.pop(0) for unused in range(3)]
    fc_refs, proj_refs = take_refs(refs, fc, proj)
    grad_hidden, sent, kept, w, w_proj, partial = refs
    w = fc.take(fc_refs, w, info[0])
    w_proj = proj.take(proj_refs, w_proj, info[0])
    half = both.shape[1]
    ff = w_proj.shape[0]
    step = ff // 3
    for f in range(3):
        cols = slice(f * step, (f + 1) * step)
        for h in range(2):
            rows = slice(h * half, (h + 1) * half)
            grad_active = dot(both[h], w_proj[cols, :], 1, 1)
            v = hidden[rows, cols]
            t = gelu_parts(v)
            slope = 0.5 * (1.0 + t) + 0.5 * v * (1.0 - t * t) * (GELU_A * (1.0 + 3.0 * GELU_B * v * v))
            grad_hidden[rows, cols] = (slope * grad_active).astype(BF)
    for h in range(2):
        partial[h] = dot(grad_hidden[h * half : (h + 1) * half, :], w[...], 1, 1)
    kept[...] = partial[info[1]]
    sent[...] = partial[1 - info[1]].astype(BF)


def feed_backward(info, both, hidden, fc, proj):
    two, half, width = both.shape
    ff = proj.shape[0]
    outs = [((2 * half, ff), BF), ((half, width), BF), ((half, width), F32)]
    return call(
        functools.partial(feed_backward_kernel, fc, proj),
        outs,
        [info, both, hidden, *fc.arrays, *proj.arrays],
        [fc.scratch(), proj.scratch(), pltpu.VMEM((2, half, width), F32)],
        flops=8 * half * width * ff,
        name="feed_back",
    )


def norm_backward_kernel(row, grad, near, far, source, vec, out, *rest):
    incoming = near[...].astype(F32) + far[...].astype(F32)
    normal, inverse = norm_parts(source[...].astype(F32))
    grad_normal = incoming * vec[row : row + 1, :]
    mean_grad = jnp.mean(grad_normal, axis=-1, keepdims=True)
    mean_cross = jnp.mean(grad_normal * normal, axis=-1, keepdims=True)
    value = grad[...].astype(F32) + inverse * (grad_normal - mean_grad - normal * mean_cross)
    out[...] = value
    if not rest:
        return
    low, sums = rest
    low[...] = value.astype(BF)
    sums[0:1, :] = jnp.sum(incoming * normal, axis=0, keepdims=True)
    sums[1:2, :] = jnp.sum(incoming, axis=0, keepdims=True)


def norm_back(row, grad, near, far, source, vec, last=False):
    shape = source.shape
    return call(
        functools.partial(norm_backward_kernel, row),
        [(shape, F32)] if last else [(shape, F32), (shape, BF), ((2, shape[1]), F32)],
        [grad, near, far, source, vec],
        name="norm_back",
    )


def attention_backward_kernel(first, signed, qkv, out, heads, *refs):
    refs = list(refs)
    info, kept_ref, both, proj, lse = [refs.pop(0) for unused in range(5)]
    pieces, out_pieces = take_refs(refs, qkv, out)
    if first:
        tokens = refs.pop(0)
    gm_ref, gp_ref, sent, kept = [refs.pop(0) for unused in range(4)]
    if first:
        sums = refs.pop(0)
    w, w_out, partial, gatt, gk_sum, gv_sum = refs
    me, low = info[0], info[1]
    qkv.load(pieces, w, me)
    out.load(out_pieces, w_out, me)
    part = w_out.shape[0]
    hd = part // heads
    group = gm_ref.shape[0]
    block = group // 4
    canonical(both, gm_ref)
    gatt[...] = dot(gm_ref[...], w_out[...].astype(BF), 1, 1).astype(BF)
    scale = hd ** (-0.5)
    gp_ref[:, 3 * part :] = jnp.zeros((group, gp_ref.shape[1] - 3 * part), BF)
    for b in reversed(range(4)):
        keys = (b + 1) * block
        rows = slice(b * block, keys)
        allowed = block_allowed(info, kept_ref, b, block, keys)
        each = range(heads)
        q = [proj[rows, h * hd : (h + 1) * hd] * scale for h in each]
        k = [proj[:keys, part + h * hd : part + (h + 1) * hd] for h in each]
        v = [proj[:keys, 2 * part + h * hd : 2 * part + (h + 1) * hd] for h in each]
        g = [gatt[rows, h * hd : (h + 1) * hd] for h in each]
        level = [lse[h : h + 1, rows] for h in each]
        scores = [dot(k[h], q[h], 1, 1) for h in each]
        grad_weights = [dot(v[h], g[h], 1, 1) for h in each]
        absolute = [jnp.exp(jnp.where(allowed, jnp.abs(scores[h]) if signed else scores[h], FLOOR_VALUE) - level[h]) for h in each]
        if signed:
            lifted = [jnp.where(allowed, absolute[h] - jnp.exp(-level[h]), 0.0) for h in each]
            weights = [jnp.where(scores[h] < 0, -lifted[h], lifted[h]) for h in each]
        else:
            weights = absolute
        shift = [jnp.sum(grad_weights[h] * weights[h], axis=0, keepdims=True) for h in each]
        if signed:
            shift = [jnp.where(scores[h] > 0, shift[h], jnp.where(scores[h] < 0, -shift[h], 0.0)) for h in each]
        gs = [(absolute[h] * (grad_weights[h] - shift[h])).astype(BF) for h in each]
        gv = [dot(weights[h].astype(BF), g[h], 1, 0) for h in each]
        gk = [dot(gs[h], q[h], 1, 0) for h in each]
        gq = [dot(k[h], gs[h], 0, 0) for h in each]
        for h in each:
            gp_ref[rows, h * hd : (h + 1) * hd] = jnp.transpose(gq[h] * scale).astype(BF)
            if b == 3:
                gk_sum[h] = gk[h]
                gv_sum[h] = gv[h]
            else:
                gk_sum[h, :keys] += gk[h]
                gv_sum[h, :keys] += gv[h]
    for h in range(heads):
        gp_ref[:, part + h * hd : part + (h + 1) * hd] = gk_sum[h].astype(BF)
        gp_ref[:, 2 * part + h * hd : 2 * part + (h + 1) * hd] = gv_sum[h].astype(BF)
    partial[...] = dot(gp_ref[...], w[...], 1, 1)
    split_halves(low, partial, kept, sent)
    if first:
        gain = bias = 0.0
        for b in range(4):
            rows = slice(b * block, (b + 1) * block)
            normal, unused = norm_parts(tokens[rows, :].astype(F32))
            value = partial[rows, :]
            gain = gain + jnp.sum(value * normal, axis=0, keepdims=True)
            bias = bias + jnp.sum(value, axis=0, keepdims=True)
        sums[0:1, :] = gain
        sums[1:2, :] = bias


def attention_backward(first, signed, info, kept, both, proj, lse, qkv, out, tokens, heads):
    two, half, width = both.shape
    group = 2 * half
    part = out.shape[0]
    wide = qkv.shape[1]
    outs = [((group, width), BF), ((group, wide), BF), ((half, width), BF), ((half, width), F32)]
    if first:
        outs += [((2, width), F32)]
    return call(
        functools.partial(attention_backward_kernel, first, signed, qkv, out, heads),
        outs,
        [info, kept, both, proj, lse, *qkv.arrays, *out.arrays] + ([tokens] if first else []),
        [
            qkv.scratch(),
            out.scratch(),
            pltpu.VMEM((group, width), F32),
            pltpu.VMEM((group, part), BF),
            pltpu.VMEM((heads, group, part // heads), F32),
            pltpu.VMEM((heads, group, part // heads), F32),
        ],
        flops=2 * group * width * 4 * part,
        name="attend_back",
    )


def outer_kernel(parts, plans, bits, *refs):
    info, scratch = refs[0], refs[-1]
    outs = refs[-3:-1] if bits else refs[-2:-1]
    shifts = halving(bits)
    start = 0
    for segments, rows, slot, span, cols in plans:
        size = rows // parts
        blank = scratch.shape[1] - cols

        def place(p):
            return place_of(p, span, parts // span) if span else p

        total = None
        for left, first, right, second, count in segments:
            term = dot(refs[left][first : first + count, :], refs[right][second : second + count, :], 0, 0)
            total = term if total is None else total + term
        scratch[:rows, :cols] = total
        if blank:
            scratch[:rows, cols:] = jnp.zeros((rows, blank), F32)
        for j in range(len(shifts) if bits else parts):
            if bits:
                targets = [at(place(info[0] ^ shifts[j] ^ bits[0]), size), at(place(info[0] ^ shifts[j]), size)]
            else:
                targets = [slice(place(j) * size, (place(j) + 1) * size)]
            for ref, target in zip(outs, targets):
                ref[j, start : start + size, :] = scratch[target, :].astype(BF)
                if slot > size:
                    ref[j, start + size : start + slot, :] = jnp.zeros((slot - size, scratch.shape[1]), BF)
        start += slot


def halving(bits):
    return [0, bits[2], bits[1], bits[1] | bits[2]] if bits else []


def slot_of(size):
    return (size + 15) // 16 * 16


def outer(parts, info, pairs, bits):
    arrays, plans = [info], []

    def number(a):
        for n, other in enumerate(arrays):
            if other is a:
                return n
        arrays.append(a)
        return len(arrays) - 1

    for segments, span in pairs:
        rows = segments[0][0].shape[1]
        numbers = [(number(a), first, number(b), second, count) for a, first, b, second, count in segments]
        plans.append((numbers, rows, slot_of(rows // parts), span, segments[0][2].shape[1]))
    cols = max(p[4] for p in plans)
    tall = sum(p[2] for p in plans)
    outs = [((parts // 2, tall, cols), BF)] * 2 if bits else [((parts, tall, cols), BF)]
    return call(
        functools.partial(outer_kernel, parts, plans, bits),
        outs,
        arrays,
        [pltpu.VMEM((max(p[1] for p in plans), cols), F32)],
        flops=sum(2 * p[1] * cols * sum(seg[4] for seg in p[0]) for p in plans),
        name="outer",
    )


def outer_pair_kernel(count, *refs):
    info, ins, (sent, kept, scratch) = refs[0], refs[1 : 1 + 2 * count], refs[1 + 2 * count :]
    size = scratch.shape[0] // 2
    low = info[0] & 1
    for i in range(count):
        scratch[...] = dot(ins[2 * i][...], ins[2 * i + 1][...], 0, 0)
        kept[i * size : (i + 1) * size, :] = scratch[at(low, size), :].astype(BF)
        sent[i * size : (i + 1) * size, :] = scratch[at(1 - low, size), :].astype(BF)


def outer_pair(info, pairs):
    rows, cols = pairs[0][0].shape[1], pairs[0][1].shape[1]
    shape = (len(pairs) * rows // 2, cols)
    return call(
        functools.partial(outer_pair_kernel, len(pairs)),
        [(shape, BF)] * 2,
        [info] + [a for pair in pairs for a in pair],
        [pltpu.VMEM((rows, cols), F32)],
        flops=len(pairs) * 2 * rows * cols * pairs[0][0].shape[0],
        name="outer",
    )


def piece_refs(refs):
    own, far, core = refs[:3]
    return [own, core.at[0], far, core.at[1]]


def finish_feed_kernel(first, unit, info, *refs):
    w_fc, w_proj, scratch = refs[-3:]
    me = info[0]
    size = w_fc.shape[0]
    rows = w_proj.shape[0] // 4
    for l in range(2):
        pieces = piece_refs(refs[3 * l :])
        values = [p[:size, :] for p in pieces]
        for k in range(4):
            value = values[3]
            for n in range(3):
                value = jnp.where((me ^ k) == n, values[n], value)
            for q in range(value.shape[1] // unit):
                scratch[:, (q * 4 + k) * unit : (q * 4 + k + 1) * unit] = value[:, q * unit : (q + 1) * unit]
        w_fc[:, l, :] = scratch[...].astype(F32)
        for n in range(4):
            w_proj[at(me ^ n, rows), l, :] = pieces[n][first : first + rows, :].astype(F32)


def finish_feed(me, blocks, first, unit, size, rows):
    width = blocks[0][0].shape[1]
    ff = 4 * width
    return call(
        functools.partial(finish_feed_kernel, first, unit),
        [((size, 2, ff), F32), ((4 * rows, 2, width), F32)],
        [me] + [a for block in blocks for a in block],
        [pltpu.VMEM((size, ff), BF)],
        name="finish_feed",
    )


def finish_attend_kernel(part, info, *refs):
    w_qkv, vectors, scratch = refs[6:]
    me = info[0]
    size = w_qkv.shape[0]
    for l in range(2):
        pieces = piece_refs(refs[3 * l :])
        values = [p[...] for p in pieces]
        for k in range(4):
            value = values[3]
            for n in range(3):
                value = jnp.where((me ^ k) == n, values[n], value)
            for i in range(3):
                scratch[:, (i * 4 + k) * part : (i * 4 + k + 1) * part] = value[:, i * part : (i + 1) * part]
        w_qkv[:, l, :] = scratch[...].astype(F32)
        if l == 0:
            tail = values[0].shape[1] - 3 * part
            pick = lax.broadcasted_iota(jnp.int32, (8, tail), 0) == lax.broadcasted_iota(jnp.int32, (8, tail), 1)
            pick = pick.astype(F32).astype(BF)
            total = None
            for value in values:
                term = dot(pick, value[:, 3 * part :], 1, 1)
                total = term if total is None else total + term
            vectors[...] = total


def finish_attend(me, blocks, part):
    size = blocks[0][0].shape[0]
    columns = 12 * part
    return call(
        functools.partial(finish_attend_kernel, part),
        [((size, 2, columns), F32), ((8, size), F32)],
        [me] + [a for block in blocks for a in block],
        [pltpu.VMEM((size, columns), BF)],
        name="finish_attend",
    )


def finish_out_kernel(near, far, w_out):
    size = w_out.shape[0]
    for l in range(2):
        rows = slice(l * size, (l + 1) * size)
        w_out[:, l, :] = near[rows, :].astype(F32) + far[rows, :].astype(F32)


def finish_out(near, far):
    rows, width = near.shape
    return call(finish_out_kernel, [((rows // 2, 2, width), F32)], [near, far], name="finish_out")


def stack_kernel(*refs):
    out = refs[-1]
    start = 0
    for ref in refs[:-1]:
        out[start : start + ref.shape[0], :] = ref[...]
        start += ref.shape[0]


def stack_rows(arrays):
    shape = (sum(a.shape[0] for a in arrays), arrays[0].shape[1])
    return call(stack_kernel, [(shape, BF)], list(arrays), name="stack")[0]


def tick(*items):
    flat = [a for item in items for a in (item.pending() if hasattr(item, "pending") else [item])]
    flat = list(lax.optimization_barrier(tuple(flat)))
    found = []
    for item in items:
        if hasattr(item, "pending"):
            count = len(item.pending())
            item.resume(flat[:count])
            del flat[:count]
        else:
            found.append(flat.pop(0))
    return found


def swap(x, axis, bit):
    size = lax.axis_size(axis)
    return lax.ppermute(x, axis, [(i, i ^ bit) for i in range(size)])


def row_moves(pb, ka):
    span = pb // ka
    return [(p * ka + k, (k * span + p % span) * ka + p // span) for p in range(pb) for k in range(ka)]


def gather_rows(x):
    return lax.all_gather(x, "pb", axis=0, tiled=True)


def whole_rows(x, parts, start, size, span=0):
    piece = x.shape[0] // parts
    return Rows([x], [(0, p * piece + start, p, False) for p in range(parts)], size, span)


class Spread:
    def __init__(self, x, direct=False):
        self.rows_each, self.parts = x.shape[0], lax.axis_size("pb")
        self.bits = [1] if direct else [2, 1]
        if self.parts != 8:
            self.kept, self.got = x, [gather_rows(x)]
        elif direct:
            self.kept, self.got = x, [swap(x, "pb", s) for s in SHIFTS[1:]]
        else:
            self.kept, self.got = x, [swap(x, "pb", 4)]

    def pending(self):
        return [self.kept, *self.got]

    def resume(self, arrays):
        self.kept, *self.got = arrays

    def step(self):
        if self.parts != 8:
            return
        self.kept = stack_rows([self.kept, *self.got])
        self.got = [swap(self.kept, "pb", self.bits.pop(0))]

    def rows(self, first=0, size=None, span=0):
        size = size or self.rows_each
        if self.parts != 8:
            return whole_rows(self.got[0], self.parts, first, size, span)
        each = self.rows_each
        plan = [(n, i * each + first, s + n, True) for n in range(2) for i, s in enumerate(SHIFTS)]
        return Rows(self.pending(), plan, size, span)


class Flow:
    def __init__(self, info, pairs, bits=(1, 2, 4)):
        self.parts = lax.axis_size("pb")
        if self.parts != 8:
            (x,) = outer(self.parts, info, pairs, ())
            self.kept = lax.psum_scatter(x.reshape(-1, x.shape[2]), "pb", scatter_dimension=0, tiled=True)
            self.got = self.kept
            self.made = x
        else:
            self.got, self.kept = outer(self.parts, info, pairs, bits)
            self.made = self.kept
            self.bits = list(bits)

    def pending(self):
        return [self.kept, self.got]

    def resume(self, arrays):
        self.kept, self.got = arrays

    def start(self):
        if self.parts == 8:
            self.got = swap(self.got, "pb", self.bits.pop(0))
        return self

    def step(self):
        if self.parts == 8:
            near = (self.kept.astype(F32) + self.got.astype(F32)).astype(BF)
            count = near.shape[0] // 2
            self.kept, self.got = near[:count], near[count:]
            self.start()

    def end(self):
        if self.parts != 8:
            return self.kept
        return (self.kept[0].astype(F32) + self.got[0].astype(F32)).astype(BF)


def root_moves(reach):
    holders = {2: lambda d: d == 0, 1: lambda d: d in (0, 2)}[reach]
    moves = []
    for z in range(4):
        for x in range(2):
            for k in range(4):
                if holders(z ^ k):
                    moves.append(((2 * z + x) * 4 + k, (2 * (z ^ reach) + x) * 4 + k))
    return moves


def at_root():
    return lax.axis_index("pb") // 2 == lax.axis_index("ka")


class OutSpread:
    def __init__(self, w_out):
        self.parts, ka = lax.axis_size("pb"), lax.axis_size("ka")
        self.span, self.size = self.parts // ka, w_out.shape[0]
        if self.parts != 8:
            self.size = w_out.shape[0] // ka
            own = lax.dynamic_slice_in_dim(w_out, lax.axis_index("ka") * self.size, self.size, 0)
            pad = jnp.zeros((slot_of(self.size) - self.size, w_out.shape[2]), BF)
            x = jnp.concatenate([own[:, 0], pad, own[:, 1], pad], axis=0)
            x = lax.ppermute(x, ("pb", "ka"), row_moves(self.parts, ka))
            self.kept, self.got = x, gather_rows(x)
        else:
            x = jnp.concatenate([w_out[:, 0], w_out[:, 1]], axis=0)
            self.kept = jnp.where(at_root(), x, jnp.zeros_like(x))
            self.got = lax.ppermute(x, ("pb", "ka"), root_moves(2))
            self.next = [1, 0]

    def pending(self):
        return [self.kept, self.got]

    def resume(self, arrays):
        self.kept, self.got = arrays

    def step(self):
        if self.parts == 8:
            self.kept = self.kept + self.got
            reach = self.next.pop(0)
            self.got = lax.ppermute(self.kept, ("pb", "ka"), root_moves(reach)) if reach else swap(self.kept, "pb", 1)

    def rows(self, l):
        if self.parts != 8:
            return whole_rows(self.got, self.parts, l * slot_of(self.size), self.size, self.span)
        return Rows(self.pending(), [(0, l * self.size, 0, True), (1, l * self.size, 1, True)], self.size, -1)


class OutFlow:
    def __init__(self, info, pairs):
        self.parts = lax.axis_size("pb")
        if self.parts != 8:
            self.flow = Flow(info, [([(a, 0, b, 0, a.shape[0])], self.parts // lax.axis_size("ka")) for a, b in pairs])
            self.size = pairs[0][0].shape[1] // self.parts
            self.kept = self.got = self.flow.end()
            self.made = self.flow.made
        else:
            sent, self.kept = outer_pair(info, pairs)
            self.made = self.kept
            self.got = swap(sent, "pb", 1)
            self.next = [1, 2]

    def pending(self):
        return [self.kept, self.got]

    def resume(self, arrays):
        self.kept, self.got = arrays

    def add(self):
        return (self.kept.astype(F32) + self.got.astype(F32)).astype(BF)

    def step(self):
        if self.parts == 8:
            self.kept = self.add()
            moves = [(b, a) for a, b in root_moves(self.next.pop(0))]
            self.got = lax.ppermute(self.kept, ("pb", "ka"), moves)

    def turn(self):
        if self.parts == 8:
            near = self.add()
            self.kept = jnp.where(at_root(), near, jnp.zeros_like(near))
            self.got = lax.ppermute(near, ("pb", "ka"), [(p * 4 + p // 2, p * 4 + (p // 2 ^ 2)) for p in range(8)])

    def cross(self):
        if self.parts == 8:
            self.kept = self.kept + self.got
            moves = [(p * 4 + k, p * 4 + (k ^ 1)) for p in range(8) for k in (p // 2, p // 2 ^ 2)]
            self.got = lax.ppermute(self.kept, ("pb", "ka"), moves)

    def end(self):
        ka, slot = lax.axis_size("ka"), slot_of(self.size)
        back = [(b, a) for a, b in row_moves(self.parts, ka)]
        x = lax.all_gather(lax.ppermute(self.kept, ("pb", "ka"), back), "ka")
        return [x[:, i * slot : i * slot + self.size].reshape(ka * self.size, -1) for i in range(2)]


def pair_gather(x):
    groups = [[i, i + 1] for i in range(0, lax.axis_size("ka"), 2)]
    return lax.all_gather(x, "ka", axis_index_groups=groups)


def core_pieces(x, far):
    return swap(jnp.stack([x, far]), "ka", 1)


def in_order(own, far, core):
    me = lax.axis_index("ka")
    near = [own, core[0], far, core[1]]
    found = []
    for k in range(4):
        value = near[3]
        for n in range(3):
            value = jnp.where((me ^ k) == n, near[n], value)
        found.append(value)
    return found


def on_device(tokens, cotangent, lengths, keep_mask, w_qkv, w_out, w_fc, w_proj, norm_gain, norm_bias):
    rows, width = tokens.shape
    pb = lax.axis_size("pb")
    ka = lax.axis_size("ka")
    me = lax.axis_index("ka")
    low, high = me % 2, me // 2
    heads = H // ka
    part = width // ka
    ff = w_fc.shape[2]
    ff_part = ff // ka
    d_rows = w_qkv.shape[0]
    proj_rows = w_proj.shape[0] // ka
    wide = (3 * part + 8 + 127) // 128 * 128
    bounds = jnp.cumsum(lengths[0])
    info = jnp.concatenate([jnp.stack([lax.axis_index("pb"), low]).astype(jnp.int32), bounds.astype(jnp.int32)])

    half, group = 2 * rows, 4 * rows

    def own_half(x, far):
        return jnp.where(high == 0, jnp.concatenate([x, far], axis=0), jnp.concatenate([far, x], axis=0))

    def block(half, which):
        return lax.dynamic_slice_in_dim(half, which * rows, rows, 0)

    def from_pair(sent):
        return lax.dynamic_index_in_dim(pair_gather(sent), 1 - low, 0, False)

    def add_low(kept, got):
        return (kept + got.astype(F32)).astype(BF)

    picked = jnp.concatenate([lax.dynamic_slice_in_dim(w_qkv, i * width + me * part, part, 2) for i in range(3)], axis=2)
    spot = jnp.arange(wide - 3 * part)[None, :] - jnp.arange(4)[:, None]
    vectors = dot(norm_gain, (spot == 0).astype(BF), 1, 0) + dot(norm_bias, (spot == 4).astype(BF), 1, 0)
    first = jnp.concatenate([picked[:, 0], vectors.astype(BF)], axis=1)
    outs = OutSpread(w_out)
    qkv0 = Spread(first, True)
    keep_rows = jnp.pad(keep_mask.astype(BF)[None, :], ((0, 15), (0, width - rows)))
    tokens_more = jnp.concatenate([tokens, keep_rows], axis=0)
    far_tokens = swap(tokens_more, "ka", 2)
    tokens_more = own_half(tokens_more, far_tokens)
    first, tokens_more, w_fc, w_proj, picked = tick(first, tokens_more, w_fc, w_proj, picked)
    tokens_both = pair_gather(tokens_more)
    tokens_own = own_half(tokens, far_tokens[:rows])
    unit = ff_part // pb
    local_fc = jnp.concatenate(
        [lax.dynamic_slice_in_dim(w_fc, (q * ka + me) * unit, unit, 2) for q in range(pb)], axis=2
    )
    fc_first, fc_second = local_fc[:, 0], local_fc[:, 1]
    local_proj = lax.dynamic_slice_in_dim(w_proj, me * proj_rows, proj_rows, 0)
    proj_first, proj_late = local_proj[:, 0], local_proj[:, 1]
    second = jnp.concatenate([picked[:, 1], jnp.zeros((d_rows, wide - 3 * part), BF)], axis=1)
    tokens_both, fc_first, proj_first, second, cotangent, proj_late = tick(
        qkv0, outs, tokens_both, fc_first, proj_first, second, cotangent, proj_late
    )
    qkv0.step()
    tick(outs, qkv0.kept)
    outs.step()
    proj0 = Spread(proj_first)
    fc0_all = gather_rows(fc_first)
    cotangent, second, fc_second, proj_late = tick(outs, proj0, cotangent, second, fc_second, proj_late)
    outs.step()
    proj0.step()
    qkv1 = Spread(second)
    far_cotangent = swap(cotangent, "ka", 2)
    tokens_both, outs.kept, proj0.kept, second = tick(qkv0, tokens_both, outs.kept, proj0.kept, second)
    qkv = [qkv0.rows(), None]

    keys = ("stream", "x", "projected", "attended", "lse", "middle", "both", "hidden", "active")
    got = attention_forward(True, True, info, group, None, tokens_both, qkv[0], part, heads)
    x_all, projected, attended, lse, tokens_all, vec, kept_all = got
    attended, proj_late = tick(attended, outs, proj_late)
    proj1_all = gather_rows(proj_late)
    out = [outs.rows(0), outs.rows(1)]
    sent, kept = attention_out(info, attended, out[0])
    got, fc_second, far_cotangent = tick(from_pair(sent), proj0, qkv1, fc_second, far_cotangent)
    near = add_low(kept, got)
    far = swap(near, "ka", 2)
    proj0.step()
    qkv1.step()
    fc1 = Spread(fc_second)
    branch = own_half(cotangent, far_cotangent)
    middle, own = norm_after(1, tokens_own, near, far, vec)
    both = pair_gather(own)
    fc = [whole_rows(fc0_all, pb, 0, d_rows), None]
    proj = [proj0.rows(), whole_rows(proj1_all, pb, 0, proj_rows)]
    hidden, active, sent, kept = feed_forward(info, both, fc[0], proj[0])
    kept0 = dict(zip(keys, (tokens_own, x_all, projected, attended, lse, middle, both, hidden, active)))
    got, branch_own = tick(from_pair(sent), qkv1, fc1, branch)
    near = add_low(kept, got)
    far = swap(near, "ka", 2)
    fc1.step()
    qkv1.step()
    branch = pair_gather(branch_own)
    qkv[1] = qkv1.rows()
    far, branch = tick(far, branch)
    stream, own = norm_after(2, middle, near, far, vec)
    both = pair_gather(own)
    x_all, projected, attended, lse = attention_forward(False, False, info, group, kept_all, both, qkv[1], part, heads)
    sent, kept = attention_out(info, attended, out[1])
    (got,) = tick(from_pair(sent), fc1)
    near = add_low(kept, got)
    far = swap(near, "ka", 2)
    fc1.step()
    fc[1] = fc1.rows()
    middle, own = norm_after(3, stream, near, far, vec)
    both = pair_gather(own)
    hidden, active, last_sent, last_kept = feed_forward(info, both, fc[1], proj[1])
    kept1 = dict(zip(keys, (stream, x_all, projected, attended, lse, middle, both, hidden, active)))

    sums = [None] * 4

    def fc_pair(kept, grad_hidden):
        return [(kept["both"].reshape(group, width), 0, grad_hidden, 0, group)], 0

    def proj_pair(kept, branch):
        return [(kept["active"], 0, branch.reshape(group, width), 0, group)], 0

    def qkv_pair(kept, grad_projected, more=()):
        return [(kept["x"], 0, grad_projected, 0, group), *more], 0

    def attend_back(l, kept, both):
        return attention_backward(
            l == 0, l == 0, info, kept_all, both, kept["projected"], kept["lse"], qkv[l], out[l], tokens_all, heads
        )

    grad_hidden, sent, kept = feed_backward(info, branch, kept1["hidden"], fc[1], proj[1])
    near = add_low(kept, from_pair(sent))
    far = swap(near, "ka", 2)
    near_in, grad_hidden, branch, last_sent, last_kept = tick(near, grad_hidden, branch, last_sent, last_kept)
    last = add_low(last_kept, from_pair(last_sent))
    flow_a = Flow(info, [fc_pair(kept1, grad_hidden)]).start()
    flow_p = Flow(info, [proj_pair(kept1, branch)], (2, 4, 1)).start()
    far, last, *unused = tick(far, last, flow_a.made, flow_p.made)
    last_far = swap(block(last, 1 - high), "ka", 2)
    grad, own, sums[3] = norm_back(3, branch_own, near, far, kept1["middle"], vec)
    both = pair_gather(own)
    middle_one, grad_projected, sent, kept = attend_back(1, kept1, both)
    got, last, last_far = tick(from_pair(sent), last, last_far, flow_a, flow_p)
    near = add_low(kept, got)
    far = swap(near, "ka", 2)
    near_in, grad_projected = tick(near, grad_projected)
    flow_b = Flow(info, [qkv_pair(kept1, grad_projected)]).start()
    flow_a.step()
    flow_p.step()
    output = (block(kept1["middle"], high) + (block(last, high).astype(F32) + last_far.astype(F32))).astype(BF)
    far, output, unused = tick(far, output, flow_b.made)
    grad, own, sums[2] = norm_back(2, grad, near, far, kept1["stream"], vec)
    branch = pair_gather(own)
    grad_hidden, sent, kept = feed_backward(info, branch, kept0["hidden"], fc[0], proj[0])
    (got,) = tick(from_pair(sent), flow_a, flow_p, flow_b)
    near = add_low(kept, got)
    far = swap(near, "ka", 2)
    near_in, grad_hidden, branch = tick(near, grad_hidden, branch)
    flow_c = Flow(info, [fc_pair(kept0, grad_hidden)]).start()
    flow_q = Flow(info, [proj_pair(kept0, branch)], (2, 4, 1)).start()
    tick(flow_a, flow_p, flow_c.made, flow_q.made)
    flow_a.step()
    flow_p.step()
    (far,) = tick(far, flow_c.made, flow_q.made)[:1]
    grad, own, sums[1] = norm_back(1, grad, near, far, kept0["middle"], vec)
    both = pair_gather(own)
    middle_all, grad_projected, sent, kept, sums[0] = attend_back(0, kept0, both)
    (got,) = tick(from_pair(sent), flow_a, flow_p, flow_b, flow_c, flow_q)
    grad_projected, got = tick(grad_projected, got)
    halved = [sums[0]] + [0.5 * s for s in sums[1:]]
    stacked = jnp.concatenate([s[i : i + 1] for i in range(2) for s in halved] + [jnp.zeros((8, width), F32)], axis=0).astype(BF)
    spots = (3 * part + jnp.arange(16)[:, None] == jnp.arange(wide)[None, :]) & (jnp.arange(16)[:, None] < 8)
    flow_d = Flow(info, [qkv_pair(kept0, grad_projected, [(stacked, 0, spots.astype(BF), 0, 16)])]).start()
    tick(flow_b, flow_c, flow_q, flow_d.made)
    near = add_low(kept, tick(got, flow_d.made)[0])
    far = swap(block(near, 1 - high), "ka", 2)
    flow_b.step()
    flow_c.step()
    flow_q.step()
    after_fc = slot_of(d_rows)
    far, unused = tick(far, flow_d.made)
    (grad_tokens,) = norm_back(0, block(grad, high), block(near, high), far, block(kept0["stream"], high), vec, True)

    middle_all, grad_tokens = tick(flow_b, flow_c, flow_q, flow_d, middle_all, grad_tokens)
    flow_d.step()
    middle_all = tick(middle_all, flow_d.kept)[0]
    tick(flow_b, flow_c, flow_q)
    flow_o = OutFlow(info, [(kept0["attended"], middle_all), (kept1["attended"], middle_one)])
    flow_b.step()
    flow_c.step()
    flow_q.step()
    done_a = jnp.concatenate([flow_a.end(), flow_p.end()], axis=0)
    tick(flow_d, flow_o)
    flow_d.step()
    flow_o.step()
    (done_a,) = tick(flow_b, flow_c, flow_q, done_a)
    far_a = swap(done_a, "ka", 2)
    done_b = flow_b.end()
    far_b = swap(done_b, "ka", 2)
    done_c = jnp.concatenate([flow_c.end(), flow_q.end()], axis=0)
    far_c = swap(done_c, "ka", 2)
    far_a, far_b = tick(flow_d, flow_o, far_a, far_b)
    done_d = flow_d.end()
    far_d = swap(done_d, "ka", 2)
    flow_o.step()
    far_d, far_c = tick(far_d, flow_o, far_c)
    core_ac = swap(jnp.stack([done_a, far_a, done_c, far_c]), "ka", 1)
    core_bd = swap(jnp.stack([done_b, far_b, done_d, far_d]), "ka", 1)
    flow_o.turn()
    core_ac, core_bd = tick(core_ac, core_bd, flow_o)
    core_a, core_c, core_b, core_d = core_ac[:2], core_ac[2:], core_bd[:2], core_bd[2:]
    flow_o.cross()
    block_a, block_b, block_c, block_d = [
        (done_a, far_a, core_a),
        (done_b, far_b, core_b),
        (done_c, far_c, core_c),
        (done_d, far_d, core_d),
    ]
    if pb == 8:
        rank = me.astype(jnp.int32).reshape(1)
        sum_fc, sum_proj = finish_feed(rank, (block_c, block_a), after_fc, unit, d_rows, proj_rows)
        sum_qkv, stacked = finish_attend(rank, (block_d, block_b), part)
        (sum_out,) = finish_out(flow_o.kept, flow_o.got)
        return (output, grad_tokens, sum_qkv, sum_out, sum_fc, sum_proj, stacked[:4].T, stacked[4:].T)

    def pair(one, other):
        return jnp.stack([one, other], axis=1).astype(F32)

    def columns(pieces):
        return jnp.stack([p[:d_rows].reshape(d_rows, pb, unit) for p in pieces], axis=2).reshape(d_rows, ff)

    def heads_of(pieces):
        return jnp.concatenate([p[:d_rows, i * part : (i + 1) * part] for i in range(3) for p in pieces], axis=1)

    def rows_of(pieces):
        return jnp.concatenate([p[after_fc : after_fc + proj_rows] for p in pieces], axis=0)

    a, b, c, d = [in_order(*pieces) for pieces in (block_a, block_b, block_c, block_d)]
    stacked = sum(p[:d_rows, 3 * part : 3 * part + 8].astype(F32) for p in d)
    return (
        output,
        grad_tokens,
        pair(heads_of(d), heads_of(b)),
        pair(*flow_o.end()),
        pair(columns(c), columns(a)),
        pair(rows_of(c), rows_of(a)),
        stacked[:, :4],
        stacked[:, 4:],
    )


def solution(mesh):
    return jax.shard_map(
        on_device,
        mesh=mesh,
        in_specs=(
            P(("pb", "ka"), None),
            P(("pb", "ka"), None),
            P("pb", None),
            P(("pb", "ka")),
            P("pb", None, None),
            P("pb", None, None),
            P("pb", None, None),
            P("pb", None, None),
            P("pb", None),
            P("pb", None),
        ),
        out_specs=(
            P(("pb", "ka"), None),
            P(("pb", "ka"), None),
            P("pb", None, None),
            P("pb", None, None),
            P("pb", None, None),
            P("pb", None, None),
            P("pb", None),
            P("pb", None),
        ),
        check_vma=False,
    )
```
